32 devices in a mesh: dp: 8 (over y, x, core), seq: 4 (over z).
Axes of the slice: x: 2, y: 2, z: 4, core: 2. Of those that a mesh axis runs over, the one named last changes fastest.
Arguments:
- tokens: bfloat16 [32, 512, 768], P('dp', 'seq'), may hold values from -6 to 6
- segment_ids: int32 [32, 512], P('dp', 'seq'), may hold values from 0 to 7, as said below
- pair_ids: int32 [256], P('dp'), may hold values from 0 to 31
- w_qkv: bfloat16 [2, 768, 2304], replicated, may hold values from -0.21875 to 0.21875
- b_query: float32 [2, 768], replicated, may hold values from -3 to 3
- b_value: float32 [2, 768], replicated, may hold values from -3 to 3
- w_out: bfloat16 [2, 768, 768], replicated, may hold values from -0.625 to 0.625
- b_out: float32 [2, 768], replicated, may hold values from -3 to 3
- gain_one: float32 [2, 768], replicated, may hold values from 0.1 to 1.9
- shift_one: float32 [2, 768], replicated, may hold values from -3 to 3
- w_up: bfloat16 [2, 768, 3072], replicated, may hold values from -0.21875 to 0.21875
- b_up: float32 [2, 3072], replicated, may hold values from -3 to 3
- w_down: bfloat16 [2, 3072, 768], replicated, may hold values from -0.109375 to 0.109375
- b_down: float32 [2, 768], replicated, may hold values from -3 to 3
- gain_two: float32 [2, 768], replicated, may hold values from 0.1 to 1.9
- shift_two: float32 [2, 768], replicated, may hold values from -3 to 3
Outputs:
- loss: float32 [8], P('dp')
- grad_tokens: float32 [32, 512, 768], P('dp', 'seq')
- grad_w_qkv: float32 [2, 768, 2304], P(None, 'dp')
- grad_b_query: float32 [2, 768], replicated
- grad_b_value: float32 [2, 768], replicated
- grad_w_out: float32 [2, 768, 768], P(None, 'dp')
- grad_b_out: float32 [2, 768], replicated
- grad_gain_one: float32 [2, 768], replicated
- grad_shift_one: float32 [2, 768], replicated
- grad_w_up: float32 [2, 768, 3072], P(None, 'dp')
- grad_b_up: float32 [2, 3072], replicated
- grad_w_down: float32 [2, 3072, 768], P(None, 'dp')
- grad_b_down: float32 [2, 768], replicated
- grad_gain_two: float32 [2, 768], replicated
- grad_shift_two: float32 [2, 768], replicated
The draws below stay inside these ranges and needn't reach their ends.
Inputs may be any that keep to these rules, and one draw needn't show every extreme that they name: `segment_ids`: each row holds exactly 8 segments, numbered 0 to 7 in order of position, each of one or more tokens. The partner of segment i of index g of dp is the segment of number pair_ids[i] among the 32 segments of the same g.
All inputs are finite; a program needn't handle non-finite values.
Results may differ from the reference program's by a relative error of at most 0.02.
Values may be sent and summed in bfloat16 or wider, within the bound.
A program may use at most 256 MiB of HBM per device.

```python
import jax
import jax.numpy as jnp
from jax import lax

D = 768
H = 12
HD = 64
FF = 3072
LAYERS = 2
LEN = 512
SEGS = 8
ROWS = 4
SEQ_DEV = 128
ROWS_ALL = 32
SG = 32
SEG_ALL = 256
N_DP = 8


def draw_segment_ids(key, part):
    key = jax.random.fold_in(key, 11)
    key_pick, key_rows = jax.random.split(key)
    chosen = jax.random.randint(key_pick, (ROWS_ALL // ROWS,), 0, ROWS)
    row_keys = jax.random.split(key_rows, ROWS_ALL)
    row_index = jnp.arange(ROWS_ALL, dtype=jnp.int32)
    spanning_rows = chosen[row_index // ROWS] == row_index % ROWS

    def one_row(row_key, spanning):
        key_free, key_edge = jax.random.split(row_key)
        free_cuts = jax.random.permutation(key_free, LEN - 1)[:SEGS - 1] + 1
        edge_raw = jax.random.permutation(key_edge, 2 * SEQ_DEV - 2)[:SEGS - 1]
        edge_cuts = jnp.where(edge_raw < SEQ_DEV - 1, edge_raw + 1, edge_raw + 2 + LEN - 2 * SEQ_DEV)
        cut_points = jnp.sort(jnp.where(spanning, edge_cuts, free_cuts)).astype(jnp.int32)
        positions = jnp.arange(LEN, dtype=jnp.int32)
        return jnp.sum((positions[:, None] >= cut_points[None, :]).astype(jnp.int32), axis=1).astype(jnp.int32)
    return jax.vmap(one_row)(row_keys, spanning_rows)


def place_ends(drawn, rng, low, high):
    longest = drawn.shape.index(max(drawn.shape))
    spots = []
    for shift in (0, 1):
        where = [jax.random.randint(jax.random.fold_in(rng, axis), (), 0, length) for axis, length in enumerate(drawn.shape)]
        where[longest] = (where[longest] + shift) % drawn.shape[longest]
        spots.append(tuple(where))
    return drawn.at[spots[0]].set(low).at[spots[1]].set(high)


def block_scale(key, extent, pieces, least, largest):
    loudness = 1.0
    for position, parts in pieces:
        draws = jax.random.uniform(jax.random.fold_in(jax.random.fold_in(key, 6), position), (parts,), jnp.float32, least / len(pieces), largest / len(pieces))
        loudness = loudness * jnp.repeat(jnp.exp(draws), extent[position] // parts).reshape((-1,) + (1,) * (len(extent) - 1 - position))
    return loudness


def gaussian(rng, extent, width, bound, cuts=(), kind=jnp.bfloat16):
    entries = jax.random.normal(rng, extent, jnp.float32) * width
    if len(cuts) > 0:
        entries = block_scale(rng, extent, cuts, -0.22, 0.18) * entries
    return jnp.clip(entries, min=-bound, max=bound).astype(kind)


def setup_inputs(seed: int = 0) -> dict:
    key_list = jax.random.split(jax.random.key(seed), 17)
    return {
        "tokens": gaussian(key_list[0], (ROWS_ALL, LEN, D), 1.0, 6.0, ((0, 8), (1, 4))),
        "segment_ids": draw_segment_ids(jax.random.fold_in(key_list[16], 71), 0),
        "pair_ids": place_ends(jax.random.randint(key_list[2], (SEG_ALL,), 0, SG), jax.random.fold_in(key_list[2], 1), 0, SG - 1).astype(jnp.int32),
        "w_qkv": gaussian(key_list[3], (LAYERS, D, 3 * D), D ** -0.5, 0.21875),
        "b_query": gaussian(key_list[4], (LAYERS, D), 0.5, 3.0, (), jnp.float32),
        "b_value": gaussian(key_list[5], (LAYERS, D), 0.5, 3.0, (), jnp.float32),
        "w_out": gaussian(key_list[6], (LAYERS, D, D), (D // 8) ** -0.5, 0.625),
        "b_out": gaussian(key_list[7], (LAYERS, D), 0.5, 3.0, (), jnp.float32),
        "gain_one": jnp.clip(1.0 + 0.18 * jax.random.normal(key_list[8], (LAYERS, D), jnp.float32), 0.1, 1.9),
        "shift_one": gaussian(key_list[9], (LAYERS, D), 0.5, 3.0, (), jnp.float32),
        "w_up": gaussian(key_list[10], (LAYERS, D, FF), D ** -0.5, 0.21875),
        "b_up": gaussian(key_list[11], (LAYERS, FF), 0.5, 3.0, (), jnp.float32),
        "w_down": gaussian(key_list[12], (LAYERS, FF, D), FF ** -0.5, 0.109375),
        "b_down": gaussian(key_list[13], (LAYERS, D), 0.5, 3.0, (), jnp.float32),
        "gain_two": jnp.clip(1.0 + 0.18 * jax.random.normal(key_list[14], (LAYERS, D), jnp.float32), 0.1, 1.9),
        "shift_two": gaussian(key_list[15], (LAYERS, D), 0.5, 3.0, (), jnp.float32),
    }


@jax.custom_vjp
def low(v):
    return lax.optimization_barrier(v.astype(jnp.bfloat16)).astype(jnp.float32)

@jax.custom_vjp
def low_back(v):
    return v

def low_keep(v):
    return (low(v), None)

def low_pass(kept, grad):
    return (grad,)

def back_keep(v):
    return (v, None)

def back_low(kept, grad):
    return (low(grad),)
low.defvjp(low_keep, low_pass)
low_back.defvjp(back_keep, back_low)
highest = lax.Precision.HIGHEST
norm_eps = 1e-06
loss_scale = 1024.0

def layer_norm(values, gain_vec, shift_vec):
    centre = values - lax.optimization_barrier(jnp.mean(values, axis=-1, keepdims=True))
    spread = lax.optimization_barrier(jnp.mean(centre * centre, axis=-1, keepdims=True))
    return centre * lax.rsqrt(spread + norm_eps) * gain_vec + shift_vec

def attend_row(inputs):
    queries, keys_row, values_row, seg_row = inputs
    query_heads = queries.reshape(LEN, H, HD)
    key_heads = keys_row.reshape(LEN, H, HD)
    value_heads = values_row.reshape(LEN, H, HD)
    scores = low_back(jnp.einsum('qhd,khd->hqk', query_heads, key_heads, precision=highest) * 0.125)
    allowed = seg_row[:, None] == seg_row[None, :]
    scores = jnp.where(allowed[None], scores, -1e+30)
    probs_low = low(jax.nn.softmax(scores, axis=-1))
    mixed = jnp.einsum('hqk,khd->qhd', probs_low, value_heads, precision=highest)
    return mixed.reshape(LEN, D)

def encoder_layer(hidden, seg_ids, params):
    w_qkv, b_query, b_value, w_out, b_out, gain_one, shift_one, w_up, b_up, w_down, b_down, gain_two, shift_two = params
    hidden_low = low(hidden)
    bias_all = jnp.concatenate([b_query, jnp.zeros_like(b_query), b_value])
    projected = low_back(low(jnp.einsum('rtd,de->rte', hidden_low, w_qkv, precision=highest) + bias_all))
    queries = projected[..., :D]
    keys_all = projected[..., D:2 * D]
    values_all = projected[..., 2 * D:]
    mixed = lax.map(jax.checkpoint(attend_row), (queries, keys_all, values_all, seg_ids))
    mixed = low_back(low(mixed))
    branch = low_back(jnp.einsum('rtd,de->rte', mixed, w_out, precision=highest) + b_out)
    normed = layer_norm(hidden + branch, gain_one, shift_one)
    pre_act = low_back(jnp.einsum('rtd,de->rte', low(normed), w_up, precision=highest) + b_up)
    activated = low(jax.nn.gelu(pre_act, approximate=False))
    second = low_back(jnp.einsum('rtf,fd->rtd', activated, w_down, precision=highest) + b_down)
    return layer_norm(normed + second, gain_two, shift_two)

def pooled_loss(pooled_sums, counts, pair_group):
    embed = pooled_sums / counts[:, None]
    unit = embed * lax.rsqrt(lax.optimization_barrier(jnp.sum(embed * embed, axis=-1, keepdims=True)) + norm_eps)
    logits = 20.0 * jnp.dot(unit, unit.T, precision=highest)
    chosen = pair_group[:, None] == jnp.arange(SG, dtype=jnp.int32)[None, :]
    picked = lax.optimization_barrier(jnp.sum(jnp.where(chosen, logits, 0.0), axis=-1))
    return jnp.mean(jax.nn.logsumexp(logits, axis=-1) - picked)

def group_loss(hidden, seg_ids, pair_group, params):
    for layer_index in range(LAYERS):
        hidden = encoder_layer(hidden, seg_ids, tuple((stacked[layer_index] for stacked in params)))
    global_ids = seg_ids + SEGS * jnp.arange(ROWS, dtype=jnp.int32)[:, None]
    member = (global_ids.reshape(-1)[:, None] == jnp.arange(SG, dtype=jnp.int32)[None, :]).astype(jnp.float32)
    pooled_sums = jnp.dot(member.T, hidden.reshape(-1, D), precision=highest)
    counts = lax.optimization_barrier(jnp.sum(member, axis=0))
    return pooled_loss(pooled_sums, counts, pair_group)

def reference(tokens, segment_ids, pair_ids, w_qkv, b_query, b_value, w_out, b_out, gain_one, shift_one, w_up, b_up, w_down, b_down, gain_two, shift_two):
    params = tuple((stacked.astype(jnp.float32) for stacked in (w_qkv, b_query, b_value, w_out, b_out, gain_one, shift_one, w_up, b_up, w_down, b_down, gain_two, shift_two)))
    hidden_all = tokens.astype(jnp.float32).reshape(N_DP, ROWS, LEN, D)
    seg_all = segment_ids.reshape(N_DP, ROWS, LEN)
    pair_all = pair_ids.reshape(N_DP, SG)

    def one_group(totals, inputs):
        group_tokens, group_segs, group_pairs = inputs
        loss_value, pullback = jax.vjp(lambda hid_in, prm: group_loss(hid_in, group_segs, group_pairs, prm), group_tokens, params)
        grad_input, grad_params = pullback(jnp.asarray(loss_scale, loss_value.dtype))
        totals = jax.tree.map(lambda left, right: left + right, totals, grad_params)
        return (totals, (loss_value, grad_input))
    zeros = jax.tree.map(jnp.zeros_like, params)
    totals, (losses, grad_input) = lax.scan(one_group, zeros, (hidden_all, seg_all, pair_all))
    return (losses, grad_input.reshape(ROWS_ALL, LEN, D), totals[0], totals[1], totals[2], totals[3], totals[4], totals[5], totals[6], totals[7], totals[8], totals[9], totals[10], totals[11], totals[12])
```

```python
import functools

import jax
import jax.numpy as jnp
from jax import lax
from jax.experimental import pallas as pl
from jax.experimental.pallas import tpu as pltpu
from jax.sharding import PartitionSpec as P

highest = lax.Precision.HIGHEST
loss_scale = 1024.0
HD = 64
norm_eps = 1e-06
FT = 512


def dot(left, right):
    return lax.dot_general(left, right, (((1,), (0,)), ((), ())), preferred_element_type=jnp.float32)


def dot_t(left, right):
    return lax.dot_general(left, right, (((1,), (1,)), ((), ())), preferred_element_type=jnp.float32)


def gelu_pair(x):
    t = 1.0 / (1.0 + 0.23164190 * jnp.abs(x))
    gauss = jnp.exp(-0.5 * x * x)
    poly = t * (0.127414796 + t * (-0.142248368 + t * (0.7107068705 + t * (-0.7265760135 + t * 0.5307027145))))
    tail = poly * gauss
    phi = jnp.where(x >= 0.0, 1.0 - tail, tail)
    return x * phi, phi + x * (gauss * 0.3989422804014327)


def fwd_kernel(
    layers, tok, segc, segr, b_query, b_value, b_out, gain_one, shift_one, b_up, b_down, gain_two, shift_two,
    w_qkv, w_out, w_up, w_down,
    hid_out, o_qkv, o_p, o_rl, o_pv, o_hidT, o_mixT, o_nrmT, o_actT, o_gp, o_n1, o_r1, o_n2, o_r2,
    wq, wo, wu, wd, bias, hid, low, qkv, pb, rl, pv, mix, nrm, gp, n1, r1, n2, r2, hidT, mixT, nrmT, actT, acc,
    wsem, psem, osem,
):
    T, D = tok.shape
    FF = w_up.shape[2]
    for l in range(layers):
        for i, (src, dst) in enumerate(((w_qkv, wq), (w_out, wo), (w_up, wu), (w_down, wd))):
            pltpu.make_async_copy(src.at[l], dst.at[l], wsem.at[l, i]).start()

    def wwait(l, i):
        src, dst = ((w_qkv, wq), (w_out, wo), (w_up, wu), (w_down, wd))[i]
        pltpu.make_async_copy(src.at[l], dst.at[l], wsem.at[l, i]).wait()

    bias[...] = jnp.where(segc[...] == segr[...], 0.0, -1e30)
    hid[...] = tok[...].astype(jnp.float32)
    lane = lax.broadcasted_iota(jnp.int32, (T, 128), 1)
    first = lane < HD

    def transpose(src, dst, n):
        def body(i, c):
            o = pl.multiple_of(i * 128, 128)
            dst[pl.ds(o, 128), :] = src[:, pl.ds(o, 128)].T
            return c
        lax.fori_loop(0, n // 128, body, 0)

    RB = 64

    def rows(fn):
        def body(i, c):
            fn(pl.ds(pl.multiple_of(i * RB, RB), RB))
            return c
        lax.fori_loop(0, T // RB, body, 0)

    outs = []

    def norm(x, gain, shift):
        centre = x - jnp.mean(x, axis=-1, keepdims=True)
        scaled = lax.rsqrt(jnp.mean(centre * centre, axis=-1, keepdims=True) + norm_eps)
        normal = centre * scaled
        return normal * gain + shift, normal, scaled

    def ship(l, src, dst, k):
        c = pltpu.make_async_copy(src, dst.at[l], osem.at[k])
        c.start()
        outs.append(c)

    for l in range(layers):
        low[...] = hid[...].astype(jnp.bfloat16)
        for c in outs:
            c.wait()
        outs.clear()
        wwait(l, 0)
        lb = low[...]
        for k in range(3):
            cols = slice(k * D, (k + 1) * D)
            y = dot(lb, wq[l, :, cols])
            if k == 0:
                y = (y + b_query[l : l + 1, :]) * 0.125
            if k == 2:
                y = y + b_value[l : l + 1, :]
            qkv[:, cols] = y.astype(jnp.bfloat16)
        ship(l, qkv, o_qkv, 0)
        transpose(low, hidT, D)
        ship(l, hidT, o_hidT, 1)

        def pcopy(i, s):
            return pltpu.make_async_copy(pb.at[s], o_p.at[l, pl.ds(2 * i, 2)], psem.at[s])

        def attend(i, c):
            s = lax.rem(i, 2)
            o = pl.multiple_of(i * 128, 128)
            q2, k2, v2 = (qkv[:, pl.ds(o + k * D, 128)] for k in range(3))

            @pl.when(i >= 2)
            def _():
                pcopy(i - 2, s).wait()

            zero = jnp.zeros_like(q2)
            total = None
            recips = []
            for h in range(2):
                sel = first if h == 0 else ~first
                sc = dot_t(jnp.where(sel, q2, zero), k2) + bias[...]
                e = jnp.exp(sc - jnp.max(sc, axis=-1, keepdims=True))
                recips.append(1.0 / jnp.sum(e, axis=-1, keepdims=True))
                p = e.astype(jnp.bfloat16)
                pb[s, h] = p
                part = dot(p, jnp.where(sel, v2, zero))
                total = part if h == 0 else total + part
            r = jnp.where(first, recips[0], recips[1])
            rl[:, pl.ds(o, 128)] = r
            total = total * r
            pv[:, pl.ds(o, 128)] = total
            mix[:, pl.ds(o, 128)] = total.astype(jnp.bfloat16)
            pcopy(i, s).start()
            return c

        n_pairs = D // 128
        lax.fori_loop(0, n_pairs, attend, 0)
        ship(l, rl, o_rl, 2)
        ship(l, pv, o_pv, 3)
        wwait(l, 1)
        acc[...] = dot(mix[...], wo[l])
        transpose(mix, mixT, D)
        ship(l, mixT, o_mixT, 4)

        def first_norm(rs):
            x = hid[rs, :] + acc[rs, :] + b_out[l : l + 1, :]
            y, n, r = norm(x, gain_one[l : l + 1, :], shift_one[l : l + 1, :])
            nrm[rs, :] = y
            low[rs, :] = y.astype(jnp.bfloat16)
            n1[rs, :] = n.astype(jnp.bfloat16)
            r1[rs, :] = jnp.broadcast_to(r, (RB, 128))

        rows(first_norm)
        ship(l, n1, o_n1, 5)
        ship(l, r1, o_r1, 6)
        transpose(low, nrmT, D)
        ship(l, nrmT, o_nrmT, 7)
        wwait(l, 2)
        wwait(l, 3)
        acc[...] = nrm[...]

        def ffn(j, c):
            o = pl.multiple_of(j * FT, FT)
            pre = dot(low[...], wu[l, :, pl.ds(o, FT)]) + b_up[l : l + 1, pl.ds(o, FT)]
            a, g = gelu_pair(pre)
            al = a.astype(jnp.bfloat16)
            gp[:, pl.ds(o, FT)] = g.astype(jnp.bfloat16)
            acc[...] += dot(al, wd[l, pl.ds(o, FT), :])
            actT[pl.ds(o, FT), :] = al.T
            return c

        lax.fori_loop(0, FF // FT, ffn, 0)
        ship(l, gp, o_gp, 8)
        ship(l, actT, o_actT, 9)

        def second_norm(rs):
            x = acc[rs, :] + b_down[l : l + 1, :]
            y, n, r = norm(x, gain_two[l : l + 1, :], shift_two[l : l + 1, :])
            hid[rs, :] = y
            n2[rs, :] = n.astype(jnp.bfloat16)
            r2[rs, :] = jnp.broadcast_to(r, (RB, 128))

        rows(second_norm)
        ship(l, n2, o_n2, 10)
        ship(l, r2, o_r2, 11)
        for i in (n_pairs - 2, n_pairs - 1):
            pcopy(i, i % 2).wait()
    hid_out[...] = hid[...]
    for c in outs:
        c.wait()


def forward(tok, seg, w):
    T, D = tok.shape
    L = w["w_qkv"].shape[0]
    FF = w["w_up"].shape[2]
    bf, f32 = jnp.bfloat16, jnp.float32
    S = jax.ShapeDtypeStruct
    vm = pl.BlockSpec(memory_space=pltpu.VMEM)
    anyspec = pl.BlockSpec(memory_space=pl.ANY)
    H = D // HD
    out_shape = (
        S((T, D), f32), S((L, T, 3 * D), bf), S((L, H, T, T), bf), S((L, T, D), f32), S((L, T, D), f32),
        S((L, D, T), bf), S((L, D, T), bf), S((L, D, T), bf), S((L, FF, T), bf), S((L, T, FF), bf),
        S((L, T, D), bf), S((L, T, 128), f32), S((L, T, D), bf), S((L, T, 128), f32),
    )
    V = pltpu.VMEM
    scratch = [
        V((L, D, 3 * D), bf), V((L, D, D), bf), V((L, D, FF), bf), V((L, FF, D), bf),
        V((T, T), f32), V((T, D), f32), V((T, D), bf), V((T, 3 * D), bf), V((2, 2, T, T), bf),
        V((T, D), f32), V((T, D), f32), V((T, D), bf), V((T, D), f32), V((T, FF), bf),
        V((T, D), bf), V((T, 128), f32), V((T, D), bf), V((T, 128), f32),
        V((D, T), bf), V((D, T), bf), V((D, T), bf), V((FF, T), bf), V((T, D), f32),
        pltpu.SemaphoreType.DMA((L, 4)), pltpu.SemaphoreType.DMA((2,)), pltpu.SemaphoreType.DMA((12,)),
    ]
    return pl.pallas_call(
        functools.partial(fwd_kernel, L),
        out_shape=out_shape,
        in_specs=[vm] * 12 + [anyspec] * 4,
        out_specs=(vm,) + (anyspec,) * 13,
        scratch_shapes=scratch,
        compiler_params=pltpu.CompilerParams(vmem_limit_bytes=60 * 1024 * 1024),
        name="forward",
    )(
        tok, seg.reshape(T, 1), seg.reshape(1, T),
        *(w[k] for k in ("b_query", "b_value", "b_out", "gain_one", "shift_one", "b_up", "b_down", "gain_two", "shift_two")),
        *(w[k] for k in ("w_qkv", "w_out", "w_up", "w_down")),
    )


MESH = pl.DeviceIdType.MESH
C = 256
CORE_SLOTS = 4
SLOTS = 6
LAGS = (0, 1, 3, 5, 7, 9, 11)
VEC_ROWS = 16
WAYS = 8


def low_sum(one, other):
    return (one.astype(jnp.float32) + other.astype(jnp.float32)).astype(jnp.bfloat16)


def remote(src, dst, send_sem, recv_sem, where):
    return pltpu.make_async_remote_copy(
        src_ref=src, dst_ref=dst, send_sem=send_sem, recv_sem=recv_sem, device_id=where, device_id_type=MESH
    )


def bwd_kernel(
    layers, g_in, gain_one, gain_two,
    w_qkv, w_out, w_up, w_down,
    h_qkv, h_p, h_rl, h_pv, h_hidT, h_mixT, h_nrmT, h_actT, h_gp, h_n1, h_r1, h_n2, h_r2,
    out, gt_out, vec_out,
    wq, wo, wu, wd, qkv, pb, rl, pv, hidT, mixT, nrmT, actT, gp, n1, r1, n2, r2,
    acc, second, branch, gm, rhsA, rhsB, vec, vrecv, gb,
    sendc, keepc, recvc, s1, k1, t1, s2, k2, t2, za, zr, zb, zt, zf,
    ldsem, psem, csem, xsem, ysem, zsem, osem, vsem, gsem,
):
    T, D = g_in.shape
    FF = w_up.shape[2]
    R = D // WAYS
    n_ffn = FF // C
    n_att = D // 128
    per = n_ffn + n_att
    n_steps = layers * per
    n_ct = D // C
    n_rb = FF // WAYS // R

    me = lax.axis_index("dp")
    zi = lax.axis_index("seq")
    oc = lax.rem(me, 2)
    ox = lax.rem(lax.div(me, 2), 2)
    oy = lax.rem(lax.div(me, 4), 2)
    core = (me + 1 - 2 * oc, zi)
    xdev = (me + 2 - 4 * ox, zi)
    ydev = (me + 4 - 8 * oy, zi)
    inner = (zi == 1) | (zi == 2)
    outer = (zi == 0) | (zi == 3)
    to_inner = (me, 1 + lax.div(zi, 2))
    across = (me, 3 - zi)
    to_outer = (me, 3 * lax.div(zi, 2))

    barrier = pltpu.get_barrier_semaphore()
    peers = [core, xdev, ydev] + [(me, lax.rem(zi + k, 4)) for k in range(1, 4)]
    for peer in peers:
        pl.semaphore_signal(barrier, inc=1, device_id=peer, device_id_type=MESH)
    pl.semaphore_wait(barrier, len(peers))

    def place(ic, i):
        y = lax.rem(oy + i // 2, 2)
        x = lax.rem(ox + i % 2, 2)
        return 4 * y + 2 * x + lax.rem(oc + ic, 2)

    def turned(src, dst, l):
        return [
            (src.at[l, place(ic, i)], dst.at[ic, pl.ds(i * R, R)]) for ic in range(2) for i in range(4)
        ]

    def group_ffn(l):
        parts = [(w_down.at[l], wd), (w_up.at[l], wu), (h_gp.at[l], gp), (h_n2.at[l], n2), (h_r2.at[l], r2)]
        parts += turned(h_nrmT, nrmT, l)
        for ic in range(2):
            for i in range(4):
                for rb in range(n_rb):
                    parts.append((h_actT.at[l, place(ic, i), rb], actT.at[ic, rb, pl.ds(i * R, R)]))
        return [pltpu.make_async_copy(a, b, ldsem.at[0, k]) for k, (a, b) in enumerate(parts)]

    def group_att(l):
        parts = [(w_out.at[l], wo), (w_qkv.at[l], wq), (h_qkv.at[l], qkv), (h_rl.at[l], rl), (h_pv.at[l], pv)]
        parts += [(h_n1.at[l], n1), (h_r1.at[l], r1)]
        parts += turned(h_hidT, hidT, l) + turned(h_mixT, mixT, l)
        return [pltpu.make_async_copy(a, b, ldsem.at[1, k]) for k, (a, b) in enumerate(parts)]

    def pcopy(l, i):
        s = lax.rem(i, 2)
        return pltpu.make_async_copy(h_p.at[l, pl.ds(2 * i, 2)], pb.at[s], psem.at[s])

    for c in group_ffn(layers - 1) + group_att(layers - 1):
        c.start()

    acc[...] = g_in[...]
    vec[...] = jnp.zeros_like(vec)
    lane = lax.broadcasted_iota(jnp.int32, (T, 128), 1)
    first = lane < HD
    RB = 64

    def rows(fn):
        def body(i, sums):
            return tuple(a + b for a, b in zip(sums, fn(pl.ds(pl.multiple_of(i * RB, RB), RB))))
        zero = jnp.zeros((1, D), jnp.float32)
        return lax.fori_loop(0, T // RB, body, (zero, zero, zero))

    def norm_back(g, n, r, gain):
        e = g * gain
        return r * (e - jnp.mean(e, axis=-1, keepdims=True) - n * jnp.mean(e * n, axis=-1, keepdims=True))

    def col_sum(v):
        return jnp.sum(v.astype(jnp.float32), axis=0, keepdims=True)

    def prologue(l):
        for c in group_ffn(l):
            c.wait()

        def fn(rs):
            g = acc[rs, :]
            n = n2[rs, :].astype(jnp.float32)
            d = norm_back(g, n, r2[rs, :1], gain_two[l])
            acc[rs, :] = d
            low = d.astype(jnp.bfloat16)
            second[rs, :] = low
            return col_sum(low), col_sum(g * n), col_sum(g)

        a, b, c = rows(fn)
        vec[l, 9:10, :] = a
        vec[l, 10:11, :] = b
        vec[l, 11:12, :] = c

    def ffn(l, j, slot):
        o = pl.multiple_of(j * C, C)
        ga = dot_t(second[...], wd[pl.ds(o, C), :])
        gpre = (ga * gp[:, pl.ds(o, C)].astype(jnp.float32)).astype(jnp.bfloat16)
        ct = lax.rem(j, n_ct)
        rb = lax.div(j, n_ct)
        cols = pl.ds(pl.multiple_of(ct * C, C), C)
        vec[l, pl.ds(5 + rb, 1), cols] = col_sum(gpre)
        sec = second[:, cols]
        for ic, buf in ((1, sendc), (0, keepc)):
            buf[slot, 0] = dot(nrmT[ic], gpre).astype(jnp.bfloat16)
            buf[slot, 1] = dot(actT[ic, rb], sec).astype(jnp.bfloat16)
        acc[...] += dot_t(gpre, wu[:, pl.ds(o, C)])

    def middle(l):
        for c in group_att(l):
            c.wait()

        def fn(rs):
            g = acc[rs, :]
            n = n1[rs, :].astype(jnp.float32)
            d = norm_back(g, n, r1[rs, :1], gain_one[l])
            acc[rs, :] = d
            low = d.astype(jnp.bfloat16)
            branch[rs, :] = low
            return col_sum(low), col_sum(g * n), col_sum(g)

        a, b, c = rows(fn)
        vec[l, 2:3, :] = a
        vec[l, 3:4, :] = b
        vec[l, 4:5, :] = c
        gm[...] = (dot_t(branch[...], wo[...]) * rl[...]).astype(jnp.bfloat16)

    def attend(l, i, slot):
        o = pl.multiple_of(i * 128, 128)
        ps = lax.rem(i, 2)
        pcopy(l, i).wait()
        q2, k2, v2 = (qkv[:, pl.ds(o + k * D, 128)] for k in range(3))
        g2 = gm[:, pl.ds(o, 128)]
        weighed = g2.astype(jnp.float32) * pv[:, pl.ds(o, 128)]
        zero = jnp.zeros_like(q2)
        q2t, g2t = q2.T, g2.T
        dq = None
        dkt, dvt = [], []
        for h in range(2):
            sel = first if h == 0 else ~first
            p = pb[ps, h]
            gprob = dot_t(jnp.where(sel, g2, zero), v2)
            centre = jnp.sum(jnp.where(sel, weighed, 0.0), axis=-1, keepdims=True)
            ds = (p.astype(jnp.float32) * (gprob - centre)).astype(jnp.bfloat16)
            part = dot(ds, jnp.where(sel, k2, zero))
            dq = part if h == 0 else dq + part
            dkt.append(dot(q2t[h * HD : (h + 1) * HD], ds))
            dvt.append(dot(g2t[h * HD : (h + 1) * HD], p))
        dq = (dq * 0.125).astype(jnp.bfloat16)
        dk = jnp.concatenate(dkt, axis=0).astype(jnp.bfloat16).T
        dv = jnp.concatenate(dvt, axis=0).astype(jnp.bfloat16).T
        vec[l, 0:1, pl.ds(o, 128)] = col_sum(dq)
        vec[l, 1:2, pl.ds(o, 128)] = col_sum(dv)
        rhsA[:, :128] = dq
        rhsA[:, 128:] = dk
        rhsB[:, :128] = dv
        rhsB[:, 128:] = branch[:, pl.ds(o, 128)]
        for ic, buf in ((1, sendc), (0, keepc)):
            buf[slot, 0] = dot(hidT[ic], rhsA[...]).astype(jnp.bfloat16)
            buf[slot, 1, :, :128] = dot(hidT[ic], rhsB[:, :128]).astype(jnp.bfloat16)
            buf[slot, 1, :, 128:] = dot(mixT[ic], rhsB[:, 128:]).astype(jnp.bfloat16)
        acc[...] += (
            dot_t(dq, wq[:, pl.ds(o, 128)]) + dot_t(dk, wq[:, pl.ds(o + D, 128)]) + dot_t(dv, wq[:, pl.ds(o + 2 * D, 128)])
        )

        @pl.when(i + 2 < n_att)
        def _():
            pcopy(l, i + 2).start()

    def copy_core(u):
        s = lax.rem(u, CORE_SLOTS)
        return remote(sendc.at[s], recvc.at[s], csem.at[0, s], csem.at[1, s], core)

    def copies_one(u):
        s = lax.rem(u, SLOTS)
        return [
            remote(s1.at[s, k], t1.at[s, k], xsem.at[0, k, s], xsem.at[1, k, s], (xdev, ydev)[k]) for k in range(2)
        ]

    def copies_two(u):
        s = lax.rem(u, SLOTS)
        return [
            remote(s2.at[s, k], t2.at[s, k], ysem.at[0, k, s], ysem.at[1, k, s], (ydev, xdev)[k]) for k in range(2)
        ]

    def copy_in(u):
        s = lax.rem(u, SLOTS)
        return remote(za.at[s], zr.at[s], zsem.at[0, s], zsem.at[1, s], to_inner)

    def copy_across(u):
        s = lax.rem(u, SLOTS)
        return remote(zb.at[s], zt.at[s], zsem.at[2, s], zsem.at[3, s], across)

    def copy_out(u):
        s = lax.rem(u, SLOTS)
        return remote(zf.at[s], out.at[u], zsem.at[4, s], zsem.at[5, s], to_outer)

    def copy_home(u):
        s = lax.rem(u, SLOTS)
        return pltpu.make_async_copy(zf.at[s], out.at[u], osem.at[s])

    def at(t, stage):
        u = t - LAGS[stage]
        return u, (u >= 0) & (u < n_steps)

    def stage_one(u):
        s = lax.rem(u, CORE_SLOTS)
        d = lax.rem(u, SLOTS)
        copy_core(u).wait()
        for k in range(2):
            sent, kept = ((1, 3), (0, 2)) if k == 0 else ((2, 3), (0, 1))
            for n, (a, b) in enumerate(zip(sent, kept)):
                to = pl.ds(n * R, R)
                s1[d, k, to] = low_sum(keepc[s, k, pl.ds(a * R, R)], recvc[s, k, pl.ds(a * R, R)])
                k1[d, k, to] = low_sum(keepc[s, k, pl.ds(b * R, R)], recvc[s, k, pl.ds(b * R, R)])
        for c in copies_one(u):
            c.start()

    def stage_two(u):
        d = lax.rem(u, SLOTS)
        for c in copies_one(u):
            c.wait()
        for k in range(2):
            s2[d, k] = low_sum(k1[d, k, pl.ds(R, R)], t1[d, k, pl.ds(R, R)])
            k2[d, k] = low_sum(k1[d, k, pl.ds(0, R)], t1[d, k, pl.ds(0, R)])
        for c in copies_two(u):
            c.start()

    def stage_three(u):
        d = lax.rem(u, SLOTS)
        for c in copies_two(u):
            c.wait()
        za[d] = low_sum(k2[d], t2[d])

        @pl.when(outer)
        def _():
            copy_in(u).start()

    def stage_four(u):
        d = lax.rem(u, SLOTS)

        @pl.when(outer)
        def _():
            copy_in(u).wait_send()

        @pl.when(inner)
        def _():
            copy_in(u).wait_recv()
            zb[d] = low_sum(za[d], zr[d])
            copy_across(u).start()

    def stage_five(u):
        d = lax.rem(u, SLOTS)

        @pl.when(inner)
        def _():
            copy_across(u).wait()
            zf[d] = low_sum(zb[d], zt[d])
            copy_out(u).start()
            copy_home(u).start()

    def stage_six(u):
        @pl.when(inner)
        def _():
            copy_out(u).wait_send()
            copy_home(u).wait()

        @pl.when(outer)
        def _():
            copy_out(u).wait_recv()

    stages = (None, stage_one, stage_two, stage_three, stage_four, stage_five, stage_six)

    swaps = (core, xdev, ydev)

    def vec_copy(k):
        where = swaps[k] if k < 3 else (to_inner, across, to_outer)[k - 3]
        return remote(vec, vrecv.at[k], vsem.at[0, k], vsem.at[1, k], where)

    def vec_step(k):
        if 1 <= k <= 3:
            vec_copy(k - 1).wait()
            vec[...] += vrecv[k - 1]
        if k < 3:
            vec_copy(k).start()
        if k == 3:
            @pl.when(outer)
            def _():
                vec_copy(3).start()
        if k == 4:
            @pl.when(outer)
            def _():
                vec_copy(3).wait_send()

            @pl.when(inner)
            def _():
                vec_copy(3).wait_recv()
                vec[...] += vrecv[3]
                vec_copy(4).start()
        if k == 5:
            @pl.when(inner)
            def _():
                vec_copy(4).wait()
                vec[...] += vrecv[4]
                vec_copy(5).start()
        if k == 6:
            @pl.when(inner)
            def _():
                vec_copy(5).wait_send()
                vec_out[...] = vec[...]

            @pl.when(outer)
            def _():
                vec_copy(5).wait_recv()
                vec_out[...] = vrecv[5]

    part = T // 4

    def gt_copy(k):
        peer = lax.rem(zi + k, 4)
        src = gb.at[pl.ds(pl.multiple_of(peer * part, part), part)]
        if k == 0:
            return pltpu.make_async_copy(src, gt_out.at[zi], gsem.at[0, 0])
        return remote(src, gt_out.at[zi], gsem.at[0, k], gsem.at[1, k], (me, peer))

    def step(t, carry):
        for k in range(6, 0, -1):
            u, live = at(t, k)

            @pl.when(live)
            def _(k=k, u=u):
                stages[k](u)

        l = layers - 1 - lax.div(t, per)
        s = lax.rem(t, per)
        slot = lax.rem(t, CORE_SLOTS)
        busy = t < n_steps

        @pl.when(busy & (s == 0))
        def _():
            prologue(l)

        @pl.when(busy & (s == 0) & (l < layers - 1))
        def _():
            for c in group_att(l):
                c.start()

        @pl.when(busy & (s < n_ffn))
        def _():
            ffn(l, s, slot)

        @pl.when(busy & (s == n_ffn - 2))
        def _():
            pcopy(l, jnp.int32(0)).start()
            pcopy(l, jnp.int32(1)).start()

        @pl.when(busy & (s == n_ffn) & (l > 0))
        def _():
            for c in group_ffn(l - 1):
                c.start()

        @pl.when(busy & (s == n_ffn))
        def _():
            middle(l)

        @pl.when(busy & (s >= n_ffn))
        def _():
            attend(l, s - n_ffn, slot)

        @pl.when(busy)
        def _():
            copy_core(t).start()

        @pl.when(t == n_steps)
        def _():
            gb[...] = acc[...].astype(jnp.bfloat16)
            for k in range(4):
                gt_copy(k).start()

        for k in range(7):
            @pl.when(t == n_steps + k)
            def _(k=k):
                vec_step(k)

        return carry

    lax.fori_loop(0, n_steps + LAGS[6] + 1, step, 0)
    for k in range(4):
        gt_copy(k).wait()


def backward(grad_hidden, res, w):
    T, D = grad_hidden.shape
    L = w["w_qkv"].shape[0]
    FF = w["w_up"].shape[2]
    qkv, p, rl, pv, hidT, mixT, nrmT, actT, gp, n1, r1, n2, r2 = res
    bf, f32 = jnp.bfloat16, jnp.float32
    S = jax.ShapeDtypeStruct
    V = pltpu.VMEM
    vm = pl.BlockSpec(memory_space=pltpu.VMEM)
    anyspec = pl.BlockSpec(memory_space=pl.ANY)
    R = D // WAYS
    n_rb = FF // WAYS // R
    n_steps = L * (FF // C + D // 128)
    U = 4 * R
    dma = pltpu.SemaphoreType.DMA
    scratch = [
        V((D, 3 * D), bf), V((D, D), bf), V((D, FF), bf), V((FF, D), bf),
        V((T, 3 * D), bf), V((2, 2, T, T), bf), V((T, D), f32), V((T, D), f32),
        V((2, U, T), bf), V((2, U, T), bf), V((2, U, T), bf), V((2, n_rb, U, T), bf),
        V((T, FF), bf), V((T, D), bf), V((T, 128), f32), V((T, D), bf), V((T, 128), f32),
        V((T, D), f32), V((T, D), bf), V((T, D), bf), V((T, D), bf), V((T, C), bf), V((T, C), bf),
        V((L, VEC_ROWS, D), f32), V((6, L, VEC_ROWS, D), f32), V((T, D), bf),
        V((CORE_SLOTS, 2, U, C), bf), V((CORE_SLOTS, 2, U, C), bf), V((CORE_SLOTS, 2, U, C), bf),
        V((SLOTS, 2, 2 * R, C), bf), V((SLOTS, 2, 2 * R, C), bf), V((SLOTS, 2, 2 * R, C), bf),
        V((SLOTS, 2, R, C), bf), V((SLOTS, 2, R, C), bf), V((SLOTS, 2, R, C), bf),
        V((SLOTS, 2, R, C), bf), V((SLOTS, 2, R, C), bf), V((SLOTS, 2, R, C), bf),
        V((SLOTS, 2, R, C), bf), V((SLOTS, 2, R, C), bf),
        dma((2, 16 + 8 * n_rb)), dma((2,)), dma((2, CORE_SLOTS)), dma((2, 2, SLOTS)), dma((2, 2, SLOTS)),
        dma((6, SLOTS)), dma((SLOTS,)), dma((2, 6)), dma((2, 4)),
    ]
    return pl.pallas_call(
        functools.partial(bwd_kernel, L),
        out_shape=(
            S((n_steps, 2, R, C), bf), S((4, T // 4, D), bf), S((L, VEC_ROWS, D), f32),
        ),
        in_specs=[vm] * 3 + [anyspec] * 17,
        out_specs=(anyspec, anyspec, vm),
        scratch_shapes=scratch,
        compiler_params=pltpu.CompilerParams(
            vmem_limit_bytes=62 * 1024 * 1024, collective_id=0, has_side_effects=True
        ),
        name="backward",
    )(
        grad_hidden, w["gain_one"].reshape(L, 1, D), w["gain_two"].reshape(L, 1, D),
        *(w[k] for k in ("w_qkv", "w_out", "w_up", "w_down")),
        qkv, p, rl, pv, hidT, mixT, nrmT, actT, gp, n1, r1, n2, r2,
    )


def pooled_loss(pooled_sums, counts, pair_local):
    embed = pooled_sums / counts[:, None]
    unit = embed * lax.rsqrt(jnp.sum(embed * embed, axis=-1, keepdims=True) + norm_eps)
    logits = 20.0 * jnp.dot(unit, unit.T, precision=highest)
    chosen = pair_local[:, None] == jnp.arange(pair_local.shape[0], dtype=jnp.int32)[None, :]
    picked = jnp.sum(jnp.where(chosen, logits, 0.0), axis=-1)
    return jnp.mean(jax.nn.logsumexp(logits, axis=-1) - picked)


NAMES = (
    "w_qkv",
    "b_query",
    "b_value",
    "w_out",
    "b_out",
    "gain_one",
    "shift_one",
    "w_up",
    "b_up",
    "w_down",
    "b_down",
    "gain_two",
    "shift_two",
)


def by_class(array, block, ways):
    layers, rows, tokens_here = array.shape
    if ways == 1:
        return array.reshape(layers, WAYS, -1, tokens_here)
    array = array.reshape(layers, ways, WAYS, block, tokens_here)
    return jnp.swapaxes(array, 1, 2).reshape(layers, WAYS, -1, tokens_here)


def on_device(dp_count, tokens, segment_ids, pair_ids, *weights):
    w = dict(zip(NAMES, weights))
    layer_count, model_width, _ = w["w_qkv"].shape
    hidden_units = w["w_up"].shape[2]
    seg_count = pair_ids.shape[0]
    local_segs = seg_count // tokens.shape[0]
    ways = dp_count // WAYS
    row_tokens = lax.all_to_all(tokens, "seq", 0, 1, tiled=True)[0]
    row_ids = lax.all_to_all(segment_ids, "seq", 0, 1, tiled=True)[0]
    hidden, *res = forward(row_tokens, row_ids, w)
    for place in (4, 5, 6):
        res[place] = by_class(res[place], model_width // dp_count, ways)
    block = model_width // WAYS
    acts = by_class(res[7], hidden_units // dp_count, ways)
    res[7] = acts.reshape(layer_count, WAYS, -1, block, acts.shape[-1])
    member = (
        row_ids[:, None] == jnp.arange(local_segs, dtype=jnp.int32)[None, :]
    ).astype(jnp.float32)
    pooled_sums = jnp.einsum("ts,td->sd", member, hidden, precision=highest)
    counts = jnp.sum(member, axis=0)
    pooled_sums = lax.all_gather(pooled_sums, "seq", axis=0, tiled=True)
    counts = lax.all_gather(counts, "seq", axis=0, tiled=True)
    loss_value, pullback = jax.vjp(
        lambda sums_in: pooled_loss(sums_in, counts, pair_ids), pooled_sums
    )
    grad_sums = pullback(jnp.float32(loss_scale))[0]
    grad_sums = lax.dynamic_slice_in_dim(
        grad_sums, lax.axis_index("seq") * local_segs, local_segs, 0
    )
    grad_hidden = jnp.einsum("ts,sd->td", member, grad_sums, precision=highest)
    units, grad_tokens, vec = backward(grad_hidden, res, w)
    if ways > 1:
        groups = [[low + WAYS * high for high in range(ways)] for low in range(WAYS)]
        vec = lax.psum(vec, "dp", axis_index_groups=groups)
    matrices = unpack(units, layer_count, model_width, hidden_units)
    if ways > 1:
        matrices = [
            lax.psum_scatter(
                matrix, "dp", scatter_dimension=1, axis_index_groups=groups, tiled=True
            )
            for matrix in matrices
        ]
    g_qkv, g_out, g_up, g_down = (matrix.astype(jnp.float32) for matrix in matrices)
    up_rows = hidden_units // model_width
    vectors = [vec[:, row] for row in (0, 1, 2, 3, 4)]
    b_up = vec[:, 5 : 5 + up_rows].reshape(layer_count, hidden_units)
    b_down, gain_two, shift_two = (vec[:, 5 + up_rows + row] for row in range(3))
    return (
        loss_value.reshape(1),
        grad_tokens.astype(jnp.float32),
        g_qkv,
        vectors[0],
        vectors[1],
        g_out,
        vectors[2],
        vectors[3],
        vectors[4],
        g_up,
        b_up,
        g_down,
        b_down,
        gain_two,
        shift_two,
    )


def unpack(units, layer_count, model_width, hidden_units):
    block = model_width // WAYS
    n_ffn = hidden_units // C
    n_att = model_width // 128
    n_ct = model_width // C
    units = units.reshape(layer_count, n_ffn + n_att, 2, block, C)[::-1]
    up = units[:, :n_ffn, 0].transpose(0, 2, 1, 3).reshape(layer_count, block, hidden_units)
    down = units[:, :n_ffn, 1].reshape(layer_count, -1, n_ct, block, C)
    down = down.transpose(0, 1, 3, 2, 4).reshape(layer_count, -1, model_width)
    att = units[:, n_ffn:].reshape(layer_count, n_att, 2, block, 2, 128)
    att = att.transpose(0, 3, 2, 4, 1, 5).reshape(layer_count, block, 4, model_width)
    qkv = att[:, :, :3].reshape(layer_count, block, 3 * model_width)
    return [qkv, att[:, :, 3], up, down]


def solution(mesh):
    return jax.shard_map(
        functools.partial(on_device, mesh.shape["dp"]),
        mesh=mesh,
        in_specs=(P("dp", "seq", None), P("dp", "seq"), P("dp")) + (P(),) * 13,
        out_specs=(
            P("dp"),
            P("dp", "seq", None),
            P(None, "dp", None),
            P(),
            P(),
            P(None, "dp", None),
            P(),
            P(),
            P(),
            P(None, "dp", None),
            P(),
            P(None, "dp", None),
            P(),
            P(),
            P(),
        ),
        check_vma=False,
    )
```

```python
import functools

import jax
import jax.numpy as jnp
from jax import lax
from jax.experimental import pallas as pl
from jax.experimental.pallas import tpu as pltpu
from jax.sharding import PartitionSpec as P

HIGHEST = lax.Precision.HIGHEST
MESH = pl.DeviceIdType.MESH
LOSS_SCALE = 1024.0
NORM_EPS = 1e-06
HD = 64
WIDE = 512
C = 256
WAYS = 8
QUEUE = 18
SLOTS = 6
LAGS = (0, 1, 3, 5, 7, 9, 11)
PACE = (2, 3)
VEC_ROWS = 16
ROW_BLOCK = 64


def dot(left, right, precision=None):
    return lax.dot_general(
        left,
        right,
        (((1,), (0,)), ((), ())),
        precision=precision,
        preferred_element_type=jnp.float32,
    )


def dot_t(left, right, precision=None):
    return lax.dot_general(
        left,
        right,
        (((1,), (1,)), ((), ())),
        precision=precision,
        preferred_element_type=jnp.float32,
    )


def remote(src, dst, send_sem, recv_sem, where):
    return pltpu.make_async_remote_copy(
        src_ref=src,
        dst_ref=dst,
        send_sem=send_sem,
        recv_sem=recv_sem,
        device_id=where,
        device_id_type=MESH,
    )


def greet(peers):
    barrier = pltpu.get_barrier_semaphore()
    for peer in peers:
        pl.semaphore_signal(barrier, inc=1, device_id=peer, device_id_type=MESH)
    pl.semaphore_wait(barrier, len(peers))


def gelu_pair(x):
    t = 1.0 / (1.0 + 0.23164190 * jnp.abs(x))
    gauss = jnp.exp(-0.5 * x * x)
    poly = t * (
        0.127414796
        + t * (-0.142248368 + t * (0.7107068705 + t * (-0.7265760135 + t * 0.5307027145)))
    )
    tail = poly * gauss
    phi = jnp.where(x >= 0.0, 1.0 - tail, tail)
    return x * phi, phi + x * (gauss * 0.3989422804014327)


def norm(x, gain, shift):
    centre = x - jnp.mean(x, axis=-1, keepdims=True)
    scaled = lax.rsqrt(jnp.mean(centre * centre, axis=-1, keepdims=True) + NORM_EPS)
    normal = centre * scaled
    return normal * gain + shift, normal, scaled


def fwd_kernel(
    layers, segs,
    tok, ids, pair, b_query, b_value, b_out, gain_one, shift_one, b_up, b_down, gain_two, shift_two,
    w_qkv, w_out, w_up, w_down,
    grad_out, loss_out, o_qkv, o_p, o_pv, o_hidT, o_mixT, o_nrmT, o_actT, o_gp, o_n1, o_r1, o_n2, o_r2,
    wq, wo, wu, wd, bias, hid, low, idbuf, qkv, pb, pv, mix, nrm, gp, n1, r1, n2, r2,
    hidT, mixT, nrmT, actT, acc, ubuf, gbuf,
    wsem, psem, osem, tsem, usem,
):
    T, D = hid.shape
    FF = w_up.shape[2]
    piece = tok.shape[1]
    parts = T // piece
    me = lax.axis_index("dp")
    zi = lax.axis_index("seq")
    pairs = ((w_qkv, wq), (w_out, wo), (w_up, wu), (w_down, wd))

    def wcopy(l, i):
        return pltpu.make_async_copy(pairs[i][0].at[l], pairs[i][1].at[l], wsem.at[l, i])

    def peer(k):
        return lax.rem(zi + k, parts)

    mine = pl.ds(pl.multiple_of(zi * piece, piece), piece)

    def tcopy(k, n):
        src, dst = ((tok, low.at[mine]), (ids, idbuf.at[zi]))[n]
        if k == 0:
            return pltpu.make_async_copy(src.at[zi], dst, tsem.at[n, 0, 0])
        return remote(src.at[peer(k)], dst, tsem.at[n, 0, k], tsem.at[n, 1, k], (me, peer(k)))

    greet([(me, peer(k)) for k in range(1, parts)])
    for k in (2, 1, 3, 0):
        for n in (1, 0):
            tcopy(k, n).start()
    for l in range(layers):
        for i in range(4):
            wcopy(l, i).start()

    lane = lax.broadcasted_iota(jnp.int32, (T, 128), 1)
    first = lane < HD

    def transpose(src, dst, n):
        def body(i, c):
            o = pl.multiple_of(i * 128, 128)
            dst[pl.ds(o, 128), :] = src[:, pl.ds(o, 128)].T
            return c

        lax.fori_loop(0, n // 128, body, 0)

    def rows(fn):
        def body(i, c):
            fn(pl.ds(pl.multiple_of(i * ROW_BLOCK, ROW_BLOCK), ROW_BLOCK))
            return c

        lax.fori_loop(0, T // ROW_BLOCK, body, 0)

    outs = []

    def ship(l, src, dst, k):
        c = pltpu.make_async_copy(src, dst.at[l], osem.at[k])
        c.start()
        outs.append(c)

    for k in range(parts):
        tcopy(k, 1).wait()
    id_rows = [idbuf[k] for k in range(parts)]
    id_cols = jnp.concatenate(
        id_rows + [jnp.zeros((8 - parts, piece), jnp.int32)], axis=0
    ).astype(jnp.float32).T
    for i in range(parts):
        for j in range(parts):
            same = id_cols[:, i : i + 1] == id_rows[j].astype(jnp.float32)
            bias[i * piece : (i + 1) * piece, j * piece : (j + 1) * piece] = jnp.where(same, 0.0, -1e30)
    for k in range(parts):
        tcopy(k, 0).wait()

    for l in range(layers):
        if l == 0:
            hid[...] = low[...].astype(jnp.float32)
        else:
            low[...] = hid[...].astype(jnp.bfloat16)
        for c in outs:
            c.wait()
        outs.clear()
        wcopy(l, 0).wait()
        for k in range(3):
            cols = slice(k * D, (k + 1) * D)
            y = dot(low[...], wq[l, :, cols])
            if k == 0:
                y = (y + b_query[l : l + 1, :]) * 0.125
            if k == 2:
                y = y + b_value[l : l + 1, :]
            qkv[:, cols] = y.astype(jnp.bfloat16)
        ship(l, qkv, o_qkv, 0)
        transpose(low, hidT, D)
        ship(l, hidT, o_hidT, 1)

        def pcopy(i, s):
            return pltpu.make_async_copy(pb.at[s], o_p.at[l, pl.ds(2 * i, 2)], psem.at[s])

        def attend(i, c):
            s = lax.rem(i, 2)
            o = pl.multiple_of(i * 128, 128)
            q2, k2, v2 = (qkv[:, pl.ds(o + k * D, 128)] for k in range(3))

            @pl.when(i >= 2)
            def _():
                pcopy(i - 2, s).wait()

            zero = jnp.zeros_like(q2)
            total = None
            for h in range(2):
                sel = first if h == 0 else ~first
                sc = dot_t(jnp.where(sel, q2, zero), k2) + bias[...]
                e = jnp.exp(sc - jnp.max(sc, axis=-1, keepdims=True))
                p = (e * (1.0 / jnp.sum(e, axis=-1, keepdims=True))).astype(jnp.bfloat16)
                pb[s, h] = p
                part = dot(p, jnp.where(sel, v2, zero))
                total = part if h == 0 else total + part
            pv[:, pl.ds(o, 128)] = total
            mix[:, pl.ds(o, 128)] = total.astype(jnp.bfloat16)
            pcopy(i, s).start()
            return c

        n_pairs = D // 128
        lax.fori_loop(0, n_pairs, attend, 0)
        ship(l, pv, o_pv, 3)
        wcopy(l, 1).wait()
        acc[...] = dot(mix[...], wo[l])
        transpose(mix, mixT, D)
        ship(l, mixT, o_mixT, 4)

        def first_norm(rs):
            x = hid[rs, :] + acc[rs, :] + b_out[l : l + 1, :]
            y, n, r = norm(x, gain_one[l : l + 1, :], shift_one[l : l + 1, :])
            nrm[rs, :] = y
            low[rs, :] = y.astype(jnp.bfloat16)
            n1[rs, :] = n.astype(jnp.bfloat16)
            r1[rs, :] = jnp.broadcast_to(r, (ROW_BLOCK, 128))

        rows(first_norm)
        ship(l, n1, o_n1, 5)
        ship(l, r1, o_r1, 6)
        transpose(low, nrmT, D)
        ship(l, nrmT, o_nrmT, 7)
        wcopy(l, 2).wait()
        wcopy(l, 3).wait()
        acc[...] = nrm[...]

        def ffn(j, c):
            o = pl.multiple_of(j * WIDE, WIDE)
            pre = dot(low[...], wu[l, :, pl.ds(o, WIDE)]) + b_up[l : l + 1, pl.ds(o, WIDE)]
            a, g = gelu_pair(pre)
            al = a.astype(jnp.bfloat16)
            gp[:, pl.ds(o, WIDE)] = g.astype(jnp.bfloat16)
            acc[...] += dot(al, wd[l, pl.ds(o, WIDE), :])
            actT[pl.ds(o, WIDE), :] = al.T
            return c

        lax.fori_loop(0, FF // WIDE, ffn, 0)
        ship(l, gp, o_gp, 8)
        ship(l, actT, o_actT, 9)

        def second_norm(rs):
            x = acc[rs, :] + b_down[l : l + 1, :]
            y, n, r = norm(x, gain_two[l : l + 1, :], shift_two[l : l + 1, :])
            hid[rs, :] = y
            n2[rs, :] = n.astype(jnp.bfloat16)
            r2[rs, :] = jnp.broadcast_to(r, (ROW_BLOCK, 128))

        rows(second_norm)
        ship(l, n2, o_n2, 10)
        ship(l, r2, o_r2, 11)
        for i in (n_pairs - 2, n_pairs - 1):
            pcopy(i, i % 2).wait()

    count = parts * segs
    member_t = jnp.concatenate(
        [
            (lax.broadcasted_iota(jnp.int32, (segs, piece), 0) == row).astype(jnp.float32)
            for row in id_rows
        ],
        axis=1,
    )
    sizes = jnp.sum(member_t, axis=-1, keepdims=True)
    embed = dot(member_t, hid[...], HIGHEST) / sizes
    scale = lax.rsqrt(jnp.sum(embed * embed, axis=-1, keepdims=True) + NORM_EPS)
    unit = embed * scale
    ubuf[...] = jnp.zeros_like(ubuf)
    own = pl.ds(pl.multiple_of(zi * segs, segs), segs)
    gbuf[zi] = unit

    def ucopy(k):
        return remote(gbuf.at[zi], gbuf.at[zi], usem.at[0, k], usem.at[1, k], (me, peer(k)))

    for k in range(1, parts):
        ucopy(k).start()
    for k in range(1, parts):
        ucopy(k).wait()
    for k in range(parts):
        ubuf[k * segs : (k + 1) * segs, :] = gbuf[k]
    units = ubuf[...]
    side = units.shape[0]
    row_no = lax.broadcasted_iota(jnp.int32, (side, side), 0)
    col_no = lax.broadcasted_iota(jnp.int32, (side, side), 1)
    live = (row_no < count) & (col_no < count)
    logits = jnp.where(live, 20.0 * dot_t(units, units, HIGHEST), -1e30)
    top = jnp.max(logits, axis=-1, keepdims=True)
    grown = jnp.exp(logits - top)
    total = jnp.sum(grown, axis=-1, keepdims=True)
    chosen = jnp.where(live & (pair[...] == col_no), 1.0, 0.0)
    picked = jnp.sum(chosen * logits, axis=-1, keepdims=True)
    losses = jnp.where(row_no[:, :1] < count, top + jnp.log(total) - picked, 0.0)
    loss_out[...] = jnp.sum(losses, axis=0, keepdims=True) / count
    pull = jnp.where(live, (grown / total - chosen) * (20.0 * LOSS_SCALE / count), 0.0)
    acc[:side, :side] = pull + pull.T
    grad_unit = dot(acc[own, :side], units, HIGHEST)
    inner = jnp.sum(grad_unit * unit, axis=-1, keepdims=True)
    grad_sums = scale * (grad_unit - unit * inner) / sizes
    for i in range(parts):
        member = (
            lax.broadcasted_iota(jnp.int32, (piece, segs), 1).astype(jnp.float32) == id_cols[:, i : i + 1]
        ).astype(jnp.float32)
        grad_out[i * piece : (i + 1) * piece, :] = dot(member, grad_sums, HIGHEST)
    for c in outs:
        c.wait()


def forward(tokens, segment_ids, pair_ids, w):
    parts, piece, D = tokens.shape
    T = parts * piece
    L = w["w_qkv"].shape[0]
    FF = w["w_up"].shape[2]
    segs = pair_ids.shape[0] // parts
    side = 128
    bf, f32 = jnp.bfloat16, jnp.float32
    S = jax.ShapeDtypeStruct
    V = pltpu.VMEM
    vm = pl.BlockSpec(memory_space=V)
    anyspec = pl.BlockSpec(memory_space=pl.ANY)
    H = D // HD
    dma = pltpu.SemaphoreType.DMA
    out_shape = (
        S((T, D), f32), S((1, 1), f32), S((L, T, 3 * D), bf), S((L, H, T, T), bf), S((L, T, D), f32),
        S((L, D, T), bf), S((L, D, T), bf), S((L, D, T), bf), S((L, FF, T), bf), S((L, T, FF), bf),
        S((L, T, D), bf), S((L, T, 128), f32), S((L, T, D), bf), S((L, T, 128), f32),
    )
    scratch = [
        V((L, D, 3 * D), bf), V((L, D, D), bf), V((L, D, FF), bf), V((L, FF, D), bf),
        V((T, T), f32), V((T, D), f32), V((T, D), bf), V((parts, 1, piece), jnp.int32),
        V((T, 3 * D), bf), V((2, 2, T, T), bf), V((T, D), f32), V((T, D), bf), V((T, D), f32), V((T, FF), bf),
        V((T, D), bf), V((T, 128), f32), V((T, D), bf), V((T, 128), f32),
        V((D, T), bf), V((D, T), bf), V((D, T), bf), V((FF, T), bf), V((T, D), f32),
        V((side, D), f32), V((parts, segs, D), f32),
        dma((L, 4)), dma((2,)), dma((12,)), dma((2, 2, parts)), dma((2, parts)),
    ]
    pair_column = jnp.pad(pair_ids, (0, side - pair_ids.shape[0])).reshape(side, 1)
    return pl.pallas_call(
        functools.partial(fwd_kernel, L, segs),
        out_shape=out_shape,
        in_specs=[anyspec] * 2 + [vm] * 10 + [anyspec] * 4,
        out_specs=(vm, vm) + (anyspec,) * 12,
        scratch_shapes=scratch,
        compiler_params=pltpu.CompilerParams(
            vmem_limit_bytes=60 * 1024 * 1024, collective_id=1, has_side_effects=True
        ),
        name="forward",
    )(
        tokens, segment_ids.reshape(parts, 1, piece), pair_column,
        *(w[k] for k in ("b_query", "b_value", "b_out", "gain_one", "shift_one", "b_up", "b_down", "gain_two", "shift_two")),
        *(w[k] for k in ("w_qkv", "w_out", "w_up", "w_down")),
    )


def low_sum(one, other):
    return (one.astype(jnp.float32) + other.astype(jnp.float32)).astype(jnp.bfloat16)


def bwd_kernel(
    layers, g_in, gain_one, gain_two,
    w_qkv, w_out, w_up, w_down,
    h_qkv, h_p, h_pv, h_hidT, h_mixT, h_nrmT, h_actT, h_gp, h_n1, h_r1, h_n2, h_r2,
    out, gt_out, vec_out,
    wd, wu, gp, actT, wq, qkv, pb, pv, wo, hidT, mixT, nrmT, n1, r1, n2, r2,
    acc, second, branch, gm, gpre, rhs, vec, vrecv, gb,
    sendc, keepq, recvq, s1, k1, t1, s2, k2, t2, za, zr, zb, zt, zf,
    fsem, asem, lsem, csem, xsem, ysem, zsem, osem, vsem, gsem,
):
    T, D = g_in.shape
    FF = w_up.shape[2]
    R = D // WAYS
    U = 4 * R
    n_ffn = FF // D
    n_att = D // 128
    group = D // C
    macros = n_ffn + n_att
    per = n_ffn * group + n_att
    n_units = layers * per
    n_macros = layers * macros

    me = lax.axis_index("dp")
    zi = lax.axis_index("seq")
    oc = lax.rem(me, 2)
    ox = lax.rem(lax.div(me, 2), 2)
    oy = lax.rem(lax.div(me, 4), 2)
    core = (me + 1 - 2 * oc, zi)
    xdev = (me + 2 - 4 * ox, zi)
    ydev = (me + 4 - 8 * oy, zi)
    inner = (zi == 1) | (zi == 2)
    outer = (zi == 0) | (zi == 3)
    to_inner = (me, 1 + lax.div(zi, 2))
    across = (me, 3 - zi)
    to_outer = (me, 3 * lax.div(zi, 2))

    def place(n):
        y = lax.rem(oy + n // 2 % 2, 2)
        x = lax.rem(ox + n % 2, 2)
        return 4 * y + 2 * x + lax.rem(oc + n // 4, 2)

    def turned(src, dst, l):
        return [(src.at[l, place(n)], dst.at[pl.ds(n * R, R)]) for n in range(WAYS)]

    def copies(parts, sem):
        return [pltpu.make_async_copy(a, b, sem.at[k]) for k, (a, b) in enumerate(parts)]

    def ffn_tile(f):
        l = layers - 1 - lax.div(f, n_ffn)
        rb = lax.rem(f, n_ffn)
        s = lax.rem(f, 2)
        span = pl.ds(pl.multiple_of(rb * D, D), D)
        parts = [(w_down.at[l, span], wd.at[s]), (w_up.at[l, :, span], wu.at[s]), (h_gp.at[l, :, span], gp.at[s])]
        parts += [(h_actT.at[l, place(n), rb], actT.at[s, pl.ds(n * R, R)]) for n in range(WAYS)]
        return copies(parts, fsem.at[s])

    def att_tile(a):
        l = layers - 1 - lax.div(a, n_att)
        i = lax.rem(a, n_att)
        s = lax.rem(a, 2)
        parts = [(h_p.at[l, pl.ds(2 * i, 2)], pb.at[s])]
        for k in range(3):
            span = pl.ds(pl.multiple_of(i * 128 + k * D, 128), 128)
            parts.append((w_qkv.at[l, :, span], wq.at[s, :, pl.ds(k * 128, 128)]))
            parts.append((h_qkv.at[l, :, span], qkv.at[s, :, pl.ds(k * 128, 128)]))
        parts.append((h_pv.at[l, :, pl.ds(pl.multiple_of(i * 128, 128), 128)], pv.at[s]))
        return copies(parts, asem.at[s])

    def ffn_layer(l):
        return copies([(h_n2.at[l], n2), (h_r2.at[l], r2)] + turned(h_nrmT, nrmT, l), lsem.at[0])

    def att_layer(l):
        parts = [(h_n1.at[l], n1), (h_r1.at[l], r1), (w_out.at[l], wo)]
        return copies(parts + turned(h_hidT, hidT, l) + turned(h_mixT, mixT, l), lsem.at[1])

    def start(made):
        for c in made:
            c.start()

    def wait(made):
        for c in made:
            c.wait()

    start(ffn_layer(layers - 1))
    for n in range(2):
        start(ffn_tile(jnp.int32(n)))
    start(att_layer(layers - 1))
    for n in range(2):
        start(att_tile(jnp.int32(n)))
    acc[...] = g_in[...]
    vec[...] = jnp.zeros_like(vec)
    greet([core, xdev, ydev] + [(me, lax.rem(zi + k, 4)) for k in range(1, 4)])

    lane = lax.broadcasted_iota(jnp.int32, (T, 128), 1)
    first = lane < HD

    def rows(fn):
        def body(i, sums):
            rs = pl.ds(pl.multiple_of(i * ROW_BLOCK, ROW_BLOCK), ROW_BLOCK)
            return tuple(a + b for a, b in zip(sums, fn(rs)))

        zero = jnp.zeros((1, D), jnp.float32)
        return lax.fori_loop(0, T // ROW_BLOCK, body, (zero, zero, zero))

    def norm_back(g, n, r, gain):
        e = g * gain
        return r * (e - jnp.mean(e, axis=-1, keepdims=True) - n * jnp.mean(e * n, axis=-1, keepdims=True))

    def col_sum(v):
        return jnp.sum(v.astype(jnp.float32), axis=0, keepdims=True)

    def through_norm(normal, root, gain, rounded):
        def fn(rs):
            g = acc[rs, :]
            n = normal[rs, :].astype(jnp.float32)
            d = norm_back(g, n, root[rs, :1], gain)
            acc[rs, :] = d
            low = d.astype(jnp.bfloat16)
            rounded[rs, :] = low
            return col_sum(low), col_sum(g * n), col_sum(g)

        return rows(fn)

    def prologue(l):
        wait(ffn_layer(l))
        sums = through_norm(n2, r2, gain_two[l], second)
        for k in range(3):
            vec[l, 5 + n_ffn + k : 6 + n_ffn + k, :] = sums[k]

    def middle(l):
        wait(att_layer(l))
        sums = through_norm(n1, r1, gain_one[l], branch)
        for k in range(3):
            vec[l, 2 + k : 3 + k, :] = sums[k]
        gm[...] = dot_t(branch[...], wo[...]).astype(jnp.bfloat16)

    def ffn(l, rb, c):
        f = (layers - 1 - l) * n_ffn + rb
        s = lax.rem(f, 2)
        q = rb * group
        wait(ffn_tile(f))
        low = (dot_t(second[...], wd[s]) * gp[s].astype(jnp.float32)).astype(jnp.bfloat16)
        gpre[...] = low
        vec[l, pl.ds(5 + rb, 1), :] = col_sum(low)
        for k, (left, right) in enumerate(((nrmT, gpre), (actT.at[s], second))):
            made = dot(left[...], right[...]).astype(jnp.bfloat16)
            for n in range(group):
                keepq[q + n, k] = made[:U, n * C : (n + 1) * C]
                sendc[c, n, k] = made[U:, n * C : (n + 1) * C]
        acc[...] += dot_t(gpre[...], wu[s])

        @pl.when(f + 2 < layers * n_ffn)
        def _():
            start(ffn_tile(f + 2))

    def attend(l, i, c):
        a = (layers - 1 - l) * n_att + i
        o = pl.multiple_of(i * 128, 128)
        s = lax.rem(a, 2)
        q = n_ffn * group + i
        wait(att_tile(a))
        q2, k2, v2 = (qkv[s, :, k * 128 : (k + 1) * 128] for k in range(3))
        g2 = gm[:, pl.ds(o, 128)]
        weighed = g2.astype(jnp.float32) * pv[s]
        zero = jnp.zeros_like(q2)
        q2t, g2t = q2.T, g2.T
        dq = None
        dkt, dvt = [], []
        for h in range(2):
            sel = first if h == 0 else ~first
            p = pb[s, h]
            gprob = dot_t(jnp.where(sel, g2, zero), v2)
            centre = jnp.sum(jnp.where(sel, weighed, 0.0), axis=-1, keepdims=True)
            ds = (p.astype(jnp.float32) * (gprob - centre)).astype(jnp.bfloat16)
            part = dot(ds, jnp.where(sel, k2, zero))
            dq = part if h == 0 else dq + part
            dkt.append(dot(q2t[h * HD : (h + 1) * HD], ds))
            dvt.append(dot(g2t[h * HD : (h + 1) * HD], p))
        dq = (dq * 0.125).astype(jnp.bfloat16)
        dk = jnp.concatenate(dkt, axis=0).astype(jnp.bfloat16).T
        dv = jnp.concatenate(dvt, axis=0).astype(jnp.bfloat16).T
        vec[l, 0:1, pl.ds(o, 128)] = col_sum(dq)
        vec[l, 1:2, pl.ds(o, 128)] = col_sum(dv)
        rhs[:, :128] = dq
        rhs[:, 128:256] = dk
        rhs[:, 256:] = dv
        made = dot(hidT[...], rhs[...]).astype(jnp.bfloat16)
        keepq[q, 0] = made[:U, :C]
        sendc[c, 0, 0] = made[U:, :C]
        keepq[q, 1, :, :128] = made[:U, C:]
        sendc[c, 0, 1, :, :128] = made[U:, C:]
        made = dot(mixT[...], branch[:, pl.ds(o, 128)]).astype(jnp.bfloat16)
        keepq[q, 1, :, 128:] = made[:U]
        sendc[c, 0, 1, :, 128:] = made[U:]
        acc[...] += dot_t(rhs[...], wq[s])

        @pl.when(a + 2 < layers * n_att)
        def _():
            start(att_tile(a + 2))

    def core_copy(m, wide):
        c = lax.rem(m, 2)
        k = lax.rem(m, macros)
        q = k * group if wide else n_ffn * group + k - n_ffn
        size = group if wide else 1
        return remote(
            sendc.at[c, pl.ds(0, size)], recvq.at[pl.ds(q, size)], csem.at[0, m], csem.at[1, m], core
        )

    def is_wide(m):
        return lax.rem(m, macros) < n_ffn

    def copies_one(u):
        s = lax.rem(u, SLOTS)
        return [
            remote(s1.at[s, k], t1.at[s, k], xsem.at[0, k, s], xsem.at[1, k, s], (xdev, ydev)[k]) for k in range(2)
        ]

    def copies_two(u):
        s = lax.rem(u, SLOTS)
        return [
            remote(s2.at[s, k], t2.at[s, k], ysem.at[0, k, s], ysem.at[1, k, s], (ydev, xdev)[k]) for k in range(2)
        ]

    def copy_in(u):
        s = lax.rem(u, SLOTS)
        return remote(za.at[s], zr.at[s], zsem.at[0, s], zsem.at[1, s], to_inner)

    def copy_across(u):
        s = lax.rem(u, SLOTS)
        return remote(zb.at[s], zt.at[s], zsem.at[2, s], zsem.at[3, s], across)

    def copy_out(u):
        s = lax.rem(u, SLOTS)
        return remote(zf.at[s], out.at[u], zsem.at[4, s], zsem.at[5, s], to_outer)

    def copy_home(u):
        s = lax.rem(u, SLOTS)
        return pltpu.make_async_copy(zf.at[s], out.at[u], osem.at[s])

    def stage_one(u):
        s = lax.rem(u, QUEUE)
        d = lax.rem(u, SLOTS)
        base = lax.div(u, per) * macros

        @pl.when((s < n_ffn * group) & (lax.rem(s, group) == 0))
        def _():
            core_copy(base + lax.div(s, group), True).wait_recv()

        @pl.when(s >= n_ffn * group)
        def _():
            core_copy(base + n_ffn + s - n_ffn * group, False).wait_recv()

        for k in range(2):
            sent, kept = ((1, 3), (0, 2)) if k == 0 else ((2, 3), (0, 1))
            for n, (a, b) in enumerate(zip(sent, kept)):
                to = pl.ds(n * R, R)
                s1[d, k, to] = low_sum(keepq[s, k, pl.ds(a * R, R)], recvq[s, k, pl.ds(a * R, R)])
                k1[d, k, to] = low_sum(keepq[s, k, pl.ds(b * R, R)], recvq[s, k, pl.ds(b * R, R)])
        start(copies_one(u))

    def stage_two(u):
        d = lax.rem(u, SLOTS)
        wait(copies_one(u))
        for k in range(2):
            s2[d, k] = low_sum(k1[d, k, pl.ds(R, R)], t1[d, k, pl.ds(R, R)])
            k2[d, k] = low_sum(k1[d, k, pl.ds(0, R)], t1[d, k, pl.ds(0, R)])
        start(copies_two(u))

    def stage_three(u):
        d = lax.rem(u, SLOTS)
        wait(copies_two(u))
        za[d] = low_sum(k2[d], t2[d])

        @pl.when(outer)
        def _():
            copy_in(u).start()

    def stage_four(u):
        d = lax.rem(u, SLOTS)

        @pl.when(outer)
        def _():
            copy_in(u).wait_send()

        @pl.when(inner)
        def _():
            copy_in(u).wait_recv()
            zb[d] = low_sum(za[d], zr[d])
            copy_across(u).start()

    def stage_five(u):
        d = lax.rem(u, SLOTS)

        @pl.when(inner)
        def _():
            copy_across(u).wait()
            zf[d] = low_sum(zb[d], zt[d])
            copy_out(u).start()
            copy_home(u).start()

    def stage_six(u):
        @pl.when(inner)
        def _():
            copy_out(u).wait_send()
            copy_home(u).wait()

        @pl.when(outer)
        def _():
            copy_out(u).wait_recv()

    stages = (None, stage_one, stage_two, stage_three, stage_four, stage_five, stage_six)

    def run_stage(i, k):
        u = i - LAGS[k]

        @pl.when((u >= 0) & (u < n_units))
        def _():
            stages[k](u)

    def vec_copy(k):
        where = (core, xdev, ydev, to_inner, across, to_outer)[k]
        return remote(vec, vrecv.at[k], vsem.at[0, k], vsem.at[1, k], where)

    def vec_step(k):
        if 1 <= k <= 3:
            vec_copy(k - 1).wait()
            vec[...] += vrecv[k - 1]
        if k < 3:
            vec_copy(k).start()
        if k == 3:

            @pl.when(outer)
            def _():
                vec_copy(3).start()

        if k == 4:

            @pl.when(outer)
            def _():
                vec_copy(3).wait_send()

            @pl.when(inner)
            def _():
                vec_copy(3).wait_recv()
                vec[...] += vrecv[3]
                vec_copy(4).start()

        if k == 5:

            @pl.when(inner)
            def _():
                vec_copy(4).wait()
                vec[...] += vrecv[4]
                vec_copy(5).start()

        if k == 6:

            @pl.when(inner)
            def _():
                vec_copy(5).wait_send()
                vec_out[...] = vec[...]

            @pl.when(outer)
            def _():
                vec_copy(5).wait_recv()
                vec_out[...] = vrecv[5]

    part = T // 4

    def gt_copy(k):
        peer = lax.rem(zi + k, 4)
        src = gb.at[pl.ds(pl.multiple_of(peer * part, part), part)]
        if k == 0:
            return pltpu.make_async_copy(src, gt_out.at[zi], gsem.at[0, 0])
        return remote(src, gt_out.at[zi], gsem.at[0, k], gsem.at[1, k], (me, peer))

    def done_by(i):
        num, den = PACE
        return jnp.minimum(lax.div(num * (i + 1) + den - 1, den), n_macros)

    last = 0
    while -(-PACE[0] * (last + 1) // PACE[1]) < n_macros:
        last += 1

    def step(i, carry):
        for k in range(6, 1, -1):
            run_stage(i, k)
        run_stage(i, 1)
        m = done_by(i - 1)
        l = layers - 1 - lax.div(m, macros)
        k = lax.rem(m, macros)
        c = lax.rem(m, 2)
        busy = done_by(i) > m

        @pl.when(busy & (m >= 2) & is_wide(m - 2))
        def _():
            core_copy(m - 2, True).wait_send()

        @pl.when(busy & (m >= 2) & ~is_wide(m - 2))
        def _():
            core_copy(m - 2, False).wait_send()

        @pl.when(busy & (k == 0))
        def _():
            prologue(l)

        @pl.when(busy & (k == 0) & (l < layers - 1))
        def _():
            start(att_layer(l))

        @pl.when(busy & (k < n_ffn))
        def _():
            ffn(l, k, c)
            core_copy(m, True).start()

        @pl.when(busy & (k == n_ffn) & (l > 0))
        def _():
            start(ffn_layer(l - 1))

        @pl.when(busy & (k == n_ffn))
        def _():
            middle(l)

        @pl.when(busy & (k >= n_ffn))
        def _():
            attend(l, k - n_ffn, c)
            core_copy(m, False).start()

        @pl.when(i == last + 1)
        def _():
            gb[...] = acc[...].astype(jnp.bfloat16)
            for n in range(4):
                gt_copy(n).start()

        for n in range(7):

            @pl.when(i == last + 1 + 2 * n)
            def _(n=n):
                vec_step(n)

        return carry

    lax.fori_loop(0, n_units + LAGS[6], step, 0)
    for m in (n_macros - 2, n_macros - 1):
        core_copy(jnp.int32(m), False).wait_send()
    for n in range(4):
        gt_copy(n).wait()


def backward(grad_hidden, res, w):
    T, D = grad_hidden.shape
    L = w["w_qkv"].shape[0]
    FF = w["w_up"].shape[2]
    bf, f32 = jnp.bfloat16, jnp.float32
    S = jax.ShapeDtypeStruct
    V = pltpu.VMEM
    vm = pl.BlockSpec(memory_space=V)
    anyspec = pl.BlockSpec(memory_space=pl.ANY)
    R = D // WAYS
    U = 4 * R
    group = D // C
    n_units = L * (FF // C + D // 128)
    n_macros = L * (FF // D + D // 128)
    dma = pltpu.SemaphoreType.DMA
    scratch = [
        V((2, D, D), bf), V((2, D, D), bf), V((2, T, D), bf), V((2, D, T), bf),
        V((2, D, 384), bf), V((2, T, 384), bf), V((2, 2, T, T), bf), V((2, T, 128), f32),
        V((D, D), bf), V((D, T), bf), V((D, T), bf), V((D, T), bf),
        V((T, D), bf), V((T, 128), f32), V((T, D), bf), V((T, 128), f32),
        V((T, D), f32), V((T, D), bf), V((T, D), bf), V((T, D), bf), V((T, D), bf), V((T, 384), bf),
        V((L, VEC_ROWS, D), f32), V((6, L, VEC_ROWS, D), f32), V((T, D), bf),
        V((2, group, 2, U, C), bf), V((QUEUE, 2, U, C), bf), V((QUEUE, 2, U, C), bf),
        V((SLOTS, 2, 2 * R, C), bf), V((SLOTS, 2, 2 * R, C), bf), V((SLOTS, 2, 2 * R, C), bf),
        V((SLOTS, 2, R, C), bf), V((SLOTS, 2, R, C), bf), V((SLOTS, 2, R, C), bf),
        V((SLOTS, 2, R, C), bf), V((SLOTS, 2, R, C), bf), V((SLOTS, 2, R, C), bf),
        V((SLOTS, 2, R, C), bf), V((SLOTS, 2, R, C), bf),
        dma((2, 3 + WAYS)), dma((2, 8)), dma((2, 3 + 2 * WAYS)), dma((2, n_macros)), dma((2, 2, SLOTS)), dma((2, 2, SLOTS)),
        dma((6, SLOTS)), dma((SLOTS,)), dma((2, 6)), dma((2, 4)),
    ]
    return pl.pallas_call(
        functools.partial(bwd_kernel, L),
        out_shape=(
            S((n_units, 2, R, C), bf), S((4, T // 4, D), bf), S((L, VEC_ROWS, D), f32),
        ),
        in_specs=[vm] * 3 + [anyspec] * 16,
        out_specs=(anyspec, anyspec, vm),
        scratch_shapes=scratch,
        compiler_params=pltpu.CompilerParams(
            vmem_limit_bytes=60 * 1024 * 1024, collective_id=0, has_side_effects=True
        ),
        name="backward",
    )(
        grad_hidden, w["gain_one"].reshape(L, 1, D), w["gain_two"].reshape(L, 1, D),
        *(w[k] for k in ("w_qkv", "w_out", "w_up", "w_down")),
        *res,
    )


def finish_kernel(units, gt, vec, g_tok, g_qkv, g_out, g_up, g_down, *vectors):
    l = pl.program_id(0)
    R, D = g_out.shape[1:]
    n_ffn = g_up.shape[2] // D
    group = D // C
    g_tok[...] = gt[...].astype(jnp.float32)

    def read(n, k, cols=slice(None)):
        return units[0, n, k, :, cols].astype(jnp.float32)

    for rb in range(n_ffn):
        for n in range(group):
            u = rb * group + n
            g_up[0, :, u * C : (u + 1) * C] = read(u, 0)
            g_down[0, rb * R : (rb + 1) * R, n * C : (n + 1) * C] = read(u, 1)
    for i in range(D // 128):
        u = n_ffn * group + i
        for k in range(3):
            half = slice(k % 2 * 128, k % 2 * 128 + 128)
            g_qkv[0, :, k * D + i * 128 : k * D + (i + 1) * 128] = read(u, k // 2, half)
        g_out[0, :, i * 128 : (i + 1) * 128] = read(u, 1, slice(128, 256))
    row = 0
    for ref in vectors:
        for k in range(ref.shape[1] // D):
            ref[pl.ds(l, 1), k * D : (k + 1) * D] = vec[0, row : row + 1, :]
            row += 1


def finish(units, grad_tokens, vec, layers, hidden_units):
    n_units, _, R, _ = units.shape
    parts, piece, D = grad_tokens.shape
    L, FF = layers, hidden_units
    f32 = jnp.float32
    S = jax.ShapeDtypeStruct
    per = n_units // L
    widths = (D, D, D, D, D, FF, D, D, D)
    return pl.pallas_call(
        finish_kernel,
        grid=(L,),
        out_shape=(
            S((parts, piece, D), f32), S((L, R, 3 * D), f32), S((L, R, D), f32), S((L, R, FF), f32),
            S((L, FF // WAYS, D), f32),
        ) + tuple(S((L, width), f32) for width in widths),
        in_specs=[
            pl.BlockSpec((1, per, 2, R, C), lambda l: (L - 1 - l, 0, 0, 0, 0)),
            pl.BlockSpec((parts // L, piece, D), lambda l: (l, 0, 0)),
            pl.BlockSpec((1, VEC_ROWS, D), lambda l: (l, 0, 0)),
        ],
        out_specs=(
            pl.BlockSpec((parts // L, piece, D), lambda l: (l, 0, 0)),
            pl.BlockSpec((1, R, 3 * D), lambda l: (l, 0, 0)),
            pl.BlockSpec((1, R, D), lambda l: (l, 0, 0)),
            pl.BlockSpec((1, R, FF), lambda l: (l, 0, 0)),
            pl.BlockSpec((1, FF // WAYS, D), lambda l: (l, 0, 0)),
        ) + tuple(pl.BlockSpec((L, width), lambda l: (0, 0)) for width in widths),
        compiler_params=pltpu.CompilerParams(vmem_limit_bytes=48 * 1024 * 1024),
        name="finish",
    )(units.reshape(L, per, 2, R, C), grad_tokens, vec)


NAMES = (
    "w_qkv",
    "b_query",
    "b_value",
    "w_out",
    "b_out",
    "gain_one",
    "shift_one",
    "w_up",
    "b_up",
    "w_down",
    "b_down",
    "gain_two",
    "shift_two",
)


def by_class(array, block, ways):
    layers, rows, tokens_here = array.shape
    if ways == 1:
        return array.reshape(layers, WAYS, -1, tokens_here)
    array = array.reshape(layers, ways, WAYS, block, tokens_here)
    return jnp.swapaxes(array, 1, 2).reshape(layers, WAYS, -1, tokens_here)


def on_device(dp_count, tokens, segment_ids, pair_ids, *weights):
    w = dict(zip(NAMES, weights))
    layer_count, model_width, _ = w["w_qkv"].shape
    hidden_units = w["w_up"].shape[2]
    ways = dp_count // WAYS
    grad_hidden, loss_value, *res = forward(tokens, segment_ids, pair_ids, w)
    for place in (3, 4, 5):
        res[place] = by_class(res[place], model_width // dp_count, ways)
    block = model_width // WAYS
    acts = by_class(res[6], hidden_units // dp_count, ways)
    res[6] = acts.reshape(layer_count, WAYS, -1, block, acts.shape[-1])
    units, grad_tokens, vec = backward(grad_hidden, res, w)
    if ways > 1:
        groups = [[low + WAYS * high for high in range(ways)] for low in range(WAYS)]
        vec = lax.psum(vec, "dp", axis_index_groups=groups)
    grad_tokens, *rest = finish(units, grad_tokens, vec, layer_count, hidden_units)
    matrices, vectors = rest[:4], rest[4:]
    if ways > 1:
        matrices = [
            lax.psum_scatter(
                matrix, "dp", scatter_dimension=1, axis_index_groups=groups, tiled=True
            )
            for matrix in matrices
        ]
    g_qkv, g_out, g_up, g_down = matrices
    return (
        loss_value.reshape(1),
        grad_tokens,
        g_qkv,
        vectors[0],
        vectors[1],
        g_out,
        vectors[2],
        vectors[3],
        vectors[4],
        g_up,
        vectors[5],
        g_down,
        vectors[6],
        vectors[7],
        vectors[8],
    )


def solution(mesh):
    return jax.shard_map(
        functools.partial(on_device, mesh.shape["dp"]),
        mesh=mesh,
        in_specs=(P("dp", "seq", None), P("dp", "seq"), P("dp")) + (P(),) * 13,
        out_specs=(
            P("dp"),
            P("dp", "seq", None),
            P(None, "dp", None),
            P(),
            P(),
            P(None, "dp", None),
            P(),
            P(),
            P(),
            P(None, "dp", None),
            P(),
            P(None, "dp", None),
            P(),
            P(),
            P(),
        ),
        check_vma=False,
    )
```

```python
import functools

import jax
import jax.numpy as jnp
from jax import lax
from jax.experimental import pallas as pl
from jax.experimental.pallas import tpu as pltpu
from jax.sharding import PartitionSpec as P

MESH = pl.DeviceIdType.MESH
LOSS_SCALE = 1024.0
NORM_EPS = 1e-06
HD = 64
WIDE = 768
C = 256
WAYS = 8
QUEUE = 18
SLOTS = 6
LAGS = (0, 1, 3, 5, 7, 9, 11)
PACE = (5, 6)
GT_PARTS = 4
VEC_ROWS = 16


def dot(left, right):
    return lax.dot_general(
        left,
        right,
        (((1,), (0,)), ((), ())),
        preferred_element_type=jnp.float32,
    )


def dot_t(left, right):
    return lax.dot_general(
        left,
        right,
        (((1,), (1,)), ((), ())),
        preferred_element_type=jnp.float32,
    )


def split(values):
    high = values.astype(jnp.bfloat16)
    return high, (values - high.astype(jnp.float32)).astype(jnp.bfloat16)


def remote(src, dst, send_sem, recv_sem, where):
    return pltpu.make_async_remote_copy(
        src_ref=src,
        dst_ref=dst,
        send_sem=send_sem,
        recv_sem=recv_sem,
        device_id=where,
        device_id_type=MESH,
    )


def greet(peers):
    barrier = pltpu.get_barrier_semaphore()
    for peer in peers:
        pl.semaphore_signal(barrier, inc=1, device_id=peer, device_id_type=MESH)
    pl.semaphore_wait(barrier, len(peers))


def gelu_pair(x):
    t = 1.0 / (1.0 + 0.23164190 * jnp.abs(x))
    gauss = jnp.exp(-0.5 * x * x)
    poly = t * (
        0.127414796
        + t * (-0.142248368 + t * (0.7107068705 + t * (-0.7265760135 + t * 0.5307027145)))
    )
    tail = poly * gauss
    phi = jnp.where(x >= 0.0, 1.0 - tail, tail)
    return x * phi, phi + x * (gauss * 0.3989422804014327)


def norm(x, gain, shift):
    centre = x - jnp.mean(x, axis=-1, keepdims=True)
    scaled = lax.rsqrt(jnp.mean(centre * centre, axis=-1, keepdims=True) + NORM_EPS)
    normal = centre * scaled
    return normal * gain + shift, normal, scaled


def fwd_kernel(
    layers, segs,
    tok, ids, pair, b_query, b_value, b_out, gain_one, shift_one, b_up, b_down, gain_two, shift_two,
    w_qkv, w_out, w_up, w_down,
    grad_out, loss_out, o_qkv, o_p, o_rl, o_pv, o_hidT, o_mixT, o_nrmT, o_actT, o_gp, o_n1, o_r1, o_n2, o_r2,
    wq, wo, wu, wd, bias, hid, low, idbuf, qkv, pb, rl, pv, mix, nrm, gp, n1, r1, n2, r2,
    hidT, mixT, nrmT, actT, acc, ubuf, gbuf, prow,
    wsem, osem, tsem, usem,
):
    T, D = hid.shape
    FF = w_up.shape[2]
    piece = tok.shape[1]
    parts = T // piece
    me = lax.axis_index("dp")
    zi = lax.axis_index("seq")
    pairs = ((w_qkv, wq), (w_out, wo), (w_up, wu), (w_down, wd))

    def wcopy(l, i):
        return pltpu.make_async_copy(pairs[i][0].at[l], pairs[i][1], wsem.at[i])

    def peer(k):
        return lax.rem(zi + k, parts)

    mine = pl.ds(pl.multiple_of(zi * piece, piece), piece)

    def tcopy(k, n):
        src, dst = ((tok, low.at[mine]), (ids, idbuf.at[zi]))[n]
        if k == 0:
            return pltpu.make_async_copy(src.at[zi], dst, tsem.at[n, 0, 0])
        return remote(src.at[peer(k)], dst, tsem.at[n, 0, k], tsem.at[n, 1, k], (me, peer(k)))

    greet([(me, peer(k)) for k in range(1, parts)])
    for k in (2, 1, 3, 0):
        for n in (1, 0):
            tcopy(k, n).start()
    for i in range(4):
        wcopy(0, i).start()

    def refill(l, *which):
        for i in which:
            if l + 1 < layers:
                wcopy(l + 1, i).start()

    lane = lax.broadcasted_iota(jnp.int32, (T, 128), 1)
    first = lane < HD

    outs = {}

    def claim(*keys):
        for key in keys:
            if key in outs:
                outs.pop(key).wait()

    def ship(l, src, dst, k):
        outs[k] = pltpu.make_async_copy(src, dst.at[l], osem.at[k])
        outs[k].start()

    for k in range(parts):
        tcopy(k, 1).wait()
    id_rows = [idbuf[k] for k in range(parts)]
    id_cols = jnp.concatenate(
        id_rows + [jnp.zeros((8 - parts, piece), jnp.int32)], axis=0
    ).astype(jnp.float32).T
    for i in range(parts):
        for j in range(parts):
            same = id_cols[:, i : i + 1] == id_rows[j].astype(jnp.float32)
            bias[i * piece : (i + 1) * piece, j * piece : (j + 1) * piece] = jnp.where(same, 0.0, -1e30)
    for k in (0, 1, 3, 2):
        tcopy(k, 0).wait()
        source = pl.ds(pl.multiple_of(lax.rem(zi + parts - k, parts) * piece, piece), piece)
        arrived = low[source, :]
        hid[source, :] = arrived.astype(jnp.float32)
        hidT[:, source] = arrived.T

    for l in range(layers):
        wcopy(l, 0).wait()
        y = dot(low[...], wq[...])
        refill(l, 0)
        claim(0)
        qkv[:, :D] = ((y[:, :D] + b_query[l : l + 1, :]) * 0.125).astype(jnp.bfloat16)
        qkv[:, D : 2 * D] = y[:, D : 2 * D].astype(jnp.bfloat16)
        qkv[:, 2 * D :] = (y[:, 2 * D :] + b_value[l : l + 1, :]).astype(jnp.bfloat16)
        ship(l, qkv, o_qkv, 0)
        ship(l, hidT, o_hidT, 1)

        def scores(n):
            o = n // 2 * 128
            q2 = qkv[:, o : o + 128]
            sel = first if n % 2 == 0 else ~first
            return dot_t(jnp.where(sel, q2, jnp.zeros_like(q2)), qkv[:, D + o : D + o + 128]) + bias[...]

        claim(2, 3, 4, 12)
        made = {0: scores(0)}
        for n in range(D // HD):
            if n + 1 < D // HD:
                made[n + 1] = scores(n + 1)
            cols = slice(n // 2 * 128, n // 2 * 128 + 128)
            v2 = qkv[:, 2 * D + cols.start : 2 * D + cols.stop]
            sel = first if n % 2 == 0 else ~first
            sc = made.pop(n)
            e = jnp.exp(sc - jnp.max(sc, axis=-1, keepdims=True))
            recip = 1.0 / jnp.sum(e, axis=-1, keepdims=True)
            p = e.astype(jnp.bfloat16)
            pb[n] = p
            part = dot(p, jnp.where(sel, v2, jnp.zeros_like(v2))) * recip
            if n % 2 == 0:
                total, before = part, recip
                continue
            total = total + part
            rl[:, cols] = jnp.where(first, before, recip)
            pv[:, cols] = total
            low_total = total.astype(jnp.bfloat16)
            mix[:, cols] = low_total
            mixT[cols, :] = low_total.T
        ship(l, pb, o_p, 12)
        ship(l, rl, o_rl, 2)
        ship(l, pv, o_pv, 3)
        wcopy(l, 1).wait()
        acc[...] = dot(mix[...], wo[...])
        refill(l, 1)
        ship(l, mixT, o_mixT, 4)

        claim(5, 6, 7)
        x = hid[...] + acc[...] + b_out[l : l + 1, :]
        y, n, r = norm(x, gain_one[l : l + 1, :], shift_one[l : l + 1, :])
        nrm[...] = y
        rounded = y.astype(jnp.bfloat16)
        low[...] = rounded
        nrmT[...] = rounded.T
        n1[...] = n.astype(jnp.bfloat16)
        r1[...] = jnp.broadcast_to(r, (T, 128))
        ship(l, n1, o_n1, 5)
        ship(l, r1, o_r1, 6)
        ship(l, nrmT, o_nrmT, 7)
        wcopy(l, 2).wait()
        wcopy(l, 3).wait()
        acc[...] = nrm[...]
        claim(8, 9)

        def raised(j):
            cols = slice(j * WIDE, (j + 1) * WIDE)
            return dot(low[...], wu[:, cols]) + b_up[l : l + 1, cols]

        made = {0: raised(0)}
        for j in range(FF // WIDE):
            cols = slice(j * WIDE, (j + 1) * WIDE)
            if j + 1 < FF // WIDE:
                made[j + 1] = raised(j + 1)
            a, g = gelu_pair(made.pop(j))
            al = a.astype(jnp.bfloat16)
            gp[:, cols] = g.astype(jnp.bfloat16)
            actT[cols, :] = al.T
            acc[...] += dot(al, wd[cols, :])
        refill(l, 2, 3)
        ship(l, gp, o_gp, 8)
        ship(l, actT, o_actT, 9)

        claim(1, 10, 11)
        x = acc[...] + b_down[l : l + 1, :]
        y, n, r = norm(x, gain_two[l : l + 1, :], shift_two[l : l + 1, :])
        hid[...] = y
        if l + 1 < layers:
            rounded = y.astype(jnp.bfloat16)
            low[...] = rounded
            hidT[...] = rounded.T
        n2[...] = n.astype(jnp.bfloat16)
        r2[...] = jnp.broadcast_to(r, (T, 128))
        ship(l, n2, o_n2, 10)
        ship(l, r2, o_r2, 11)

    count = parts * segs
    member_t = jnp.concatenate(
        [
            (lax.broadcasted_iota(jnp.int32, (segs, piece), 0) == row).astype(jnp.float32)
            for row in id_rows
        ],
        axis=1,
    )
    sizes = jnp.sum(member_t, axis=-1, keepdims=True)
    member_t = member_t.astype(jnp.bfloat16)
    high, rest = split(hid[...])
    embed = (dot(member_t, high) + dot(member_t, rest)) / sizes
    scale = lax.rsqrt(jnp.sum(embed * embed, axis=-1, keepdims=True) + NORM_EPS)
    unit = embed * scale
    ubuf[...] = jnp.zeros_like(ubuf)
    gbuf[zi] = unit

    def ucopy(k):
        return remote(gbuf.at[zi], gbuf.at[zi], usem.at[0, k], usem.at[1, k], (me, peer(k)))

    for k in range(1, parts):
        ucopy(k).start()
    prow[...] = jnp.zeros_like(prow)
    prow[:1, :count] = pair[...].astype(jnp.float32)
    partner = prow[...].T[:, :1]
    side = ubuf.shape[0]
    row_no = lax.broadcasted_iota(jnp.int32, (side, side), 0)
    col_no = lax.broadcasted_iota(jnp.int32, (side, side), 1)
    live = (row_no < count) & (col_no < count)
    chosen = jnp.where(live & (partner == col_no.astype(jnp.float32)), 1.0, 0.0)
    for k in range(1, parts):
        ucopy(k).wait()
    for k in range(parts):
        ubuf[k * segs : (k + 1) * segs, :] = gbuf[k]
    high, rest = split(ubuf[...])
    logits = 20.0 * (dot_t(high, high) + dot_t(high, rest) + dot_t(rest, high))
    logits = jnp.where(live, logits, -1e30)
    top = jnp.max(logits, axis=-1, keepdims=True)
    grown = jnp.exp(logits - top)
    total = jnp.sum(grown, axis=-1, keepdims=True)
    pull = jnp.where(live, (grown / total - chosen) * (20.0 * LOSS_SCALE / count), 0.0)
    acc[:side, :side] = pull + pull.T
    own = pl.ds(pl.multiple_of(zi * segs, segs), segs)
    ours, ours_rest = split(acc[own, :side])
    grad_unit = dot(ours, high) + dot(ours, rest) + dot(ours_rest, high)
    inner = jnp.sum(grad_unit * unit, axis=-1, keepdims=True)
    grad_sums = scale * (grad_unit - unit * inner) / sizes
    high, rest = split(grad_sums)
    both = jnp.concatenate([grad_sums, grad_sums - high.astype(jnp.float32)], axis=0).astype(jnp.bfloat16)
    lanes = lax.broadcasted_iota(jnp.int32, (piece, 2 * segs), 1)
    lanes = jnp.where(lanes < segs, lanes, lanes - segs).astype(jnp.float32)
    for i in range(parts):
        member = (lanes == id_cols[:, i : i + 1]).astype(jnp.bfloat16)
        grad_out[i * piece : (i + 1) * piece, :] = dot(member, both)
    picked = jnp.sum(chosen * logits, axis=-1, keepdims=True)
    losses = jnp.where(row_no[:, :1] < count, top + jnp.log(total) - picked, 0.0)
    loss_out[...] = jnp.sum(losses, axis=0, keepdims=True) / count
    claim(*list(outs))


def forward(tokens, segment_ids, pair_ids, w):
    parts, piece, D = tokens.shape
    T = parts * piece
    L = w["w_qkv"].shape[0]
    FF = w["w_up"].shape[2]
    segs = pair_ids.shape[0] // parts
    side = 128
    bf, f32 = jnp.bfloat16, jnp.float32
    S = jax.ShapeDtypeStruct
    V = pltpu.VMEM
    vm = pl.BlockSpec(memory_space=V)
    anyspec = pl.BlockSpec(memory_space=pl.ANY)
    H = D // HD
    dma = pltpu.SemaphoreType.DMA
    out_shape = (
        S((T, D), f32), S((1, 1), f32), S((L, T, 3 * D), bf), S((L, H, T, T), bf), S((L, T, D), f32), S((L, T, D), f32),
        S((L, D, T), bf), S((L, D, T), bf), S((L, D, T), bf), S((L, FF, T), bf), S((L, T, FF), bf),
        S((L, T, D), bf), S((L, T, 128), f32), S((L, T, D), bf), S((L, T, 128), f32),
    )
    scratch = [
        V((D, 3 * D), bf), V((D, D), bf), V((D, FF), bf), V((FF, D), bf),
        V((T, T), f32), V((T, D), f32), V((T, D), bf), V((parts, 1, piece), jnp.int32),
        V((T, 3 * D), bf), V((H, T, T), bf), V((T, D), f32), V((T, D), f32), V((T, D), bf), V((T, D), f32), V((T, FF), bf),
        V((T, D), bf), V((T, 128), f32), V((T, D), bf), V((T, 128), f32),
        V((D, T), bf), V((D, T), bf), V((D, T), bf), V((FF, T), bf), V((T, D), f32),
        V((side, D), f32), V((parts, segs, D), f32), V((8, side), f32),
        dma((4,)), dma((13,)), dma((2, 2, parts)), dma((2, parts)),
    ]
    return pl.pallas_call(
        functools.partial(fwd_kernel, L, segs),
        out_shape=out_shape,
        in_specs=[anyspec] * 2 + [vm] * 10 + [anyspec] * 4,
        out_specs=(vm, vm) + (anyspec,) * 13,
        scratch_shapes=scratch,
        compiler_params=pltpu.CompilerParams(
            vmem_limit_bytes=60 * 1024 * 1024, collective_id=1, has_side_effects=True
        ),
        name="forward",
    )(
        tokens, segment_ids.reshape(parts, 1, piece), pair_ids.reshape(1, -1),
        *(w[k] for k in ("b_query", "b_value", "b_out", "gain_one", "shift_one", "b_up", "b_down", "gain_two", "shift_two")),
        *(w[k] for k in ("w_qkv", "w_out", "w_up", "w_down")),
    )


def low_sum(one, other):
    return (one.astype(jnp.float32) + other.astype(jnp.float32)).astype(jnp.bfloat16)


def bwd_kernel(
    layers, g_in, gain_one, gain_two,
    w_qkv, w_out, w_up, w_down,
    h_qkv, h_p, h_rl, h_pv, h_hidT, h_mixT, h_nrmT, h_actT, h_gp, h_n1, h_r1, h_n2, h_r2,
    out, gt_out, vec_out,
    wd, wu, gp, actT, wq, qkv, pb, rl, pv, wo, hidT, mixT, nrmT, n1, r1, n2, r2,
    acc, second, branch, gm, gpre, rhs, vec, vrecv, gb,
    sendc, keepq, recvq, s1, k1, t1, s2, k2, t2, za, zr, zb, zt, zf,
    fsem, asem, lsem, csem, xsem, ysem, zsem, osem, vsem, gsem,
):
    T, D = g_in.shape
    FF = w_up.shape[2]
    R = D // WAYS
    U = 4 * R
    n_ffn = FF // D
    n_att = D // 128
    group = D // C
    macros = n_ffn + n_att
    per = n_ffn * group + n_att
    n_units = layers * per
    n_macros = layers * macros

    me = lax.axis_index("dp")
    zi = lax.axis_index("seq")
    oc = lax.rem(me, 2)
    ox = lax.rem(lax.div(me, 2), 2)
    oy = lax.rem(lax.div(me, 4), 2)
    core = (me + 1 - 2 * oc, zi)
    xdev = (me + 2 - 4 * ox, zi)
    ydev = (me + 4 - 8 * oy, zi)
    inner = (zi == 1) | (zi == 2)
    outer = (zi == 0) | (zi == 3)
    to_inner = (me, 1 + lax.div(zi, 2))
    across = (me, 3 - zi)
    to_outer = (me, 3 * lax.div(zi, 2))

    def place(n):
        y = lax.rem(oy + n // 2 % 2, 2)
        x = lax.rem(ox + n % 2, 2)
        return 4 * y + 2 * x + lax.rem(oc + n // 4, 2)

    def turned(src, dst, l):
        return [(src.at[l, place(n)], dst.at[pl.ds(n * R, R)]) for n in range(WAYS)]

    def copies(parts, sem):
        return [pltpu.make_async_copy(a, b, sem.at[k]) for k, (a, b) in enumerate(parts)]

    def ffn_tile(f):
        l = layers - 1 - lax.div(f, n_ffn)
        rb = lax.rem(f, n_ffn)
        s = lax.rem(f, 2)
        span = pl.ds(pl.multiple_of(rb * D, D), D)
        parts = [(w_down.at[l, span], wd.at[s]), (w_up.at[l, :, span], wu.at[s]), (h_gp.at[l, :, span], gp.at[s])]
        parts += [(h_actT.at[l, place(n), rb], actT.at[s, pl.ds(n * R, R)]) for n in range(WAYS)]
        return copies(parts, fsem.at[s])

    def att_tile(a):
        l = layers - 1 - lax.div(a, n_att)
        i = lax.rem(a, n_att)
        s = lax.rem(a, 2)
        parts = [(h_p.at[l, pl.ds(2 * i, 2)], pb.at[s])]
        for k in range(3):
            span = pl.ds(pl.multiple_of(i * 128 + k * D, 128), 128)
            parts.append((w_qkv.at[l, :, span], wq.at[s, :, pl.ds(k * 128, 128)]))
            parts.append((h_qkv.at[l, :, span], qkv.at[s, :, pl.ds(k * 128, 128)]))
        span = pl.ds(pl.multiple_of(i * 128, 128), 128)
        parts += [(h_rl.at[l, :, span], rl.at[s]), (h_pv.at[l, :, span], pv.at[s])]
        return copies(parts, asem.at[s])

    def ffn_layer(l):
        return copies([(h_n2.at[l], n2), (h_r2.at[l], r2)] + turned(h_nrmT, nrmT, l), lsem.at[0])

    def att_layer(l):
        parts = [(h_n1.at[l], n1), (h_r1.at[l], r1), (w_out.at[l], wo)]
        return copies(parts + turned(h_hidT, hidT, l) + turned(h_mixT, mixT, l), lsem.at[1])

    def start(made):
        for c in made:
            c.start()

    def wait(made):
        for c in made:
            c.wait()

    start(ffn_layer(layers - 1))
    for n in range(2):
        start(ffn_tile(jnp.int32(n)))
    start(att_layer(layers - 1))
    for n in range(2):
        start(att_tile(jnp.int32(n)))
    acc[...] = g_in[...]
    vec[...] = jnp.zeros_like(vec)
    greet([core, xdev, ydev] + [(me, lax.rem(zi + k, 4)) for k in range(1, 4)])

    lane = lax.broadcasted_iota(jnp.int32, (T, 128), 1)
    first = lane < HD

    def norm_back(g, n, r, gain):
        e = g * gain
        return r * (e - jnp.mean(e, axis=-1, keepdims=True) - n * jnp.mean(e * n, axis=-1, keepdims=True))

    def col_sum(v):
        return jnp.sum(v.astype(jnp.float32), axis=0, keepdims=True)

    def through_norm(l, base, normal, root, gain, rounded):
        g = acc[...]
        n = normal[...].astype(jnp.float32)
        d = norm_back(g, n, root[:, :1], gain)
        acc[...] = d
        low = d.astype(jnp.bfloat16)
        rounded[...] = low
        for k, v in enumerate((low, g * n, g)):
            vec[l, base + k : base + k + 1, :] = col_sum(v)

    def prologue(l):
        wait(ffn_layer(l))
        through_norm(l, 5 + n_ffn, n2, r2, gain_two[pl.ds(l, 1), :], second)

    def middle(l):
        wait(att_layer(l))
        through_norm(l, 2, n1, r1, gain_one[pl.ds(l, 1), :], branch)
        gm[...] = dot_t(branch[...], wo[...]).astype(jnp.bfloat16)

    def ffn(l, rb, c):
        f = (layers - 1 - l) * n_ffn + rb
        s = lax.rem(f, 2)
        q = rb * group
        wait(ffn_tile(f))
        low = (dot_t(second[...], wd[s]) * gp[s].astype(jnp.float32)).astype(jnp.bfloat16)
        gpre[...] = low
        vec[l, pl.ds(5 + rb, 1), :] = col_sum(low)
        for k, (left, right) in enumerate(((nrmT, gpre), (actT.at[s], second))):
            made = dot(left[...], right[...]).astype(jnp.bfloat16)
            for n in range(group):
                keepq[q + n, k] = made[:U, n * C : (n + 1) * C]
                sendc[c, n, k] = made[U:, n * C : (n + 1) * C]
        acc[...] += dot_t(gpre[...], wu[s])

        @pl.when(f + 2 < layers * n_ffn)
        def _():
            start(ffn_tile(f + 2))

    def attend(l, i, c):
        a = (layers - 1 - l) * n_att + i
        o = pl.multiple_of(i * 128, 128)
        s = lax.rem(a, 2)
        q = n_ffn * group + i
        wait(att_tile(a))
        q2, k2, v2 = (qkv[s, :, k * 128 : (k + 1) * 128] for k in range(3))
        g2 = (gm[:, pl.ds(o, 128)].astype(jnp.float32) * rl[s]).astype(jnp.bfloat16)
        weighed = g2.astype(jnp.float32) * pv[s]
        zero = jnp.zeros_like(q2)
        q2t, g2t = q2.T, g2.T
        dq = None
        dkt, dvt = [], []
        for h in range(2):
            sel = first if h == 0 else ~first
            p = pb[s, h]
            gprob = dot_t(jnp.where(sel, g2, zero), v2)
            centre = jnp.sum(jnp.where(sel, weighed, 0.0), axis=-1, keepdims=True)
            ds = (p.astype(jnp.float32) * (gprob - centre)).astype(jnp.bfloat16)
            part = dot(ds, jnp.where(sel, k2, zero))
            dq = part if h == 0 else dq + part
            dkt.append(dot(q2t[h * HD : (h + 1) * HD], ds))
            dvt.append(dot(g2t[h * HD : (h + 1) * HD], p))
        dq = (dq * 0.125).astype(jnp.bfloat16)
        dk = jnp.concatenate(dkt, axis=0).astype(jnp.bfloat16).T
        dv = jnp.concatenate(dvt, axis=0).astype(jnp.bfloat16).T
        vec[l, 0:1, pl.ds(o, 128)] = col_sum(dq)
        vec[l, 1:2, pl.ds(o, 128)] = col_sum(dv)
        rhs[:, :128] = dq
        rhs[:, 128:256] = dk
        rhs[:, 256:] = dv
        made = dot(hidT[...], rhs[...]).astype(jnp.bfloat16)
        keepq[q, 0] = made[:U, :C]
        sendc[c, 0, 0] = made[U:, :C]
        keepq[q, 1, :, :128] = made[:U, C:]
        sendc[c, 0, 1, :, :128] = made[U:, C:]
        made = dot(mixT[...], branch[:, pl.ds(o, 128)]).astype(jnp.bfloat16)
        keepq[q, 1, :, 128:] = made[:U]
        sendc[c, 0, 1, :, 128:] = made[U:]
        acc[...] += dot_t(rhs[...], wq[s])

        @pl.when(a + 2 < layers * n_att)
        def _():
            start(att_tile(a + 2))

    def core_copy(m, wide):
        c = lax.rem(m, 2)
        k = lax.rem(m, macros)
        q = k * group if wide else n_ffn * group + k - n_ffn
        size = group if wide else 1
        return remote(
            sendc.at[c, pl.ds(0, size)], recvq.at[pl.ds(q, size)], csem.at[0, m], csem.at[1, m], core
        )

    def is_wide(m):
        return lax.rem(m, macros) < n_ffn

    def copies_one(u):
        s = lax.rem(u, SLOTS)
        return [
            remote(s1.at[s, k], t1.at[s, k], xsem.at[0, k, s], xsem.at[1, k, s], (xdev, ydev)[k]) for k in range(2)
        ]

    def copy_two(u, k):
        s = lax.rem(u, SLOTS)
        return remote(s2.at[s, k], t2.at[s, k], ysem.at[0, k, s], ysem.at[1, k, s], (ydev, xdev)[k])

    def copy_in(u, k):
        s = lax.rem(u, SLOTS)
        return remote(za.at[s, k], zr.at[s, k], zsem.at[0, k, s], zsem.at[1, k, s], to_inner)

    def copy_across(u, k):
        s = lax.rem(u, SLOTS)
        return remote(zb.at[s, k], zt.at[s, k], zsem.at[2, k, s], zsem.at[3, k, s], across)

    def copy_out(u, k):
        s = lax.rem(u, SLOTS)
        return remote(zf.at[s, k], out.at[u, k], zsem.at[4, k, s], zsem.at[5, k, s], to_outer)

    def copy_home(u):
        s = lax.rem(u, SLOTS)
        return pltpu.make_async_copy(zf.at[s], out.at[u], osem.at[s])

    def stage_one(u):
        s = lax.rem(u, QUEUE)
        d = lax.rem(u, SLOTS)
        base = lax.div(u, per) * macros

        @pl.when(u == 0)
        def _():
            core_copy(base, True).wait_recv()

        @pl.when(u >= n_units - 2)
        def _():
            core_copy(base + n_ffn + s - n_ffn * group, False).wait_recv()

        for k in range(2):
            sent, kept = ((1, 3), (0, 2)) if k == 0 else ((2, 3), (0, 1))
            for n, (a, b) in enumerate(zip(sent, kept)):
                to = pl.ds(n * R, R)
                s1[d, k, to] = low_sum(keepq[s, k, pl.ds(a * R, R)], recvq[s, k, pl.ds(a * R, R)])
                k1[d, k, to] = low_sum(keepq[s, k, pl.ds(b * R, R)], recvq[s, k, pl.ds(b * R, R)])
        start(copies_one(u))

    def stage_two(u):
        d = lax.rem(u, SLOTS)
        wait(copies_one(u))
        for k in range(2):
            s2[d, k] = low_sum(k1[d, k, pl.ds(R, R)], t1[d, k, pl.ds(R, R)])
            k2[d, k] = low_sum(k1[d, k, pl.ds(0, R)], t1[d, k, pl.ds(0, R)])
        start([copy_two(u, k) for k in range(2)])

    def stage_three(u):
        d = lax.rem(u, SLOTS)
        for k in range(2):
            copy_two(u, k).wait()
            za[d, k] = low_sum(k2[d, k], t2[d, k])

            @pl.when(outer)
            def _(k=k):
                copy_in(u, k).start()

    def stage_four(u):
        d = lax.rem(u, SLOTS)

        @pl.when(outer)
        def _():
            for k in range(2):
                copy_in(u, k).wait_send()

        @pl.when(inner)
        def _():
            for k in range(2):
                copy_in(u, k).wait_recv()
                zb[d, k] = low_sum(za[d, k], zr[d, k])
                copy_across(u, k).start()

    def stage_five(u):
        d = lax.rem(u, SLOTS)

        @pl.when(inner)
        def _():
            for k in range(2):
                copy_across(u, k).wait()
                zf[d, k] = low_sum(zb[d, k], zt[d, k])
                copy_out(u, k).start()
            copy_home(u).start()

    def stage_six(u):
        @pl.when(inner)
        def _():
            for k in range(2):
                copy_out(u, k).wait_send()
            copy_home(u).wait()

        @pl.when(outer)
        def _():
            for k in range(2):
                copy_out(u, k).wait_recv()

    stages = (None, stage_one, stage_two, stage_three, stage_four, stage_five, stage_six)

    def run_stage(i, k):
        u = i - LAGS[k]

        @pl.when((u >= 0) & (u < n_units))
        def _():
            stages[k](u)

    def vec_copy(k):
        where = (core, xdev, ydev, to_inner, across, to_outer)[k]
        return remote(vec, vrecv.at[k], vsem.at[0, k], vsem.at[1, k], where)

    def vec_step(k):
        if 1 <= k <= 3:
            vec_copy(k - 1).wait()
            vec[...] += vrecv[k - 1]
        if k < 3:
            vec_copy(k).start()
        if k == 3:

            @pl.when(outer)
            def _():
                vec_copy(3).start()

        if k == 4:

            @pl.when(outer)
            def _():
                vec_copy(3).wait_send()

            @pl.when(inner)
            def _():
                vec_copy(3).wait_recv()
                vec[...] += vrecv[3]
                vec_copy(4).start()

        if k == 5:

            @pl.when(inner)
            def _():
                vec_copy(4).wait()
                vec[...] += vrecv[4]
                vec_copy(5).start()

        if k == 6:

            @pl.when(inner)
            def _():
                vec_copy(5).wait_send()
                vec_out[...] = vec[...]

            @pl.when(outer)
            def _():
                vec_copy(5).wait_recv()
                vec_out[...] = vrecv[5]

    part = T // 4
    slab = part // GT_PARTS

    def gt_own():
        own = pl.ds(pl.multiple_of(zi * part, part), part)
        return pltpu.make_async_copy(gb.at[own], gt_out.at[zi], gsem.at[0, 3 * GT_PARTS])

    def gt_copy(n):
        peer = lax.rem(zi + 1 + lax.rem(n, 3), 4)
        o = lax.div(n, 3) * slab
        src = gb.at[pl.ds(pl.multiple_of(peer * part + o, slab), slab)]
        dst = gt_out.at[zi, pl.ds(pl.multiple_of(o, slab), slab)]
        return remote(src, dst, gsem.at[0, n], gsem.at[1, n], (me, peer))

    def done_by(i):
        num, den = PACE
        return jnp.minimum(lax.div(num * (i + 1) + den - 1, den), n_macros)

    last = 0
    while -(-PACE[0] * (last + 1) // PACE[1]) < n_macros:
        last += 1

    def step(i, carry):
        for k in range(6, 1, -1):
            run_stage(i, k)
        run_stage(i, 1)
        m = done_by(i - 1)
        l = layers - 1 - lax.div(m, macros)
        k = lax.rem(m, macros)
        c = lax.rem(m, 2)
        busy = done_by(i) > m

        @pl.when(busy & (m >= 2) & is_wide(m - 2))
        def _():
            core_copy(m - 2, True).wait_send()

        @pl.when(busy & (m >= 3) & is_wide(m - 2))
        def _():
            core_copy(m - 2, True).wait_recv()

        @pl.when(busy & (m >= 2) & ~is_wide(m - 2))
        def _():
            core_copy(m - 2, False).wait()

        @pl.when(busy & (k == 0))
        def _():
            prologue(l)

        @pl.when(busy & (k == 0) & (l < layers - 1))
        def _():
            start(att_layer(l))

        @pl.when(busy & (k < n_ffn))
        def _():
            ffn(l, k, c)
            core_copy(m, True).start()

        @pl.when(busy & (k == n_ffn) & (l > 0))
        def _():
            start(ffn_layer(l - 1))

        @pl.when(busy & (k == n_ffn))
        def _():
            middle(l)

        @pl.when(busy & (k >= n_ffn))
        def _():
            attend(l, k - n_ffn, c)
            core_copy(m, False).start()

        @pl.when(i == last + 1)
        def _():
            gb[...] = acc[...].astype(jnp.bfloat16)
            gt_own().start()

        @pl.when((i > last) & (i <= last + 3 * GT_PARTS))
        def _():
            gt_copy(i - last - 1).start()

        for n in range(7):

            @pl.when(i == last + 1 + 2 * n)
            def _(n=n):
                vec_step(n)

        return carry

    lax.fori_loop(0, n_units + LAGS[6], step, 0)
    for m in (n_macros - 2, n_macros - 1):
        core_copy(jnp.int32(m), False).wait_send()
    gt_own().wait()

    def gt_wait(n, c):
        gt_copy(n).wait()
        return c

    lax.fori_loop(0, 3 * GT_PARTS, gt_wait, 0)


def backward(grad_hidden, res, w):
    T, D = grad_hidden.shape
    L = w["w_qkv"].shape[0]
    FF = w["w_up"].shape[2]
    bf, f32 = jnp.bfloat16, jnp.float32
    S = jax.ShapeDtypeStruct
    V = pltpu.VMEM
    vm = pl.BlockSpec(memory_space=V)
    anyspec = pl.BlockSpec(memory_space=pl.ANY)
    R = D // WAYS
    U = 4 * R
    group = D // C
    n_units = L * (FF // C + D // 128)
    n_macros = L * (FF // D + D // 128)
    dma = pltpu.SemaphoreType.DMA
    scratch = [
        V((2, D, D), bf), V((2, D, D), bf), V((2, T, D), bf), V((2, D, T), bf),
        V((2, D, 384), bf), V((2, T, 384), bf), V((2, 2, T, T), bf), V((2, T, 128), f32), V((2, T, 128), f32),
        V((D, D), bf), V((D, T), bf), V((D, T), bf), V((D, T), bf),
        V((T, D), bf), V((T, 128), f32), V((T, D), bf), V((T, 128), f32),
        V((T, D), f32), V((T, D), bf), V((T, D), bf), V((T, D), bf), V((T, D), bf), V((T, 384), bf),
        V((L, VEC_ROWS, D), f32), V((6, L, VEC_ROWS, D), f32), V((T, D), bf),
        V((2, group, 2, U, C), bf), V((QUEUE, 2, U, C), bf), V((QUEUE, 2, U, C), bf),
        V((SLOTS, 2, 2 * R, C), bf), V((SLOTS, 2, 2 * R, C), bf), V((SLOTS, 2, 2 * R, C), bf),
        V((SLOTS, 2, R, C), bf), V((SLOTS, 2, R, C), bf), V((SLOTS, 2, R, C), bf),
        V((SLOTS, 2, R, C), bf), V((SLOTS, 2, R, C), bf), V((SLOTS, 2, R, C), bf),
        V((SLOTS, 2, R, C), bf), V((SLOTS, 2, R, C), bf),
        dma((2, 3 + WAYS)), dma((2, 9)), dma((2, 3 + 2 * WAYS)), dma((2, n_macros)), dma((2, 2, SLOTS)), dma((2, 2, SLOTS)),
        dma((6, 2, SLOTS)), dma((SLOTS,)), dma((2, 6)), dma((2, 3 * GT_PARTS + 1)),
    ]
    return pl.pallas_call(
        functools.partial(bwd_kernel, L),
        out_shape=(
            S((n_units, 2, R, C), bf), S((4, T // 4, D), bf), S((L, VEC_ROWS, D), f32),
        ),
        in_specs=[vm] * 3 + [anyspec] * 17,
        out_specs=(anyspec, anyspec, vm),
        scratch_shapes=scratch,
        compiler_params=pltpu.CompilerParams(
            vmem_limit_bytes=60 * 1024 * 1024, collective_id=0, has_side_effects=True
        ),
        name="backward",
    )(
        grad_hidden, w["gain_one"], w["gain_two"],
        *(w[k] for k in ("w_qkv", "w_out", "w_up", "w_down")),
        *res,
    )


def finish_kernel(units, gt, vec, g_tok, g_qkv, g_out, g_up, g_down, *vectors):
    l = pl.program_id(0)
    R, D = g_out.shape[1:]
    n_ffn = g_up.shape[2] // D
    group = D // C
    g_tok[...] = gt[...].astype(jnp.float32)

    def read(n, k, cols=slice(None)):
        return units[0, n, k, :, cols].astype(jnp.float32)

    for rb in range(n_ffn):
        for n in range(group):
            u = rb * group + n
            g_up[0, :, u * C : (u + 1) * C] = read(u, 0)
            g_down[0, rb * R : (rb + 1) * R, n * C : (n + 1) * C] = read(u, 1)
    for i in range(D // 128):
        u = n_ffn * group + i
        for k in range(3):
            half = slice(k % 2 * 128, k % 2 * 128 + 128)
            g_qkv[0, :, k * D + i * 128 : k * D + (i + 1) * 128] = read(u, k // 2, half)
        g_out[0, :, i * 128 : (i + 1) * 128] = read(u, 1, slice(128, 256))
    row = 0
    for ref in vectors:
        for k in range(ref.shape[1] // D):
            ref[pl.ds(l, 1), k * D : (k + 1) * D] = vec[0, row : row + 1, :]
            row += 1


def finish(units, grad_tokens, vec, layers, hidden_units):
    n_units, _, R, _ = units.shape
    parts, piece, D = grad_tokens.shape
    L, FF = layers, hidden_units
    f32 = jnp.float32
    S = jax.ShapeDtypeStruct
    per = n_units // L
    widths = (D, D, D, D, D, FF, D, D, D)
    return pl.pallas_call(
        finish_kernel,
        grid=(L,),
        out_shape=(
            S((parts, piece, D), f32), S((L, R, 3 * D), f32), S((L, R, D), f32), S((L, R, FF), f32),
            S((L, FF // WAYS, D), f32),
        ) + tuple(S((L, width), f32) for width in widths),
        in_specs=[
            pl.BlockSpec((1, per, 2, R, C), lambda l: (L - 1 - l, 0, 0, 0, 0)),
            pl.BlockSpec((parts // L, piece, D), lambda l: (l, 0, 0)),
            pl.BlockSpec((1, VEC_ROWS, D), lambda l: (l, 0, 0)),
        ],
        out_specs=(
            pl.BlockSpec((parts // L, piece, D), lambda l: (l, 0, 0)),
            pl.BlockSpec((1, R, 3 * D), lambda l: (l, 0, 0)),
            pl.BlockSpec((1, R, D), lambda l: (l, 0, 0)),
            pl.BlockSpec((1, R, FF), lambda l: (l, 0, 0)),
            pl.BlockSpec((1, FF // WAYS, D), lambda l: (l, 0, 0)),
        ) + tuple(pl.BlockSpec((L, width), lambda l: (0, 0)) for width in widths),
        compiler_params=pltpu.CompilerParams(vmem_limit_bytes=60 * 1024 * 1024),
        name="finish",
    )(units.reshape(L, per, 2, R, C), grad_tokens, vec)


NAMES = (
    "w_qkv",
    "b_query",
    "b_value",
    "w_out",
    "b_out",
    "gain_one",
    "shift_one",
    "w_up",
    "b_up",
    "w_down",
    "b_down",
    "gain_two",
    "shift_two",
)


def by_class(array, block, ways):
    layers, rows, tokens_here = array.shape
    if ways == 1:
        return array.reshape(layers, WAYS, -1, tokens_here)
    array = array.reshape(layers, ways, WAYS, block, tokens_here)
    return jnp.swapaxes(array, 1, 2).reshape(layers, WAYS, -1, tokens_here)


def on_device(dp_count, tokens, segment_ids, pair_ids, *weights):
    w = dict(zip(NAMES, weights))
    layer_count, model_width, _ = w["w_qkv"].shape
    hidden_units = w["w_up"].shape[2]
    ways = dp_count // WAYS
    grad_hidden, loss_value, *res = forward(tokens, segment_ids, pair_ids, w)
    for place in (4, 5, 6):
        res[place] = by_class(res[place], model_width // dp_count, ways)
    block = model_width // WAYS
    acts = by_class(res[7], hidden_units // dp_count, ways)
    res[7] = acts.reshape(layer_count, WAYS, -1, block, acts.shape[-1])
    units, grad_tokens, vec = backward(grad_hidden, res, w)
    if ways > 1:
        groups = [[low + WAYS * high for high in range(ways)] for low in range(WAYS)]
        vec = lax.psum(vec, "dp", axis_index_groups=groups)
    grad_tokens, *rest = finish(units, grad_tokens, vec, layer_count, hidden_units)
    matrices, vectors = rest[:4], rest[4:]
    if ways > 1:
        matrices = [
            lax.psum_scatter(
                matrix, "dp", scatter_dimension=1, axis_index_groups=groups, tiled=True
            )
            for matrix in matrices
        ]
    g_qkv, g_out, g_up, g_down = matrices
    return (
        loss_value.reshape(1),
        grad_tokens,
        g_qkv,
        vectors[0],
        vectors[1],
        g_out,
        vectors[2],
        vectors[3],
        vectors[4],
        g_up,
        vectors[5],
        g_down,
        vectors[6],
        vectors[7],
        vectors[8],
    )


def solution(mesh):
    return jax.shard_map(
        functools.partial(on_device, mesh.shape["dp"]),
        mesh=mesh,
        in_specs=(P("dp", "seq", None), P("dp", "seq"), P("dp")) + (P(),) * 13,
        out_specs=(
            P("dp"),
            P("dp", "seq", None),
            P(None, "dp", None),
            P(),
            P(),
            P(None, "dp", None),
            P(),
            P(),
            P(),
            P(None, "dp", None),
            P(),
            P(None, "dp", None),
            P(),
            P(),
            P(),
        ),
        check_vma=False,
    )
```

```python
import functools

import jax
import jax.numpy as jnp
from jax import lax
from jax.experimental import pallas as pl
from jax.experimental.pallas import tpu as pltpu
from jax.sharding import PartitionSpec as P

MESH = pl.DeviceIdType.MESH
LOSS_SCALE = 1024.0
NORM_EPS = 1e-06
HD = 64
WIDE = 768
C = 256
WAYS = 8
QUEUE = 18
SLOTS = 6
LAGS = (0, 1, 3, 5, 7, 9, 11)
PACE = (5, 6)
GT_PARTS = 4
VEC_ROWS = 16


def dot(left, right):
    return lax.dot_general(
        left,
        right,
        (((1,), (0,)), ((), ())),
        preferred_element_type=jnp.float32,
    )


def dot_t(left, right):
    return lax.dot_general(
        left,
        right,
        (((1,), (1,)), ((), ())),
        preferred_element_type=jnp.float32,
    )


def split(values):
    high = values.astype(jnp.bfloat16)
    return high, (values - high.astype(jnp.float32)).astype(jnp.bfloat16)


def remote(src, dst, send_sem, recv_sem, where):
    return pltpu.make_async_remote_copy(
        src_ref=src,
        dst_ref=dst,
        send_sem=send_sem,
        recv_sem=recv_sem,
        device_id=where,
        device_id_type=MESH,
    )


def greet(peers):
    barrier = pltpu.get_barrier_semaphore()
    for peer in peers:
        pl.semaphore_signal(barrier, inc=1, device_id=peer, device_id_type=MESH)
    pl.semaphore_wait(barrier, len(peers))


def gelu_pair(x):
    t = 1.0 / (1.0 + 0.23164190 * jnp.abs(x))
    gauss = jnp.exp(-0.5 * x * x)
    poly = t * (
        0.127414796
        + t * (-0.142248368 + t * (0.7107068705 + t * (-0.7265760135 + t * 0.5307027145)))
    )
    tail = poly * gauss
    phi = jnp.where(x >= 0.0, 1.0 - tail, tail)
    return x * phi, phi + x * (gauss * 0.3989422804014327)


def norm(x, gain, shift):
    centre = x - jnp.mean(x, axis=-1, keepdims=True)
    scaled = lax.rsqrt(jnp.mean(centre * centre, axis=-1, keepdims=True) + NORM_EPS)
    normal = centre * scaled
    return normal * gain + shift, normal, scaled


def fwd_kernel(
    layers, segs,
    tok, ids, pair, b_query, b_value, b_out, gain_one, shift_one, b_up, b_down, gain_two, shift_two,
    w_qkv, w_out, w_up, w_down,
    grad_out, loss_out, o_qkv, o_p, o_rl, o_pv, o_hidT, o_mixT, o_nrmT, o_actT, o_gp, o_n1, o_r1, o_n2, o_r2,
    wq, wo, wu, wd, bias, hid, low, idbuf, qkv, pb, rl, pv, mix, nrm, gp, n1, r1, n2, r2,
    hidT, mixT, nrmT, actT, acc, ubuf, gbuf, prow,
    wsem, osem, tsem, usem,
):
    T, D = hid.shape
    FF = w_up.shape[2]
    piece = tok.shape[1]
    parts = T // piece
    me = lax.axis_index("dp")
    zi = lax.axis_index("seq")
    pairs = ((w_qkv, wq), (w_out, wo), (w_up, wu), (w_down, wd))

    def wcopy(l, i):
        return pltpu.make_async_copy(pairs[i][0].at[l], pairs[i][1], wsem.at[i])

    def peer(k):
        return lax.rem(zi + k, parts)

    mine = pl.ds(pl.multiple_of(zi * piece, piece), piece)

    def tcopy(k, n):
        src, dst = ((tok, low.at[mine]), (ids, idbuf.at[zi]))[n]
        if k == 0:
            return pltpu.make_async_copy(src.at[zi], dst, tsem.at[n, 0, 0])
        return remote(src.at[peer(k)], dst, tsem.at[n, 0, k], tsem.at[n, 1, k], (me, peer(k)))

    greet([(me, peer(k)) for k in range(1, parts)])
    for k in (2, 1, 3, 0):
        for n in (1, 0):
            tcopy(k, n).start()
    for i in range(4):
        wcopy(0, i).start()

    def refill(l, *which):
        @pl.when(l + 1 < layers)
        def _():
            for i in which:
                wcopy(l + 1, i).start()

    lane = lax.broadcasted_iota(jnp.int32, (T, 128), 1)
    first = lane < HD

    homes = (
        (qkv, o_qkv), (hidT, o_hidT), (rl, o_rl), (pv, o_pv), (mixT, o_mixT), (n1, o_n1), (r1, o_r1),
        (nrmT, o_nrmT), (gp, o_gp), (actT, o_actT), (n2, o_n2), (r2, o_r2), (pb, o_p),
    )

    def home(l, k):
        return pltpu.make_async_copy(homes[k][0], homes[k][1].at[l], osem.at[k])

    def ship(l, *keys):
        for k in keys:
            home(l, k).start()

    def claim(l, *keys):
        @pl.when(l > 0)
        def _():
            for k in keys:
                home(l - 1, k).wait()

    for k in range(parts):
        tcopy(k, 1).wait()
    id_rows = [idbuf[k] for k in range(parts)]
    id_cols = jnp.concatenate(
        id_rows + [jnp.zeros((8 - parts, piece), jnp.int32)], axis=0
    ).astype(jnp.float32).T
    for i in range(parts):
        for j in range(parts):
            same = id_cols[:, i : i + 1] == id_rows[j].astype(jnp.float32)
            bias[i * piece : (i + 1) * piece, j * piece : (j + 1) * piece] = jnp.where(same, 0.0, -1e30)
    for k in (0, 1, 3, 2):
        tcopy(k, 0).wait()
        source = pl.ds(pl.multiple_of(lax.rem(zi + parts - k, parts) * piece, piece), piece)
        arrived = low[source, :]
        hid[source, :] = arrived.astype(jnp.float32)
        hidT[:, source] = arrived.T

    def layer(l, carry):
        row = pl.ds(l, 1)
        wcopy(l, 0).wait()
        y = dot(low[...], wq[...])
        refill(l, 0)
        claim(l, 0)
        qkv[:, :D] = ((y[:, :D] + b_query[row, :]) * 0.125).astype(jnp.bfloat16)
        qkv[:, D : 2 * D] = y[:, D : 2 * D].astype(jnp.bfloat16)
        qkv[:, 2 * D :] = (y[:, 2 * D :] + b_value[row, :]).astype(jnp.bfloat16)
        ship(l, 0)
        ship(l, 1)

        def scores(n):
            o = n // 2 * 128
            q2 = qkv[:, o : o + 128]
            sel = first if n % 2 == 0 else ~first
            return dot_t(jnp.where(sel, q2, jnp.zeros_like(q2)), qkv[:, D + o : D + o + 128]) + bias[...]

        claim(l, 2, 3, 4, 12)
        made = {0: scores(0)}
        for n in range(D // HD):
            if n + 1 < D // HD:
                made[n + 1] = scores(n + 1)
            cols = slice(n // 2 * 128, n // 2 * 128 + 128)
            v2 = qkv[:, 2 * D + cols.start : 2 * D + cols.stop]
            sel = first if n % 2 == 0 else ~first
            sc = made.pop(n)
            e = jnp.exp(sc - jnp.max(sc, axis=-1, keepdims=True))
            recip = 1.0 / jnp.sum(e, axis=-1, keepdims=True)
            p = e.astype(jnp.bfloat16)
            pb[n] = p
            part = dot(p, jnp.where(sel, v2, jnp.zeros_like(v2))) * recip
            if n % 2 == 0:
                total, before = part, recip
                continue
            total = total + part
            rl[:, cols] = jnp.where(first, before, recip)
            pv[:, cols] = total
            low_total = total.astype(jnp.bfloat16)
            mix[:, cols] = low_total
            mixT[cols, :] = low_total.T
        ship(l, 12)
        ship(l, 2)
        ship(l, 3)
        wcopy(l, 1).wait()
        acc[...] = dot(mix[...], wo[...])
        refill(l, 1)
        ship(l, 4)

        claim(l, 5, 6, 7)
        x = hid[...] + acc[...] + b_out[row, :]
        y, n, r = norm(x, gain_one[row, :], shift_one[row, :])
        nrm[...] = y
        rounded = y.astype(jnp.bfloat16)
        low[...] = rounded
        nrmT[...] = rounded.T
        n1[...] = n.astype(jnp.bfloat16)
        r1[...] = jnp.broadcast_to(r, (T, 128))
        ship(l, 5)
        ship(l, 6)
        ship(l, 7)
        wcopy(l, 2).wait()
        wcopy(l, 3).wait()
        acc[...] = nrm[...]
        claim(l, 8, 9)

        def raised(j):
            cols = slice(j * WIDE, (j + 1) * WIDE)
            return dot(low[...], wu[:, cols]) + b_up[row, cols]

        made = {0: raised(0)}
        for j in range(FF // WIDE):
            cols = slice(j * WIDE, (j + 1) * WIDE)
            if j + 1 < FF // WIDE:
                made[j + 1] = raised(j + 1)
            a, g = gelu_pair(made.pop(j))
            al = a.astype(jnp.bfloat16)
            gp[:, cols] = g.astype(jnp.bfloat16)
            actT[cols, :] = al.T
            acc[...] += dot(al, wd[cols, :])
        refill(l, 2, 3)
        ship(l, 8)
        ship(l, 9)

        claim(l, 10, 11)
        home(l, 1).wait()
        x = acc[...] + b_down[row, :]
        y, n, r = norm(x, gain_two[row, :], shift_two[row, :])
        hid[...] = y

        @pl.when(l + 1 < layers)
        def _():
            rounded = hid[...].astype(jnp.bfloat16)
            low[...] = rounded
            hidT[...] = rounded.T

        n2[...] = n.astype(jnp.bfloat16)
        r2[...] = jnp.broadcast_to(r, (T, 128))
        ship(l, 10)
        ship(l, 11)
        return carry

    lax.fori_loop(0, layers, layer, 0)

    count = parts * segs
    member_t = jnp.concatenate(
        [
            (lax.broadcasted_iota(jnp.int32, (segs, piece), 0) == row).astype(jnp.float32)
            for row in id_rows
        ],
        axis=1,
    )
    sizes = jnp.sum(member_t, axis=-1, keepdims=True)
    member_t = member_t.astype(jnp.bfloat16)
    high, rest = split(hid[...])
    embed = (dot(member_t, high) + dot(member_t, rest)) / sizes
    scale = lax.rsqrt(jnp.sum(embed * embed, axis=-1, keepdims=True) + NORM_EPS)
    unit = embed * scale
    ubuf[...] = jnp.zeros_like(ubuf)
    gbuf[zi] = unit

    def ucopy(k):
        return remote(gbuf.at[zi], gbuf.at[zi], usem.at[0, k], usem.at[1, k], (me, peer(k)))

    for k in range(1, parts):
        ucopy(k).start()
    prow[...] = jnp.zeros_like(prow)
    prow[:1, :count] = pair[...].astype(jnp.float32)
    partner = prow[...].T[:, :1]
    side = ubuf.shape[0]
    row_no = lax.broadcasted_iota(jnp.int32, (side, side), 0)
    col_no = lax.broadcasted_iota(jnp.int32, (side, side), 1)
    live = (row_no < count) & (col_no < count)
    chosen = jnp.where(live & (partner == col_no.astype(jnp.float32)), 1.0, 0.0)
    for k in range(1, parts):
        ucopy(k).wait()
    for k in range(parts):
        ubuf[k * segs : (k + 1) * segs, :] = gbuf[k]
    high, rest = split(ubuf[...])
    logits = 20.0 * (dot_t(high, high) + dot_t(high, rest) + dot_t(rest, high))
    logits = jnp.where(live, logits, -1e30)
    top = jnp.max(logits, axis=-1, keepdims=True)
    grown = jnp.exp(logits - top)
    total = jnp.sum(grown, axis=-1, keepdims=True)
    pull = jnp.where(live, (grown / total - chosen) * (20.0 * LOSS_SCALE / count), 0.0)
    acc[:side, :side] = pull + pull.T
    own = pl.ds(pl.multiple_of(zi * segs, segs), segs)
    ours, ours_rest = split(acc[own, :side])
    grad_unit = dot(ours, high) + dot(ours, rest) + dot(ours_rest, high)
    inner = jnp.sum(grad_unit * unit, axis=-1, keepdims=True)
    grad_sums = scale * (grad_unit - unit * inner) / sizes
    high, rest = split(grad_sums)
    both = jnp.concatenate([grad_sums, grad_sums - high.astype(jnp.float32)], axis=0).astype(jnp.bfloat16)
    lanes = lax.broadcasted_iota(jnp.int32, (piece, 2 * segs), 1)
    lanes = jnp.where(lanes < segs, lanes, lanes - segs).astype(jnp.float32)
    for i in range(parts):
        member = (lanes == id_cols[:, i : i + 1]).astype(jnp.bfloat16)
        grad_out[i * piece : (i + 1) * piece, :] = dot(member, both)
    picked = jnp.sum(chosen * logits, axis=-1, keepdims=True)
    losses = jnp.where(row_no[:, :1] < count, top + jnp.log(total) - picked, 0.0)
    loss_out[...] = jnp.sum(losses, axis=0, keepdims=True) / count
    for k in range(len(homes)):
        if k != 1:
            home(layers - 1, k).wait()


def forward(tokens, segment_ids, pair_ids, w):
    parts, piece, D = tokens.shape
    T = parts * piece
    L = w["w_qkv"].shape[0]
    FF = w["w_up"].shape[2]
    segs = pair_ids.shape[0] // parts
    side = 128
    bf, f32 = jnp.bfloat16, jnp.float32
    S = jax.ShapeDtypeStruct
    V = pltpu.VMEM
    vm = pl.BlockSpec(memory_space=V)
    anyspec = pl.BlockSpec(memory_space=pl.ANY)
    H = D // HD
    dma = pltpu.SemaphoreType.DMA
    out_shape = (
        S((T, D), f32), S((1, 1), f32), S((L, T, 3 * D), bf), S((L, H, T, T), bf), S((L, T, D), f32), S((L, T, D), f32),
        S((L, D, T), bf), S((L, D, T), bf), S((L, D, T), bf), S((L, FF, T), bf), S((L, T, FF), bf),
        S((L, T, D), bf), S((L, T, 128), f32), S((L, T, D), bf), S((L, T, 128), f32),
    )
    scratch = [
        V((D, 3 * D), bf), V((D, D), bf), V((D, FF), bf), V((FF, D), bf),
        V((T, T), f32), V((T, D), f32), V((T, D), bf), V((parts, 1, piece), jnp.int32),
        V((T, 3 * D), bf), V((H, T, T), bf), V((T, D), f32), V((T, D), f32), V((T, D), bf), V((T, D), f32), V((T, FF), bf),
        V((T, D), bf), V((T, 128), f32), V((T, D), bf), V((T, 128), f32),
        V((D, T), bf), V((D, T), bf), V((D, T), bf), V((FF, T), bf), V((T, D), f32),
        V((side, D), f32), V((parts, segs, D), f32), V((8, side), f32),
        dma((4,)), dma((13,)), dma((2, 2, parts)), dma((2, parts)),
    ]
    return pl.pallas_call(
        functools.partial(fwd_kernel, L, segs),
        out_shape=out_shape,
        in_specs=[anyspec] * 2 + [vm] * 10 + [anyspec] * 4,
        out_specs=(vm, vm) + (anyspec,) * 13,
        scratch_shapes=scratch,
        compiler_params=pltpu.CompilerParams(
            vmem_limit_bytes=60 * 1024 * 1024, collective_id=1, has_side_effects=True
        ),
        name="forward",
    )(
        tokens, segment_ids.reshape(parts, 1, piece), pair_ids.reshape(1, -1),
        *(w[k] for k in ("b_query", "b_value", "b_out", "gain_one", "shift_one", "b_up", "b_down", "gain_two", "shift_two")),
        *(w[k] for k in ("w_qkv", "w_out", "w_up", "w_down")),
    )


def low_sum(one, other):
    return one + other


def bwd_kernel(
    layers, g_in, gain_one, gain_two,
    w_qkv, w_out, w_up, w_down,
    h_qkv, h_p, h_rl, h_pv, h_hidT, h_mixT, h_nrmT, h_actT, h_gp, h_n1, h_r1, h_n2, h_r2,
    out, gt_out, vec_out,
    wd, wu, gp, actT, wq, qkv, pb, rl, pv, wo, hidT, mixT, nrmT, n1, r1, n2, r2,
    acc, second, branch, gm, gpre, rhs, vec, vrecv, gb,
    sendc, keepq, recvq, s1, k1, t1, s2, k2, t2, za, zr, zb, zt, zf,
    fsem, asem, lsem, csem, xsem, ysem, zsem, osem, vsem, gsem,
):
    T, D = g_in.shape
    FF = w_up.shape[2]
    R = D // WAYS
    U = 4 * R
    n_ffn = FF // D
    n_att = D // 128
    group = D // C
    macros = n_ffn + n_att
    per = n_ffn * group + n_att
    n_units = layers * per
    n_macros = layers * macros

    me = lax.axis_index("dp")
    zi = lax.axis_index("seq")
    oc = lax.rem(me, 2)
    ox = lax.rem(lax.div(me, 2), 2)
    oy = lax.rem(lax.div(me, 4), 2)
    core = (me + 1 - 2 * oc, zi)
    xdev = (me + 2 - 4 * ox, zi)
    ydev = (me + 4 - 8 * oy, zi)
    inner = (zi == 1) | (zi == 2)
    outer = (zi == 0) | (zi == 3)
    to_inner = (me, 1 + lax.div(zi, 2))
    across = (me, 3 - zi)
    to_outer = (me, 3 * lax.div(zi, 2))

    def place(n):
        y = lax.rem(oy + n // 2 % 2, 2)
        x = lax.rem(ox + n % 2, 2)
        return 4 * y + 2 * x + lax.rem(oc + n // 4, 2)

    def turned(src, dst, l):
        return [(src.at[l, place(n)], dst.at[pl.ds(n * R, R)]) for n in range(WAYS)]

    def copies(parts, sem):
        return [pltpu.make_async_copy(a, b, sem.at[k]) for k, (a, b) in enumerate(parts)]

    def ffn_tile(f):
        l = layers - 1 - lax.div(f, n_ffn)
        rb = lax.rem(f, n_ffn)
        s = lax.rem(f, 2)
        span = pl.ds(pl.multiple_of(rb * D, D), D)
        parts = [(w_down.at[l, span], wd.at[s]), (w_up.at[l, :, span], wu.at[s]), (h_gp.at[l, :, span], gp.at[s])]
        parts += [(h_actT.at[l, place(n), rb], actT.at[s, pl.ds(n * R, R)]) for n in range(WAYS)]
        return copies(parts, fsem.at[s])

    def att_tile(a):
        l = layers - 1 - lax.div(a, n_att)
        i = lax.rem(a, n_att)
        s = lax.rem(a, 2)
        parts = [(h_p.at[l, pl.ds(2 * i, 2)], pb.at[s])]
        for k in range(3):
            span = pl.ds(pl.multiple_of(i * 128 + k * D, 128), 128)
            parts.append((w_qkv.at[l, :, span], wq.at[s, :, pl.ds(k * 128, 128)]))
            parts.append((h_qkv.at[l, :, span], qkv.at[s, :, pl.ds(k * 128, 128)]))
        span = pl.ds(pl.multiple_of(i * 128, 128), 128)
        parts += [(h_rl.at[l, :, span], rl.at[s]), (h_pv.at[l, :, span], pv.at[s])]
        return copies(parts, asem.at[s])

    def ffn_layer(l):
        return copies([(h_n2.at[l], n2), (h_r2.at[l], r2)] + turned(h_nrmT, nrmT, l), lsem.at[0])

    def att_layer(l):
        parts = [(h_n1.at[l], n1), (h_r1.at[l], r1), (w_out.at[l], wo)]
        return copies(parts + turned(h_hidT, hidT, l) + turned(h_mixT, mixT, l), lsem.at[1])

    def start(made):
        for c in made:
            c.start()

    def wait(made):
        for c in made:
            c.wait()

    start(ffn_layer(layers - 1))
    for n in range(2):
        start(ffn_tile(jnp.int32(n)))
    start(att_layer(layers - 1))
    for n in range(2):
        start(att_tile(jnp.int32(n)))
    acc[...] = g_in[...]
    vec[...] = jnp.zeros_like(vec)
    greet([core, xdev, ydev] + [(me, lax.rem(zi + k, 4)) for k in range(1, 4)])

    lane = lax.broadcasted_iota(jnp.int32, (T, 128), 1)
    first = lane < HD

    def norm_back(g, n, r, gain):
        e = g * gain
        return r * (e - jnp.mean(e, axis=-1, keepdims=True) - n * jnp.mean(e * n, axis=-1, keepdims=True))

    def col_sum(v):
        return jnp.sum(v.astype(jnp.float32), axis=0, keepdims=True)

    def through_norm(l, base, normal, root, gain, rounded):
        g = acc[...]
        n = normal[...].astype(jnp.float32)
        d = norm_back(g, n, root[:, :1], gain)
        acc[...] = d
        low = d.astype(jnp.bfloat16)
        rounded[...] = low
        for k, v in enumerate((low, g * n, g)):
            vec[l, base + k : base + k + 1, :] = col_sum(v)

    def prologue(l):
        wait(ffn_layer(l))
        through_norm(l, 5 + n_ffn, n2, r2, gain_two[pl.ds(l, 1), :], second)

    def middle(l):
        wait(att_layer(l))
        through_norm(l, 2, n1, r1, gain_one[pl.ds(l, 1), :], branch)
        gm[...] = dot_t(branch[...], wo[...]).astype(jnp.bfloat16)

    def ffn(l, rb, c):
        f = (layers - 1 - l) * n_ffn + rb
        s = lax.rem(f, 2)
        q = rb * group
        wait(ffn_tile(f))
        low = (dot_t(second[...], wd[s]) * gp[s].astype(jnp.float32)).astype(jnp.bfloat16)
        gpre[...] = low
        vec[l, pl.ds(5 + rb, 1), :] = col_sum(low)
        for k, (left, right) in enumerate(((nrmT, gpre), (actT.at[s], second))):
            made = dot(left[...], right[...]).astype(jnp.bfloat16)
            for n in range(group):
                keepq[q + n, k] = made[:U, n * C : (n + 1) * C]
                sendc[c, n, k] = made[U:, n * C : (n + 1) * C]
        acc[...] += dot_t(gpre[...], wu[s])

        @pl.when(f + 2 < layers * n_ffn)
        def _():
            start(ffn_tile(f + 2))

    def attend(l, i, c):
        a = (layers - 1 - l) * n_att + i
        o = pl.multiple_of(i * 128, 128)
        s = lax.rem(a, 2)
        q = n_ffn * group + i
        wait(att_tile(a))
        q2, k2, v2 = (qkv[s, :, k * 128 : (k + 1) * 128] for k in range(3))
        g2 = (gm[:, pl.ds(o, 128)].astype(jnp.float32) * rl[s]).astype(jnp.bfloat16)
        weighed = g2.astype(jnp.float32) * pv[s]
        zero = jnp.zeros_like(q2)
        q2t, g2t = q2.T, g2.T
        dq = None
        dkt, dvt = [], []
        for h in range(2):
            sel = first if h == 0 else ~first
            p = pb[s, h]
            gprob = dot_t(jnp.where(sel, g2, zero), v2)
            centre = jnp.sum(jnp.where(sel, weighed, 0.0), axis=-1, keepdims=True)
            ds = (p.astype(jnp.float32) * (gprob - centre)).astype(jnp.bfloat16)
            part = dot(ds, jnp.where(sel, k2, zero))
            dq = part if h == 0 else dq + part
            dkt.append(dot(q2t[h * HD : (h + 1) * HD], ds))
            dvt.append(dot(g2t[h * HD : (h + 1) * HD], p))
        dq = (dq * 0.125).astype(jnp.bfloat16)
        dk = jnp.concatenate(dkt, axis=0).astype(jnp.bfloat16).T
        dv = jnp.concatenate(dvt, axis=0).astype(jnp.bfloat16).T
        vec[l, 0:1, pl.ds(o, 128)] = col_sum(dq)
        vec[l, 1:2, pl.ds(o, 128)] = col_sum(dv)
        rhs[:, :128] = dq
        rhs[:, 128:256] = dk
        rhs[:, 256:] = dv
        made = dot(hidT[...], rhs[...]).astype(jnp.bfloat16)
        keepq[q, 0] = made[:U, :C]
        sendc[c, 0, 0] = made[U:, :C]
        keepq[q, 1, :, :128] = made[:U, C:]
        sendc[c, 0, 1, :, :128] = made[U:, C:]
        made = dot(mixT[...], branch[:, pl.ds(o, 128)]).astype(jnp.bfloat16)
        keepq[q, 1, :, 128:] = made[:U]
        sendc[c, 0, 1, :, 128:] = made[U:]
        acc[...] += dot_t(rhs[...], wq[s])

        @pl.when(a + 2 < layers * n_att)
        def _():
            start(att_tile(a + 2))

    def core_copy(m, wide):
        c = lax.rem(m, 2)
        k = lax.rem(m, macros)
        q = k * group if wide else n_ffn * group + k - n_ffn
        size = group if wide else 1
        return remote(
            sendc.at[c, pl.ds(0, size)], recvq.at[pl.ds(q, size)], csem.at[0, m], csem.at[1, m], core
        )

    def is_wide(m):
        return lax.rem(m, macros) < n_ffn

    def copies_one(u):
        s = lax.rem(u, SLOTS)
        return [
            remote(s1.at[s, k], t1.at[s, k], xsem.at[0, k, s], xsem.at[1, k, s], (xdev, ydev)[k]) for k in range(2)
        ]

    def copy_two(u, k):
        s = lax.rem(u, SLOTS)
        return remote(s2.at[s, k], t2.at[s, k], ysem.at[0, k, s], ysem.at[1, k, s], (ydev, xdev)[k])

    def copy_in(u, k):
        s = lax.rem(u, SLOTS)
        return remote(za.at[s, k], zr.at[s, k], zsem.at[0, k, s], zsem.at[1, k, s], to_inner)

    def copy_across(u, k):
        s = lax.rem(u, SLOTS)
        return remote(zb.at[s, k], zt.at[s, k], zsem.at[2, k, s], zsem.at[3, k, s], across)

    def copy_out(u, k):
        s = lax.rem(u, SLOTS)
        return remote(zf.at[s, k], out.at[u, k], zsem.at[4, k, s], zsem.at[5, k, s], to_outer)

    def copy_home(u):
        s = lax.rem(u, SLOTS)
        return pltpu.make_async_copy(zf.at[s], out.at[u], osem.at[s])

    def stage_one(u):
        s = lax.rem(u, QUEUE)
        d = lax.rem(u, SLOTS)
        base = lax.div(u, per) * macros

        @pl.when(u == 0)
        def _():
            core_copy(base, True).wait_recv()

        @pl.when(u >= n_units - 2)
        def _():
            core_copy(base + n_ffn + s - n_ffn * group, False).wait_recv()

        for k in range(2):
            sent, kept = ((1, 3), (0, 2)) if k == 0 else ((2, 3), (0, 1))
            for n, (a, b) in enumerate(zip(sent, kept)):
                to = pl.ds(n * R, R)
                s1[d, k, to] = low_sum(keepq[s, k, pl.ds(a * R, R)], recvq[s, k, pl.ds(a * R, R)])
                k1[d, k, to] = low_sum(keepq[s, k, pl.ds(b * R, R)], recvq[s, k, pl.ds(b * R, R)])
        start(copies_one(u))

    def stage_two(u):
        d = lax.rem(u, SLOTS)
        wait(copies_one(u))
        for k in range(2):
            s2[d, k] = low_sum(k1[d, k, pl.ds(R, R)], t1[d, k, pl.ds(R, R)])
            k2[d, k] = low_sum(k1[d, k, pl.ds(0, R)], t1[d, k, pl.ds(0, R)])
        start([copy_two(u, k) for k in range(2)])

    def stage_three(u):
        d = lax.rem(u, SLOTS)
        for k in range(2):
            copy_two(u, k).wait()
            za[d, k] = low_sum(k2[d, k], t2[d, k])

            @pl.when(outer)
            def _(k=k):
                copy_in(u, k).start()

    def stage_four(u):
        d = lax.rem(u, SLOTS)

        @pl.when(outer)
        def _():
            for k in range(2):
                copy_in(u, k).wait_send()

        @pl.when(inner)
        def _():
            for k in range(2):
                copy_in(u, k).wait_recv()
                zb[d, k] = low_sum(za[d, k], zr[d, k])
                copy_across(u, k).start()

    def stage_five(u):
        d = lax.rem(u, SLOTS)

        @pl.when(inner)
        def _():
            for k in range(2):
                copy_across(u, k).wait()
                zf[d, k] = low_sum(zb[d, k], zt[d, k])
                copy_out(u, k).start()
            copy_home(u).start()

    def stage_six(u):
        @pl.when(inner)
        def _():
            for k in range(2):
                copy_out(u, k).wait_send()
            copy_home(u).wait()

        @pl.when(outer)
        def _():
            for k in range(2):
                copy_out(u, k).wait_recv()

    stages = (None, stage_one, stage_two, stage_three, stage_four, stage_five, stage_six)

    def run_stage(i, k):
        u = i - LAGS[k]

        @pl.when((u >= 0) & (u < n_units))
        def _():
            stages[k](u)

    def vec_copy(k):
        where = (core, xdev, ydev, to_inner, across, to_outer)[k]
        return remote(vec, vrecv.at[k], vsem.at[0, k], vsem.at[1, k], where)

    def vec_step(k):
        if 1 <= k <= 3:
            vec_copy(k - 1).wait()
            vec[...] += vrecv[k - 1]
        if k < 3:
            vec_copy(k).start()
        if k == 3:

            @pl.when(outer)
            def _():
                vec_copy(3).start()

        if k == 4:

            @pl.when(outer)
            def _():
                vec_copy(3).wait_send()

            @pl.when(inner)
            def _():
                vec_copy(3).wait_recv()
                vec[...] += vrecv[3]
                vec_copy(4).start()

        if k == 5:

            @pl.when(inner)
            def _():
                vec_copy(4).wait()
                vec[...] += vrecv[4]
                vec_copy(5).start()

        if k == 6:

            @pl.when(inner)
            def _():
                vec_copy(5).wait_send()
                vec_out[...] = vec[...]

            @pl.when(outer)
            def _():
                vec_copy(5).wait_recv()
                vec_out[...] = vrecv[5]

    part = T // 4
    slab = part // GT_PARTS

    def gt_own():
        own = pl.ds(pl.multiple_of(zi * part, part), part)
        return pltpu.make_async_copy(gb.at[own], gt_out.at[zi], gsem.at[0, 3 * GT_PARTS])

    def gt_copy(n):
        peer = lax.rem(zi + 1 + lax.rem(n, 3), 4)
        o = lax.div(n, 3) * slab
        src = gb.at[pl.ds(pl.multiple_of(peer * part + o, slab), slab)]
        dst = gt_out.at[zi, pl.ds(pl.multiple_of(o, slab), slab)]
        return remote(src, dst, gsem.at[0, n], gsem.at[1, n], (me, peer))

    def done_by(i):
        num, den = PACE
        return jnp.minimum(lax.div(num * (i + 1) + den - 1, den), n_macros)

    last = 0
    while -(-PACE[0] * (last + 1) // PACE[1]) < n_macros:
        last += 1

    def step(i, carry):
        for k in range(6, 1, -1):
            run_stage(i, k)
        run_stage(i, 1)
        m = done_by(i - 1)
        l = layers - 1 - lax.div(m, macros)
        k = lax.rem(m, macros)
        c = lax.rem(m, 2)
        busy = done_by(i) > m

        @pl.when(busy & (m >= 2) & is_wide(m - 2))
        def _():
            core_copy(m - 2, True).wait_send()

        @pl.when(busy & (m >= 3) & is_wide(m - 2))
        def _():
            core_copy(m - 2, True).wait_recv()

        @pl.when(busy & (m >= 2) & ~is_wide(m - 2))
        def _():
            core_copy(m - 2, False).wait()

        @pl.when(busy & (k == 0))
        def _():
            prologue(l)

        @pl.when(busy & (k == 0) & (l < layers - 1))
        def _():
            start(att_layer(l))

        @pl.when(busy & (k < n_ffn))
        def _():
            ffn(l, k, c)
            core_copy(m, True).start()

        @pl.when(busy & (k == n_ffn) & (l > 0))
        def _():
            start(ffn_layer(l - 1))

        @pl.when(busy & (k == n_ffn))
        def _():
            middle(l)

        @pl.when(busy & (k >= n_ffn))
        def _():
            attend(l, k - n_ffn, c)
            core_copy(m, False).start()

        @pl.when(i == last + 1)
        def _():
            gb[...] = acc[...].astype(jnp.bfloat16)
            gt_own().start()

        @pl.when((i > last) & (i <= last + 3 * GT_PARTS))
        def _():
            gt_copy(i - last - 1).start()

        for n in range(7):

            @pl.when(i == last + 1 + 2 * n)
            def _(n=n):
                vec_step(n)

        return carry

    lax.fori_loop(0, n_units + LAGS[6], step, 0)
    for m in (n_macros - 2, n_macros - 1):
        core_copy(jnp.int32(m), False).wait_send()
    gt_own().wait()

    def gt_wait(n, c):
        gt_copy(n).wait()
        return c

    lax.fori_loop(0, 3 * GT_PARTS, gt_wait, 0)


def backward(grad_hidden, res, w):
    T, D = grad_hidden.shape
    L = w["w_qkv"].shape[0]
    FF = w["w_up"].shape[2]
    bf, f32 = jnp.bfloat16, jnp.float32
    S = jax.ShapeDtypeStruct
    V = pltpu.VMEM
    vm = pl.BlockSpec(memory_space=V)
    anyspec = pl.BlockSpec(memory_space=pl.ANY)
    R = D // WAYS
    U = 4 * R
    group = D // C
    n_units = L * (FF // C + D // 128)
    n_macros = L * (FF // D + D // 128)
    dma = pltpu.SemaphoreType.DMA
    scratch = [
        V((2, D, D), bf), V((2, D, D), bf), V((2, T, D), bf), V((2, D, T), bf),
        V((2, D, 384), bf), V((2, T, 384), bf), V((2, 2, T, T), bf), V((2, T, 128), f32), V((2, T, 128), f32),
        V((D, D), bf), V((D, T), bf), V((D, T), bf), V((D, T), bf),
        V((T, D), bf), V((T, 128), f32), V((T, D), bf), V((T, 128), f32),
        V((T, D), f32), V((T, D), bf), V((T, D), bf), V((T, D), bf), V((T, D), bf), V((T, 384), bf),
        V((L, VEC_ROWS, D), f32), V((6, L, VEC_ROWS, D), f32), V((T, D), bf),
        V((2, group, 2, U, C), bf), V((QUEUE, 2, U, C), bf), V((QUEUE, 2, U, C), bf),
        V((SLOTS, 2, 2 * R, C), bf), V((SLOTS, 2, 2 * R, C), bf), V((SLOTS, 2, 2 * R, C), bf),
        V((SLOTS, 2, R, C), bf), V((SLOTS, 2, R, C), bf), V((SLOTS, 2, R, C), bf),
        V((SLOTS, 2, R, C), bf), V((SLOTS, 2, R, C), bf), V((SLOTS, 2, R, C), bf),
        V((SLOTS, 2, R, C), bf), V((SLOTS, 2, R, C), bf),
        dma((2, 3 + WAYS)), dma((2, 9)), dma((2, 3 + 2 * WAYS)), dma((2, n_macros)), dma((2, 2, SLOTS)), dma((2, 2, SLOTS)),
        dma((6, 2, SLOTS)), dma((SLOTS,)), dma((2, 6)), dma((2, 3 * GT_PARTS + 1)),
    ]
    return pl.pallas_call(
        functools.partial(bwd_kernel, L),
        out_shape=(
            S((n_units, 2, R, C), bf), S((4, T // 4, D), bf), S((L, VEC_ROWS, D), f32),
        ),
        in_specs=[vm] * 3 + [anyspec] * 17,
        out_specs=(anyspec, anyspec, vm),
        scratch_shapes=scratch,
        compiler_params=pltpu.CompilerParams(
            vmem_limit_bytes=60 * 1024 * 1024, collective_id=0, has_side_effects=True
        ),
        name="backward",
    )(
        grad_hidden, w["gain_one"], w["gain_two"],
        *(w[k] for k in ("w_qkv", "w_out", "w_up", "w_down")),
        *res,
    )


def finish_kernel(units, gt, vec, g_tok, g_qkv, g_out, g_up, g_down, *vectors):
    l = pl.program_id(0)
    R, D = g_out.shape[1:]
    n_ffn = g_up.shape[2] // D
    group = D // C
    g_tok[...] = gt[...].astype(jnp.float32)

    def read(n, k, cols=slice(None)):
        return units[0, n, k, :, cols].astype(jnp.float32)

    for rb in range(n_ffn):
        for n in range(group):
            u = rb * group + n
            g_up[0, :, u * C : (u + 1) * C] = read(u, 0)
            g_down[0, rb * R : (rb + 1) * R, n * C : (n + 1) * C] = read(u, 1)
    for i in range(D // 128):
        u = n_ffn * group + i
        for k in range(3):
            half = slice(k % 2 * 128, k % 2 * 128 + 128)
            g_qkv[0, :, k * D + i * 128 : k * D + (i + 1) * 128] = read(u, k // 2, half)
        g_out[0, :, i * 128 : (i + 1) * 128] = read(u, 1, slice(128, 256))
    row = 0
    for ref in vectors:
        for k in range(ref.shape[1] // D):
            ref[pl.ds(l, 1), k * D : (k + 1) * D] = vec[0, row : row + 1, :]
            row += 1


def finish(units, grad_tokens, vec, layers, hidden_units):
    n_units, _, R, _ = units.shape
    parts, piece, D = grad_tokens.shape
    L, FF = layers, hidden_units
    f32 = jnp.float32
    S = jax.ShapeDtypeStruct
    per = n_units // L
    widths = (D, D, D, D, D, FF, D, D, D)
    return pl.pallas_call(
        finish_kernel,
        grid=(L,),
        out_shape=(
            S((parts, piece, D), f32), S((L, R, 3 * D), f32), S((L, R, D), f32), S((L, R, FF), f32),
            S((L, FF // WAYS, D), f32),
        ) + tuple(S((L, width), f32) for width in widths),
        in_specs=[
            pl.BlockSpec((1, per, 2, R, C), lambda l: (L - 1 - l, 0, 0, 0, 0)),
            pl.BlockSpec((parts // L, piece, D), lambda l: (l, 0, 0)),
            pl.BlockSpec((1, VEC_ROWS, D), lambda l: (l, 0, 0)),
        ],
        out_specs=(
            pl.BlockSpec((parts // L, piece, D), lambda l: (l, 0, 0)),
            pl.BlockSpec((1, R, 3 * D), lambda l: (l, 0, 0)),
            pl.BlockSpec((1, R, D), lambda l: (l, 0, 0)),
            pl.BlockSpec((1, R, FF), lambda l: (l, 0, 0)),
            pl.BlockSpec((1, FF // WAYS, D), lambda l: (l, 0, 0)),
        ) + tuple(pl.BlockSpec((L, width), lambda l: (0, 0)) for width in widths),
        compiler_params=pltpu.CompilerParams(vmem_limit_bytes=60 * 1024 * 1024),
        name="finish",
    )(units.reshape(L, per, 2, R, C), grad_tokens, vec)


NAMES = (
    "w_qkv",
    "b_query",
    "b_value",
    "w_out",
    "b_out",
    "gain_one",
    "shift_one",
    "w_up",
    "b_up",
    "w_down",
    "b_down",
    "gain_two",
    "shift_two",
)


def by_class(array, block, ways):
    layers, rows, tokens_here = array.shape
    if ways == 1:
        return array.reshape(layers, WAYS, -1, tokens_here)
    array = array.reshape(layers, ways, WAYS, block, tokens_here)
    return jnp.swapaxes(array, 1, 2).reshape(layers, WAYS, -1, tokens_here)


def on_device(dp_count, tokens, segment_ids, pair_ids, *weights):
    w = dict(zip(NAMES, weights))
    layer_count, model_width, _ = w["w_qkv"].shape
    hidden_units = w["w_up"].shape[2]
    ways = dp_count // WAYS
    grad_hidden, loss_value, *res = forward(tokens, segment_ids, pair_ids, w)
    for place in (4, 5, 6):
        res[place] = by_class(res[place], model_width // dp_count, ways)
    block = model_width // WAYS
    acts = by_class(res[7], hidden_units // dp_count, ways)
    res[7] = acts.reshape(layer_count, WAYS, -1, block, acts.shape[-1])
    units, grad_tokens, vec = backward(grad_hidden, res, w)
    if ways > 1:
        groups = [[low + WAYS * high for high in range(ways)] for low in range(WAYS)]
        vec = lax.psum(vec, "dp", axis_index_groups=groups)
    grad_tokens, *rest = finish(units, grad_tokens, vec, layer_count, hidden_units)
    matrices, vectors = rest[:4], rest[4:]
    if ways > 1:
        matrices = [
            lax.psum_scatter(
                matrix, "dp", scatter_dimension=1, axis_index_groups=groups, tiled=True
            )
            for matrix in matrices
        ]
    g_qkv, g_out, g_up, g_down = matrices
    return (
        loss_value.reshape(1),
        grad_tokens,
        g_qkv,
        vectors[0],
        vectors[1],
        g_out,
        vectors[2],
        vectors[3],
        vectors[4],
        g_up,
        vectors[5],
        g_down,
        vectors[6],
        vectors[7],
        vectors[8],
    )


def solution(mesh):
    return jax.shard_map(
        functools.partial(on_device, mesh.shape["dp"]),
        mesh=mesh,
        in_specs=(P("dp", "seq", None), P("dp", "seq"), P("dp")) + (P(),) * 13,
        out_specs=(
            P("dp"),
            P("dp", "seq", None),
            P(None, "dp", None),
            P(),
            P(),
            P(None, "dp", None),
            P(),
            P(),
            P(),
            P(None, "dp", None),
            P(),
            P(None, "dp", None),
            P(),
            P(),
            P(),
        ),
        check_vma=False,
    )
```

```python
import functools

import jax
import jax.numpy as jnp
from jax import lax
from jax.experimental import pallas as pl
from jax.experimental.pallas import tpu as pltpu
from jax.sharding import PartitionSpec as P

MESH = pl.DeviceIdType.MESH
LOSS_SCALE = 1024.0
NORM_EPS = 1e-06
HD = 64
WIDE = 768
C = 256
WAYS = 8
QUEUE = 18
SLOTS_ONE = 7
SLOTS = 6
LAGS = (0, 1, 4, 6, 8, 10, 12)
PACE = (5, 6)
GT_PARTS = 4
EARLY = 2
VEC_ROWS = 16


def dot(left, right):
    return lax.dot_general(
        left,
        right,
        (((1,), (0,)), ((), ())),
        preferred_element_type=jnp.float32,
    )


def dot_t(left, right):
    return lax.dot_general(
        left,
        right,
        (((1,), (1,)), ((), ())),
        preferred_element_type=jnp.float32,
    )


def split(values):
    high = values.astype(jnp.bfloat16)
    return high, (values - high.astype(jnp.float32)).astype(jnp.bfloat16)


def remote(src, dst, send_sem, recv_sem, where):
    return pltpu.make_async_remote_copy(
        src_ref=src,
        dst_ref=dst,
        send_sem=send_sem,
        recv_sem=recv_sem,
        device_id=where,
        device_id_type=MESH,
    )


def greet(peers):
    barrier = pltpu.get_barrier_semaphore()
    for peer in peers:
        pl.semaphore_signal(barrier, inc=1, device_id=peer, device_id_type=MESH)


def await_greetings(peers):
    pl.semaphore_wait(pltpu.get_barrier_semaphore(), len(peers))


def gelu_pair(x):
    t = 1.0 / (1.0 + 0.23164190 * jnp.abs(x))
    gauss = jnp.exp(-0.5 * x * x)
    poly = t * (
        0.127414796
        + t * (-0.142248368 + t * (0.7107068705 + t * (-0.7265760135 + t * 0.5307027145)))
    )
    tail = poly * gauss
    phi = jnp.where(x >= 0.0, 1.0 - tail, tail)
    return x * phi, phi + x * (gauss * 0.3989422804014327)


def norm(x, gain, shift):
    centre = x - jnp.mean(x, axis=-1, keepdims=True)
    scaled = lax.rsqrt(jnp.mean(centre * centre, axis=-1, keepdims=True) + NORM_EPS)
    normal = centre * scaled
    return normal * gain + shift, normal, scaled


def fwd_kernel(
    layers, segs,
    tok, ids, pair, b_query, b_value, b_out, gain_one, shift_one, b_up, b_down, gain_two, shift_two,
    w_qkv, w_out, w_up, w_down,
    grad_out, loss_out, o_qkv, o_p, o_rl, o_pv, o_hidT, o_mixT, o_nrmT, o_actT, o_gp, o_n1, o_r1, o_n2, o_r2,
    wq, wo, wu, wd, bias, hid, low, idbuf, qkv, pb, rl, pv, mix, nrm, gp, n1, r1, n2, r2,
    hidT, mixT, nrmT, actT, acc, ubuf, gbuf, prow,
    wsem, osem, tsem, usem,
):
    T, D = hid.shape
    FF = w_up.shape[2]
    piece = tok.shape[1]
    parts = T // piece
    me = lax.axis_index("dp")
    zi = lax.axis_index("seq")
    pairs = ((w_qkv, wq), (w_out, wo), (w_up, wu), (w_down, wd))

    def wcopy(l, i):
        return pltpu.make_async_copy(pairs[i][0].at[l], pairs[i][1], wsem.at[i])

    def peer(k):
        return lax.rem(zi + k, parts)

    mine = pl.ds(pl.multiple_of(zi * piece, piece), piece)

    def tcopy(k, n):
        src, dst = ((tok, low.at[mine]), (ids, idbuf.at[zi]))[n]
        if k == 0:
            return pltpu.make_async_copy(src.at[zi], dst, tsem.at[n, 0, 0])
        return remote(src.at[peer(k)], dst, tsem.at[n, 0, k], tsem.at[n, 1, k], (me, peer(k)))

    peers = [(me, peer(k)) for k in range(1, parts)]
    greet(peers)
    await_greetings(peers)
    for k in (2, 1, 3, 0):
        for n in (1, 0):
            tcopy(k, n).start()
    for i in range(4):
        wcopy(0, i).start()

    def refill(l, *which):
        @pl.when(l + 1 < layers)
        def _():
            for i in which:
                wcopy(l + 1, i).start()

    lane = lax.broadcasted_iota(jnp.int32, (T, 128), 1)
    first = lane < HD

    homes = (
        (qkv, o_qkv), (hidT, o_hidT), (rl, o_rl), (pv, o_pv), (mixT, o_mixT), (n1, o_n1), (r1, o_r1),
        (nrmT, o_nrmT), (gp, o_gp), (actT, o_actT), (n2, o_n2), (r2, o_r2), (pb, o_p),
    )

    def home(l, k):
        return pltpu.make_async_copy(homes[k][0], homes[k][1].at[l], osem.at[k])

    def ship(l, *keys):
        for k in keys:
            home(l, k).start()

    def claim(l, *keys):
        @pl.when(l > 0)
        def _():
            for k in keys:
                home(l - 1, k).wait()

    for k in range(parts):
        tcopy(k, 1).wait()
    id_rows = [idbuf[k] for k in range(parts)]
    id_cols = jnp.concatenate(
        id_rows + [jnp.zeros((8 - parts, piece), jnp.int32)], axis=0
    ).astype(jnp.float32).T
    for i in range(parts):
        for j in range(parts):
            same = id_cols[:, i : i + 1] == id_rows[j].astype(jnp.float32)
            bias[i * piece : (i + 1) * piece, j * piece : (j + 1) * piece] = jnp.where(same, 0.0, -1e30)
    for k in (0, 1, 3, 2):
        tcopy(k, 0).wait()
        source = pl.ds(pl.multiple_of(lax.rem(zi + parts - k, parts) * piece, piece), piece)
        arrived = low[source, :]
        hid[source, :] = arrived.astype(jnp.float32)
        hidT[:, source] = arrived.T

    def layer(l, carry):
        row = pl.ds(l, 1)
        wcopy(l, 0).wait()
        y = dot(low[...], wq[...])
        refill(l, 0)
        claim(l, 0)
        qkv[:, :D] = ((y[:, :D] + b_query[row, :]) * 0.125).astype(jnp.bfloat16)
        qkv[:, D : 2 * D] = y[:, D : 2 * D].astype(jnp.bfloat16)
        qkv[:, 2 * D :] = (y[:, 2 * D :] + b_value[row, :]).astype(jnp.bfloat16)
        ship(l, 0)
        ship(l, 1)

        def scores(n):
            o = n // 2 * 128
            q2 = qkv[:, o : o + 128]
            sel = first if n % 2 == 0 else ~first
            return dot_t(jnp.where(sel, q2, jnp.zeros_like(q2)), qkv[:, D + o : D + o + 128]) + bias[...]

        claim(l, 2, 3, 4, 12)
        made = {0: scores(0)}
        for n in range(D // HD):
            if n + 1 < D // HD:
                made[n + 1] = scores(n + 1)
            cols = slice(n // 2 * 128, n // 2 * 128 + 128)
            v2 = qkv[:, 2 * D + cols.start : 2 * D + cols.stop]
            sel = first if n % 2 == 0 else ~first
            sc = made.pop(n)
            e = jnp.exp(sc - jnp.max(sc, axis=-1, keepdims=True))
            recip = 1.0 / jnp.sum(e, axis=-1, keepdims=True)
            p = e.astype(jnp.bfloat16)
            pb[n] = p
            part = dot(p, jnp.where(sel, v2, jnp.zeros_like(v2))) * recip
            if n % 2 == 0:
                total, before = part, recip
                continue
            total = total + part
            rl[:, cols] = jnp.where(first, before, recip)
            pv[:, cols] = total
            low_total = total.astype(jnp.bfloat16)
            mix[:, cols] = low_total
            mixT[cols, :] = low_total.T
        ship(l, 12)
        ship(l, 2)
        ship(l, 3)
        wcopy(l, 1).wait()
        acc[...] = dot(mix[...], wo[...])
        refill(l, 1)
        ship(l, 4)

        claim(l, 5, 6, 7)
        x = hid[...] + acc[...] + b_out[row, :]
        y, n, r = norm(x, gain_one[row, :], shift_one[row, :])
        nrm[...] = y
        rounded = y.astype(jnp.bfloat16)
        low[...] = rounded
        nrmT[...] = rounded.T
        n1[...] = n.astype(jnp.bfloat16)
        r1[...] = jnp.broadcast_to(r, (T, 128))
        ship(l, 5)
        ship(l, 6)
        ship(l, 7)
        wcopy(l, 2).wait()
        wcopy(l, 3).wait()
        acc[...] = nrm[...]
        claim(l, 8, 9)

        def raised(j):
            cols = slice(j * WIDE, (j + 1) * WIDE)
            return dot(low[...], wu[:, cols]) + b_up[row, cols]

        made = {0: raised(0)}
        for j in range(FF // WIDE):
            cols = slice(j * WIDE, (j + 1) * WIDE)
            if j + 1 < FF // WIDE:
                made[j + 1] = raised(j + 1)
            a, g = gelu_pair(made.pop(j))
            al = a.astype(jnp.bfloat16)
            gp[:, cols] = g.astype(jnp.bfloat16)
            actT[cols, :] = al.T
            acc[...] += dot(al, wd[cols, :])
        refill(l, 2, 3)
        ship(l, 8)
        ship(l, 9)

        claim(l, 10, 11)
        home(l, 1).wait()
        x = acc[...] + b_down[row, :]
        y, n, r = norm(x, gain_two[row, :], shift_two[row, :])
        hid[...] = y

        @pl.when(l + 1 < layers)
        def _():
            rounded = hid[...].astype(jnp.bfloat16)
            low[...] = rounded
            hidT[...] = rounded.T

        n2[...] = n.astype(jnp.bfloat16)
        r2[...] = jnp.broadcast_to(r, (T, 128))
        ship(l, 10)
        ship(l, 11)
        return carry

    lax.fori_loop(0, layers, layer, 0)

    count = parts * segs
    member_t = jnp.concatenate(
        [
            (lax.broadcasted_iota(jnp.int32, (segs, piece), 0) == row).astype(jnp.float32)
            for row in id_rows
        ],
        axis=1,
    )
    sizes = jnp.sum(member_t, axis=-1, keepdims=True)
    member_t = member_t.astype(jnp.bfloat16)
    high, rest = split(hid[...])
    embed = (dot(member_t, high) + dot(member_t, rest)) / sizes
    scale = lax.rsqrt(jnp.sum(embed * embed, axis=-1, keepdims=True) + NORM_EPS)
    unit = embed * scale
    ubuf[...] = jnp.zeros_like(ubuf)
    gbuf[zi] = unit

    def ucopy(k):
        return remote(gbuf.at[zi], gbuf.at[zi], usem.at[0, k], usem.at[1, k], (me, peer(k)))

    for k in range(1, parts):
        ucopy(k).start()
    prow[...] = jnp.zeros_like(prow)
    prow[:1, :count] = pair[...].astype(jnp.float32)
    partner = prow[...].T[:, :1]
    side = ubuf.shape[0]
    row_no = lax.broadcasted_iota(jnp.int32, (side, side), 0)
    col_no = lax.broadcasted_iota(jnp.int32, (side, side), 1)
    live = (row_no < count) & (col_no < count)
    chosen = jnp.where(live & (partner == col_no.astype(jnp.float32)), 1.0, 0.0)
    for k in range(1, parts):
        ucopy(k).wait()
    for k in range(parts):
        ubuf[k * segs : (k + 1) * segs, :] = gbuf[k]
    high, rest = split(ubuf[...])
    logits = 20.0 * (dot_t(high, high) + dot_t(high, rest) + dot_t(rest, high))
    logits = jnp.where(live, logits, -1e30)
    top = jnp.max(logits, axis=-1, keepdims=True)
    grown = jnp.exp(logits - top)
    total = jnp.sum(grown, axis=-1, keepdims=True)
    pull = jnp.where(live, (grown / total - chosen) * (20.0 * LOSS_SCALE / count), 0.0)
    acc[:side, :side] = pull + pull.T
    own = pl.ds(pl.multiple_of(zi * segs, segs), segs)
    ours, ours_rest = split(acc[own, :side])
    grad_unit = dot(ours, high) + dot(ours, rest) + dot(ours_rest, high)
    inner = jnp.sum(grad_unit * unit, axis=-1, keepdims=True)
    grad_sums = scale * (grad_unit - unit * inner) / sizes
    high, rest = split(grad_sums)
    both = jnp.concatenate([grad_sums, grad_sums - high.astype(jnp.float32)], axis=0).astype(jnp.bfloat16)
    lanes = lax.broadcasted_iota(jnp.int32, (piece, 2 * segs), 1)
    lanes = jnp.where(lanes < segs, lanes, lanes - segs).astype(jnp.float32)
    for i in range(parts):
        member = (lanes == id_cols[:, i : i + 1]).astype(jnp.bfloat16)
        grad_out[i * piece : (i + 1) * piece, :] = dot(member, both)
    picked = jnp.sum(chosen * logits, axis=-1, keepdims=True)
    losses = jnp.where(row_no[:, :1] < count, top + jnp.log(total) - picked, 0.0)
    loss_out[...] = jnp.sum(losses, axis=0, keepdims=True) / count
    for k in range(len(homes)):
        if k != 1:
            home(layers - 1, k).wait()


def forward(tokens, segment_ids, pair_ids, w):
    parts, piece, D = tokens.shape
    T = parts * piece
    L = w["w_qkv"].shape[0]
    FF = w["w_up"].shape[2]
    segs = pair_ids.shape[0] // parts
    side = 128
    bf, f32 = jnp.bfloat16, jnp.float32
    S = jax.ShapeDtypeStruct
    V = pltpu.VMEM
    vm = pl.BlockSpec(memory_space=V)
    anyspec = pl.BlockSpec(memory_space=pl.ANY)
    H = D // HD
    dma = pltpu.SemaphoreType.DMA
    out_shape = (
        S((T, D), f32), S((1, 1), f32), S((L, T, 3 * D), bf), S((L, H, T, T), bf), S((L, T, D), f32), S((L, T, D), f32),
        S((L, D, T), bf), S((L, D, T), bf), S((L, D, T), bf), S((L, FF, T), bf), S((L, T, FF), bf),
        S((L, T, D), bf), S((L, T, 128), f32), S((L, T, D), bf), S((L, T, 128), f32),
    )
    scratch = [
        V((D, 3 * D), bf), V((D, D), bf), V((D, FF), bf), V((FF, D), bf),
        V((T, T), f32), V((T, D), f32), V((T, D), bf), V((parts, 1, piece), jnp.int32),
        V((T, 3 * D), bf), V((H, T, T), bf), V((T, D), f32), V((T, D), f32), V((T, D), bf), V((T, D), f32), V((T, FF), bf),
        V((T, D), bf), V((T, 128), f32), V((T, D), bf), V((T, 128), f32),
        V((D, T), bf), V((D, T), bf), V((D, T), bf), V((FF, T), bf), V((T, D), f32),
        V((side, D), f32), V((parts, segs, D), f32), V((8, side), f32),
        dma((4,)), dma((13,)), dma((2, 2, parts)), dma((2, parts)),
    ]
    return pl.pallas_call(
        functools.partial(fwd_kernel, L, segs),
        out_shape=out_shape,
        in_specs=[anyspec] * 2 + [vm] * 10 + [anyspec] * 4,
        out_specs=(vm, vm) + (anyspec,) * 13,
        scratch_shapes=scratch,
        compiler_params=pltpu.CompilerParams(
            vmem_limit_bytes=60 * 1024 * 1024, collective_id=1, has_side_effects=True
        ),
        name="forward",
    )(
        tokens, segment_ids.reshape(parts, 1, piece), pair_ids.reshape(1, -1),
        *(w[k] for k in ("b_query", "b_value", "b_out", "gain_one", "shift_one", "b_up", "b_down", "gain_two", "shift_two")),
        *(w[k] for k in ("w_qkv", "w_out", "w_up", "w_down")),
    )


def low_sum(one, other):
    return one + other


def bwd_kernel(
    layers, g_in, gain_one, gain_two,
    w_qkv, w_out, w_up, w_down,
    h_qkv, h_p, h_rl, h_pv, h_hidT, h_mixT, h_nrmT, h_actT, h_gp, h_n1, h_r1, h_n2, h_r2,
    out, gt_out, vec_out,
    wd, wu, gp, actT, wq, qkv, pb, rl, pv, wo, hidT, mixT, nrmT, n1, r1, n2, r2,
    acc, second, gm, rhs, vec, vlow, vrecv,
    sendc, keepq, recvq, s1, k1, t1, s2, k2, t2, za, zr, zb, zt, zf,
    zq, zin, e1, h1, f1, e2, h2, f2, ef, qsem, esem, gather,
    fsem, asem, lsem, csem, dsem, xsem, ysem, zsem, osem, vsem, gsem,
):
    T, D = g_in.shape
    FF = w_up.shape[2]
    R = D // WAYS
    U = 4 * R
    n_ffn = FF // D
    n_att = D // 128
    group = D // C
    macros = n_ffn + n_att
    per = n_ffn * group + n_att
    n_units = layers * per
    n_main = n_units - EARLY
    n_macros = layers * macros

    me = lax.axis_index("dp")
    zi = lax.axis_index("seq")
    oc = lax.rem(me, 2)
    ox = lax.rem(lax.div(me, 2), 2)
    oy = lax.rem(lax.div(me, 4), 2)
    core = (me + 1 - 2 * oc, zi)
    xdev = (me + 2 - 4 * ox, zi)
    ydev = (me + 4 - 8 * oy, zi)
    inner = (zi == 1) | (zi == 2)
    outer = (zi == 0) | (zi == 3)
    to_inner = (me, 1 + lax.div(zi, 2))
    across = (me, 3 - zi)
    to_outer = (me, 3 * lax.div(zi, 2))

    def place(n):
        y = lax.rem(oy + n // 2 % 2, 2)
        x = lax.rem(ox + n % 2, 2)
        return 4 * y + 2 * x + lax.rem(oc + n // 4, 2)

    def turned(src, dst, l):
        return [(src.at[l, place(n)], dst.at[pl.ds(n * R, R)]) for n in range(WAYS)]

    def copies(parts, sem):
        return [pltpu.make_async_copy(a, b, sem.at[k]) for k, (a, b) in enumerate(parts)]

    def ffn_tile(f):
        l = layers - 1 - lax.div(f, n_ffn)
        rb = lax.rem(f, n_ffn)
        s = lax.rem(f, 2)
        span = pl.ds(pl.multiple_of(rb * D, D), D)
        parts = [(w_down.at[l, span], wd.at[s]), (w_up.at[l, :, span], wu.at[s]), (h_gp.at[l, :, span], gp.at[s])]
        parts += [(h_actT.at[l, place(n), rb], actT.at[s, pl.ds(n * R, R)]) for n in range(WAYS)]
        return copies(parts, fsem.at[s])

    def att_tile(a):
        l = layers - 1 - lax.div(a, n_att)
        i = lax.rem(a, n_att)
        s = lax.rem(a, 2)
        parts = [(h_p.at[l, pl.ds(2 * i, 2)], pb.at[s])]
        for k in range(3):
            span = pl.ds(pl.multiple_of(i * 128 + k * D, 128), 128)
            parts.append((w_qkv.at[l, :, span], wq.at[s, :, pl.ds(k * 128, 128)]))
            parts.append((h_qkv.at[l, :, span], qkv.at[s, :, pl.ds(k * 128, 128)]))
        span = pl.ds(pl.multiple_of(i * 128, 128), 128)
        parts += [(h_rl.at[l, :, span], rl.at[s]), (h_pv.at[l, :, span], pv.at[s])]
        return copies(parts, asem.at[s])

    def ffn_layer(l):
        return copies([(h_n2.at[l], n2), (h_r2.at[l], r2)] + turned(h_nrmT, nrmT, l), lsem.at[0])

    def att_layer(l):
        parts = [(h_n1.at[l], n1), (h_r1.at[l], r1), (w_out.at[l], wo)]
        return copies(parts + turned(h_hidT, hidT, l) + turned(h_mixT, mixT, l), lsem.at[1])

    peers = [core, xdev, ydev] + [(me, lax.rem(zi + k, 4)) for k in range(1, 4)]
    greet(peers)

    def start(made):
        for c in made:
            c.start()

    def wait(made):
        for c in made:
            c.wait()

    start(ffn_layer(layers - 1))
    for n in range(2):
        start(ffn_tile(jnp.int32(n)))
    start(att_layer(layers - 1))
    for n in range(2):
        start(att_tile(jnp.int32(n)))
    acc[...] = g_in[...]
    vec[...] = jnp.zeros_like(vec)

    lane = lax.broadcasted_iota(jnp.int32, (T, 128), 1)
    first = lane < HD

    def norm_back(g, n, r, gain):
        e = g * gain
        return r * (e - jnp.mean(e, axis=-1, keepdims=True) - n * jnp.mean(e * n, axis=-1, keepdims=True))

    def col_sum(v):
        return jnp.sum(v.astype(jnp.float32), axis=0, keepdims=True)

    branch, gpre = second, gm

    def through_norm(l, base, normal, root, gain, rounded):
        g = acc[...]
        n = normal[...].astype(jnp.float32)
        d = norm_back(g, n, root[:, :1], gain)
        acc[...] = d
        low = d.astype(jnp.bfloat16)
        rounded[...] = low
        for k, v in enumerate((low, g * n, g)):
            vec[l, base + k : base + k + 1, :] = col_sum(v)

    def prologue(l):
        wait(ffn_layer(l))
        through_norm(l, 5 + n_ffn, n2, r2, gain_two[pl.ds(l, 1), :], second)

    def middle(l):
        wait(att_layer(l))
        through_norm(l, 2, n1, r1, gain_one[pl.ds(l, 1), :], branch)
        gm[...] = dot_t(branch[...], wo[...]).astype(jnp.bfloat16)

    def ffn(l, rb, c, send=None):
        f = (layers - 1 - l) * n_ffn + rb
        s = lax.rem(f, 2)
        q = rb * group
        wait(ffn_tile(f))
        low = (dot_t(second[...], wd[s]) * gp[s].astype(jnp.float32)).astype(jnp.bfloat16)
        gpre[...] = low
        vec[l, pl.ds(5 + rb, 1), :] = col_sum(low)
        for k, (left, right) in enumerate(((nrmT, gpre), (actT.at[s], second))):
            made = dot(left[...], right[...]).astype(jnp.bfloat16)
            for n in range(group):
                keepq[q + n, k] = made[:U, n * C : (n + 1) * C]
                sendc[c, n, k] = made[U:, n * C : (n + 1) * C]
        if send is not None:
            send()
        acc[...] += dot_t(gpre[...], wu[s])

        @pl.when(f + 2 < layers * n_ffn)
        def _():
            start(ffn_tile(f + 2))

    def attend(l, i, c):
        a = (layers - 1 - l) * n_att + i
        o = pl.multiple_of(i * 128, 128)
        s = lax.rem(a, 2)
        q = n_ffn * group + i
        wait(att_tile(a))
        q2, k2, v2 = (qkv[s, :, k * 128 : (k + 1) * 128] for k in range(3))
        g2 = (gm[:, pl.ds(o, 128)].astype(jnp.float32) * rl[s]).astype(jnp.bfloat16)
        weighed = g2.astype(jnp.float32) * pv[s]
        zero = jnp.zeros_like(q2)
        q2t, g2t = q2.T, g2.T
        dq = None
        dkt, dvt = [], []
        for h in range(2):
            sel = first if h == 0 else ~first
            p = pb[s, h]
            gprob = dot_t(jnp.where(sel, g2, zero), v2)
            centre = jnp.sum(jnp.where(sel, weighed, 0.0), axis=-1, keepdims=True)
            ds = (p.astype(jnp.float32) * (gprob - centre)).astype(jnp.bfloat16)
            part = dot(ds, jnp.where(sel, k2, zero))
            dq = part if h == 0 else dq + part
            dkt.append(dot(q2t[h * HD : (h + 1) * HD], ds))
            dvt.append(dot(g2t[h * HD : (h + 1) * HD], p))
        dq = (dq * 0.125).astype(jnp.bfloat16)
        dk = jnp.concatenate(dkt, axis=0).astype(jnp.bfloat16).T
        dv = jnp.concatenate(dvt, axis=0).astype(jnp.bfloat16).T
        vec[l, 0:1, pl.ds(o, 128)] = col_sum(dq)
        vec[l, 1:2, pl.ds(o, 128)] = col_sum(dv)
        rhs[:, :128] = dq
        rhs[:, 128:256] = dk
        rhs[:, 256:] = dv
        made = dot(hidT[...], rhs[...]).astype(jnp.bfloat16)
        keepq[q, 0] = made[:U, :C]
        sendc[c, 0, 0] = made[U:, :C]
        keepq[q, 1, :, :128] = made[:U, C:]
        sendc[c, 0, 1, :, :128] = made[U:, C:]
        made = dot(mixT[...], branch[:, pl.ds(o, 128)]).astype(jnp.bfloat16)
        keepq[q, 1, :, 128:] = made[:U]
        sendc[c, 0, 1, :, 128:] = made[U:]
        acc[...] += dot_t(rhs[...], wq[s])

        @pl.when(a + 2 < layers * n_att)
        def _():
            start(att_tile(a + 2))

    def core_copy(m, wide):
        c = lax.rem(m, 2)
        k = lax.rem(m, macros)
        q = k * group if wide else n_ffn * group + k - n_ffn
        size = group if wide else 1
        return remote(
            sendc.at[c, pl.ds(0, size)], recvq.at[pl.ds(q, size)], csem.at[0, m], csem.at[1, m], core
        )

    def first_copy(n):
        return remote(sendc.at[0, n], recvq.at[n], dsem.at[0, n], dsem.at[1, n], core)

    def is_wide(m):
        return lax.rem(m, macros) < n_ffn

    def unit_of(v):
        return v + jnp.minimum(lax.div(v, 2), EARLY)

    def copies_one(u):
        s = lax.rem(u, SLOTS_ONE)
        return [
            remote(s1.at[s, k], t1.at[s, k], xsem.at[0, k, s], xsem.at[1, k, s], (xdev, ydev)[k]) for k in range(2)
        ]

    def copy_two(u, k):
        s = lax.rem(u, SLOTS)
        return remote(s2.at[s, k], t2.at[s, k], ysem.at[0, k, s], ysem.at[1, k, s], (ydev, xdev)[k])

    def copy_in(u, k):
        s = lax.rem(u, SLOTS)
        return remote(za.at[s, k], zr.at[s, k], zsem.at[0, k, s], zsem.at[1, k, s], to_inner)

    def copy_across(u, k):
        s = lax.rem(u, SLOTS)
        return remote(zb.at[s, k], zt.at[s, k], zsem.at[2, k, s], zsem.at[3, k, s], across)

    def copy_out(u, k):
        s = lax.rem(u, SLOTS)
        return remote(zf.at[s, k], out.at[unit_of(u), k], zsem.at[4, k, s], zsem.at[5, k, s], to_outer)

    def copy_home(u):
        s = lax.rem(u, SLOTS)
        return pltpu.make_async_copy(zf.at[s], out.at[unit_of(u)], osem.at[s])

    def stage_one(v):
        u = unit_of(v)
        s = lax.rem(u, QUEUE)
        d = lax.rem(v, SLOTS_ONE)

        @pl.when(u < group)
        def _():
            first_copy(u).wait_recv()

        @pl.when(u == n_units - 1)
        def _():
            core_copy(jnp.int32(n_macros - 1), False).wait_recv()

        for k in range(2):
            sent, kept = ((1, 3), (0, 2)) if k == 0 else ((2, 3), (0, 1))
            for n, (a, b) in enumerate(zip(sent, kept)):
                to = pl.ds(n * R, R)
                s1[d, k, to] = low_sum(keepq[s, k, pl.ds(a * R, R)], recvq[s, k, pl.ds(a * R, R)])
                k1[d, k, to] = low_sum(keepq[s, k, pl.ds(b * R, R)], recvq[s, k, pl.ds(b * R, R)])
        start(copies_one(v))

    def stage_two(u):
        d = lax.rem(u, SLOTS_ONE)
        e = lax.rem(u, SLOTS)
        wait(copies_one(u))
        for k in range(2):
            s2[e, k] = low_sum(k1[d, k, pl.ds(R, R)], t1[d, k, pl.ds(R, R)])
            k2[e, k] = low_sum(k1[d, k, pl.ds(0, R)], t1[d, k, pl.ds(0, R)])
        start([copy_two(u, k) for k in range(2)])

    def stage_three(u):
        d = lax.rem(u, SLOTS)
        for k in range(2):
            copy_two(u, k).wait()
            za[d, k] = low_sum(k2[d, k], t2[d, k])

            @pl.when(outer)
            def _(k=k):
                copy_in(u, k).start()

    def stage_four(u):
        d = lax.rem(u, SLOTS)

        @pl.when(outer)
        def _():
            for k in range(2):
                copy_in(u, k).wait_send()

        @pl.when(inner)
        def _():
            for k in range(2):
                copy_in(u, k).wait_recv()
                zb[d, k] = low_sum(za[d, k], zr[d, k])
                copy_across(u, k).start()

    def stage_five(u):
        d = lax.rem(u, SLOTS)

        @pl.when(inner)
        def _():
            for k in range(2):
                copy_across(u, k).wait()
                zf[d, k] = low_sum(zb[d, k], zt[d, k])
                copy_out(u, k).start()
            copy_home(u).start()

    def stage_six(u):
        @pl.when(inner)
        def _():
            for k in range(2):
                copy_out(u, k).wait_send()
            copy_home(u).wait()

        @pl.when(outer)
        def _():
            for k in range(2):
                copy_out(u, k).wait_recv()

    stages = (None, stage_one, stage_two, stage_three, stage_four, stage_five, stage_six)

    def run_stage(i, k):
        u = i - LAGS[k]

        @pl.when((u >= 0) & (u < n_main))
        def _():
            stages[k](u)

    def quarter_copy(n, d):
        peer = lax.rem(zi + d, 4)
        return remote(
            zq.at[n, peer], zin.at[n, d - 1], qsem.at[0, n, d - 1], qsem.at[1, n, d - 1], (me, peer)
        )

    def early_one(n):
        return remote(e1.at[n], f1.at[n], esem.at[0, n], esem.at[1, n], (xdev, ydev)[n % 2])

    def early_two(n):
        return remote(e2.at[n], f2.at[n], esem.at[2, n], esem.at[3, n], (ydev, xdev)[n % 2])

    def early_place(n):
        half = pl.ds(pl.multiple_of(lax.rem(zi, 2) * 128, 128), 128)
        return out.at[group * n + group - 1, lax.div(zi, 2), :, half]

    def early_out(n, d):
        peer = lax.rem(zi + d, 4)
        return remote(ef.at[n], early_place(n), gather.at[0, n, d], gather.at[1, n, d], (me, peer))

    def early_home(n):
        return pltpu.make_async_copy(ef.at[n], early_place(n), gather.at[0, n, 0])

    def early_steps(i, n):
        u = group * n + group - 1

        @pl.when(i == 1 + 2 * n)
        def _():
            if n == 0:
                first_copy(u).wait_recv()
            for k in range(2):
                made = low_sum(keepq[u, k], recvq[u, k])
                for h in range(2):
                    zq[n, 2 * k + h] = made[:, h * 128 : (h + 1) * 128]
            for d in (2, 1, 3):
                quarter_copy(n, d).start()

        @pl.when(i == 10 + 2 * n)
        def _():
            for d in range(1, 4):
                quarter_copy(n, d).wait()
            made = zq[n, zi].astype(jnp.float32)
            for d in range(3):
                made = made + zin[n, d].astype(jnp.float32)
            made = made.astype(jnp.bfloat16)
            sent, kept = ((1, 3), (0, 2)) if n % 2 == 0 else ((2, 3), (0, 1))
            for j in range(2):
                e1[n, j * R : (j + 1) * R] = made[sent[j] * R : (sent[j] + 1) * R]
                h1[n, j * R : (j + 1) * R] = made[kept[j] * R : (kept[j] + 1) * R]

        @pl.when(i == n_main + 1)
        def _():
            early_one(n).start()

        @pl.when(i == n_main + 5)
        def _():
            early_one(n).wait()
            e2[n] = low_sum(h1[n, R:], f1[n, R:])
            h2[n] = low_sum(h1[n, :R], f1[n, :R])
            early_two(n).start()

        @pl.when(i == n_main + 9)
        def _():
            early_two(n).wait()
            ef[n] = low_sum(h2[n], f2[n])
            for d in range(1, 4):
                early_out(n, d).start()
            early_home(n).start()

    def vec_copy(k):
        where = (core, xdev, ydev, to_inner, across, to_outer)[k]
        return remote(vlow, vrecv.at[k], vsem.at[0, k], vsem.at[1, k], where)

    def vec_step(k):
        if 1 <= k <= 3:
            vec_copy(k - 1).wait()
            vlow[...] += vrecv[k - 1]
        if k == 0:
            vlow[...] = vec[...].astype(jnp.bfloat16)
        if k < 3:
            vec_copy(k).start()
        if k == 3:

            @pl.when(outer)
            def _():
                vec_copy(3).start()

        if k == 4:

            @pl.when(outer)
            def _():
                vec_copy(3).wait_send()

            @pl.when(inner)
            def _():
                vec_copy(3).wait_recv()
                vlow[...] += vrecv[3]
                vec_copy(4).start()

        if k == 5:

            @pl.when(inner)
            def _():
                vec_copy(4).wait()
                vlow[...] += vrecv[4]
                vec_copy(5).start()

        if k == 6:

            @pl.when(inner)
            def _():
                vec_copy(5).wait_send()
                vec_out[...] = vlow[...].astype(jnp.float32)

            @pl.when(outer)
            def _():
                vec_copy(5).wait_recv()
                vec_out[...] = vrecv[5].astype(jnp.float32)

    part = T // 4
    slab = part // GT_PARTS

    def gt_own():
        own = pl.ds(pl.multiple_of(zi * part, part), part)
        return pltpu.make_async_copy(gm.at[own], gt_out.at[zi], gsem.at[0, 3 * GT_PARTS])

    def gt_copy(n):
        peer = lax.rem(zi + 1 + lax.rem(n, 3), 4)
        o = lax.div(n, 3) * slab
        src = gm.at[pl.ds(pl.multiple_of(peer * part + o, slab), slab)]
        dst = gt_out.at[zi, pl.ds(pl.multiple_of(o, slab), slab)]
        return remote(src, dst, gsem.at[0, n], gsem.at[1, n], (me, peer))

    def done_by(i):
        num, den = PACE
        return jnp.minimum(lax.div(num * (i + 1) + den - 1, den), n_macros)

    last = 0
    while -(-PACE[0] * (last + 1) // PACE[1]) < n_macros:
        last += 1

    def step(i, carry):
        for k in range(6, 1, -1):
            run_stage(i, k)
        run_stage(i, 1)
        m = done_by(i - 1)
        l = layers - 1 - lax.div(m, macros)
        k = lax.rem(m, macros)
        c = lax.rem(m, 2)
        busy = (done_by(i) > m) & (m > 0)

        @pl.when(busy & (m == 2))
        def _():
            for n in range(group):
                first_copy(n).wait_send()

        @pl.when(busy & (m >= 3) & is_wide(m - 2))
        def _():
            core_copy(m - 2, True).wait_send()

        @pl.when(busy & (m >= 2) & ~is_wide(m - 2))
        def _():
            core_copy(m - 2, False).wait_send()

        @pl.when(busy & (k == 0))
        def _():
            prologue(l)

        @pl.when(busy & (k == 0) & (l < layers - 1))
        def _():
            start(att_layer(l))

        @pl.when(busy & (k < n_ffn))
        def _():
            ffn(l, k, c)

        @pl.when(busy & (k == n_ffn) & (l > 0))
        def _():
            start(ffn_layer(l - 1))

        @pl.when(busy & (k == n_ffn))
        def _():
            middle(l)

        @pl.when(busy & (k >= n_ffn))
        def _():
            attend(l, k - n_ffn, c)

        @pl.when(busy & (m >= 2) & is_wide(m - 1))
        def _():
            core_copy(m - 1, True).wait_recv()

        @pl.when(busy & (m >= 2) & ~is_wide(m - 1))
        def _():
            core_copy(m - 1, False).wait_recv()

        @pl.when(busy & (k < n_ffn))
        def _():
            core_copy(m, True).start()

        @pl.when(busy & (k >= n_ffn))
        def _():
            core_copy(m, False).start()

        for n in range(EARLY):
            early_steps(i, n)

        @pl.when(i == last + 1)
        def _():
            gm[...] = acc[...].astype(jnp.bfloat16)
            gt_own().start()

        @pl.when((i > last) & (i <= last + 3 * GT_PARTS))
        def _():
            gt_copy(i - last - 1).start()

        for n in range(7):

            @pl.when(i == last + 1 + 2 * n)
            def _(n=n):
                vec_step(n)

        return carry

    def first_sends():
        await_greetings(peers)
        for n in range(group):
            first_copy(n).start()

    prologue(layers - 1)
    ffn(layers - 1, jnp.int32(0), 0, first_sends)
    lax.fori_loop(1, n_main + LAGS[6], step, 0)
    for n in range(EARLY):
        early_home(n).wait()
        for d in range(1, 4):
            early_out(n, d).wait()
    for m in (n_macros - 2, n_macros - 1):
        core_copy(jnp.int32(m), False).wait_send()
    gt_own().wait()

    def gt_wait(n, c):
        gt_copy(n).wait()
        return c

    lax.fori_loop(0, 3 * GT_PARTS, gt_wait, 0)


def backward(grad_hidden, res, w):
    T, D = grad_hidden.shape
    L = w["w_qkv"].shape[0]
    FF = w["w_up"].shape[2]
    bf, f32 = jnp.bfloat16, jnp.float32
    S = jax.ShapeDtypeStruct
    V = pltpu.VMEM
    vm = pl.BlockSpec(memory_space=V)
    anyspec = pl.BlockSpec(memory_space=pl.ANY)
    R = D // WAYS
    U = 4 * R
    group = D // C
    n_units = L * (FF // C + D // 128)
    n_macros = L * (FF // D + D // 128)
    dma = pltpu.SemaphoreType.DMA
    scratch = [
        V((2, D, D), bf), V((2, D, D), bf), V((2, T, D), bf), V((2, D, T), bf),
        V((2, D, 384), bf), V((2, T, 384), bf), V((2, 2, T, T), bf), V((2, T, 128), f32), V((2, T, 128), f32),
        V((D, D), bf), V((D, T), bf), V((D, T), bf), V((D, T), bf),
        V((T, D), bf), V((T, 128), f32), V((T, D), bf), V((T, 128), f32),
        V((T, D), f32), V((T, D), bf), V((T, D), bf), V((T, 384), bf),
        V((L, VEC_ROWS, D), f32), V((L, VEC_ROWS, D), bf), V((6, L, VEC_ROWS, D), bf),
        V((2, group, 2, U, C), bf), V((QUEUE, 2, U, C), bf), V((QUEUE, 2, U, C), bf),
        V((SLOTS_ONE, 2, 2 * R, C), bf), V((SLOTS_ONE, 2, 2 * R, C), bf), V((SLOTS_ONE, 2, 2 * R, C), bf),
        V((SLOTS, 2, R, C), bf), V((SLOTS, 2, R, C), bf), V((SLOTS, 2, R, C), bf),
        V((SLOTS, 2, R, C), bf), V((SLOTS, 2, R, C), bf), V((SLOTS, 2, R, C), bf),
        V((SLOTS, 2, R, C), bf), V((SLOTS, 2, R, C), bf),
        V((EARLY, 4, U, 128), bf), V((EARLY, 3, U, 128), bf),
        V((EARLY, 2 * R, 128), bf), V((EARLY, 2 * R, 128), bf), V((EARLY, 2 * R, 128), bf),
        V((EARLY, R, 128), bf), V((EARLY, R, 128), bf), V((EARLY, R, 128), bf), V((EARLY, R, 128), bf),
        dma((2, EARLY, 3)), dma((4, EARLY)), dma((2, EARLY, 4)),
        dma((2, 3 + WAYS)), dma((2, 9)), dma((2, 3 + 2 * WAYS)), dma((2, n_macros)), dma((2, group)), dma((2, 2, SLOTS_ONE)), dma((2, 2, SLOTS)),
        dma((6, 2, SLOTS)), dma((SLOTS,)), dma((2, 6)), dma((2, 3 * GT_PARTS + 1)),
    ]
    return pl.pallas_call(
        functools.partial(bwd_kernel, L),
        out_shape=(
            S((n_units, 2, R, C), bf), S((4, T // 4, D), bf), S((L, VEC_ROWS, D), f32),
        ),
        in_specs=[vm] * 3 + [anyspec] * 17,
        out_specs=(anyspec, anyspec, vm),
        scratch_shapes=scratch,
        compiler_params=pltpu.CompilerParams(
            vmem_limit_bytes=60 * 1024 * 1024, collective_id=0, has_side_effects=True
        ),
        name="backward",
    )(
        grad_hidden, w["gain_one"], w["gain_two"],
        *(w[k] for k in ("w_qkv", "w_out", "w_up", "w_down")),
        *res,
    )


def finish_kernel(units, gt, vec, g_tok, g_qkv, g_out, g_up, g_down, *vectors):
    l = pl.program_id(0)
    R, D = g_out.shape[1:]
    n_ffn = g_up.shape[2] // D
    group = D // C
    g_tok[...] = gt[...].astype(jnp.float32)

    def read(n, k, cols=slice(None)):
        return units[0, n, k, :, cols].astype(jnp.float32)

    for rb in range(n_ffn):
        for n in range(group):
            u = rb * group + n
            g_up[0, :, u * C : (u + 1) * C] = read(u, 0)
            g_down[0, rb * R : (rb + 1) * R, n * C : (n + 1) * C] = read(u, 1)
    for i in range(D // 128):
        u = n_ffn * group + i
        for k in range(3):
            half = slice(k % 2 * 128, k % 2 * 128 + 128)
            g_qkv[0, :, k * D + i * 128 : k * D + (i + 1) * 128] = read(u, k // 2, half)
        g_out[0, :, i * 128 : (i + 1) * 128] = read(u, 1, slice(128, 256))
    row = 0
    for ref in vectors:
        for k in range(ref.shape[1] // D):
            ref[pl.ds(l, 1), k * D : (k + 1) * D] = vec[0, row : row + 1, :]
            row += 1


def finish(units, grad_tokens, vec, layers, hidden_units):
    n_units, _, R, _ = units.shape
    parts, piece, D = grad_tokens.shape
    L, FF = layers, hidden_units
    f32 = jnp.float32
    S = jax.ShapeDtypeStruct
    per = n_units // L
    widths = (D, D, D, D, D, FF, D, D, D)
    return pl.pallas_call(
        finish_kernel,
        grid=(L,),
        out_shape=(
            S((parts, piece, D), f32), S((L, R, 3 * D), f32), S((L, R, D), f32), S((L, R, FF), f32),
            S((L, FF // WAYS, D), f32),
        ) + tuple(S((L, width), f32) for width in widths),
        in_specs=[
            pl.BlockSpec((1, per, 2, R, C), lambda l: (L - 1 - l, 0, 0, 0, 0)),
            pl.BlockSpec((parts // L, piece, D), lambda l: (l, 0, 0)),
            pl.BlockSpec((1, VEC_ROWS, D), lambda l: (l, 0, 0)),
        ],
        out_specs=(
            pl.BlockSpec((parts // L, piece, D), lambda l: (l, 0, 0)),
            pl.BlockSpec((1, R, 3 * D), lambda l: (l, 0, 0)),
            pl.BlockSpec((1, R, D), lambda l: (l, 0, 0)),
            pl.BlockSpec((1, R, FF), lambda l: (l, 0, 0)),
            pl.BlockSpec((1, FF // WAYS, D), lambda l: (l, 0, 0)),
        ) + tuple(pl.BlockSpec((L, width), lambda l: (0, 0)) for width in widths),
        compiler_params=pltpu.CompilerParams(vmem_limit_bytes=60 * 1024 * 1024),
        name="finish",
    )(units.reshape(L, per, 2, R, C), grad_tokens, vec)


NAMES = (
    "w_qkv",
    "b_query",
    "b_value",
    "w_out",
    "b_out",
    "gain_one",
    "shift_one",
    "w_up",
    "b_up",
    "w_down",
    "b_down",
    "gain_two",
    "shift_two",
)


def by_class(array, block, ways):
    layers, rows, tokens_here = array.shape
    if ways == 1:
        return array.reshape(layers, WAYS, -1, tokens_here)
    array = array.reshape(layers, ways, WAYS, block, tokens_here)
    return jnp.swapaxes(array, 1, 2).reshape(layers, WAYS, -1, tokens_here)


def on_device(dp_count, tokens, segment_ids, pair_ids, *weights):
    w = dict(zip(NAMES, weights))
    layer_count, model_width, _ = w["w_qkv"].shape
    hidden_units = w["w_up"].shape[2]
    ways = dp_count // WAYS
    grad_hidden, loss_value, *res = forward(tokens, segment_ids, pair_ids, w)
    for place in (4, 5, 6):
        res[place] = by_class(res[place], model_width // dp_count, ways)
    block = model_width // WAYS
    acts = by_class(res[7], hidden_units // dp_count, ways)
    res[7] = acts.reshape(layer_count, WAYS, -1, block, acts.shape[-1])
    units, grad_tokens, vec = backward(grad_hidden, res, w)
    if ways > 1:
        groups = [[low + WAYS * high for high in range(ways)] for low in range(WAYS)]
        vec = lax.psum(vec, "dp", axis_index_groups=groups)
    grad_tokens, *rest = finish(units, grad_tokens, vec, layer_count, hidden_units)
    matrices, vectors = rest[:4], rest[4:]
    if ways > 1:
        matrices = [
            lax.psum_scatter(
                matrix, "dp", scatter_dimension=1, axis_index_groups=groups, tiled=True
            )
            for matrix in matrices
        ]
    g_qkv, g_out, g_up, g_down = matrices
    return (
        loss_value.reshape(1),
        grad_tokens,
        g_qkv,
        vectors[0],
        vectors[1],
        g_out,
        vectors[2],
        vectors[3],
        vectors[4],
        g_up,
        vectors[5],
        g_down,
        vectors[6],
        vectors[7],
        vectors[8],
    )


def solution(mesh):
    return jax.shard_map(
        functools.partial(on_device, mesh.shape["dp"]),
        mesh=mesh,
        in_specs=(P("dp", "seq", None), P("dp", "seq"), P("dp")) + (P(),) * 13,
        out_specs=(
            P("dp"),
            P("dp", "seq", None),
            P(None, "dp", None),
            P(),
            P(),
            P(None, "dp", None),
            P(),
            P(),
            P(),
            P(None, "dp", None),
            P(),
            P(None, "dp", None),
            P(),
            P(),
            P(),
        ),
        check_vma=False,
    )
```

```python
import functools

import jax
import jax.numpy as jnp
from jax import lax
from jax.experimental import pallas as pl
from jax.experimental.pallas import tpu as pltpu
from jax.sharding import PartitionSpec as P

MESH = pl.DeviceIdType.MESH
LOSS_SCALE = 1024.0
NORM_EPS = 1e-06
HD = 64
WIDE = 768
C = 256
WAYS = 8
QUEUE = 18
SLOTS_ONE = 7
SLOTS = 6
LAGS = (0, 1, 4, 6, 8, 10, 12)
PACE = (5, 6)
GT_PARTS = 4
EARLY = 2
VEC_ROWS = 16


def dot(left, right):
    return lax.dot_general(
        left,
        right,
        (((1,), (0,)), ((), ())),
        preferred_element_type=jnp.float32,
    )


def dot_t(left, right):
    return lax.dot_general(
        left,
        right,
        (((1,), (1,)), ((), ())),
        preferred_element_type=jnp.float32,
    )


def split(values):
    high = values.astype(jnp.bfloat16)
    return high, (values - high.astype(jnp.float32)).astype(jnp.bfloat16)


def remote(src, dst, send_sem, recv_sem, where):
    return pltpu.make_async_remote_copy(
        src_ref=src,
        dst_ref=dst,
        send_sem=send_sem,
        recv_sem=recv_sem,
        device_id=where,
        device_id_type=MESH,
    )


def greet(peers):
    barrier = pltpu.get_barrier_semaphore()
    for peer in peers:
        pl.semaphore_signal(barrier, inc=1, device_id=peer, device_id_type=MESH)


def await_greetings(peers):
    pl.semaphore_wait(pltpu.get_barrier_semaphore(), len(peers))


def gelu_pair(x):
    t = 1.0 / (1.0 + 0.23164190 * jnp.abs(x))
    gauss = jnp.exp(-0.5 * x * x)
    poly = t * (
        0.127414796
        + t * (-0.142248368 + t * (0.7107068705 + t * (-0.7265760135 + t * 0.5307027145)))
    )
    tail = poly * gauss
    phi = jnp.where(x >= 0.0, 1.0 - tail, tail)
    return x * phi, phi + x * (gauss * 0.3989422804014327)


def norm(x, gain, shift):
    centre = x - jnp.mean(x, axis=-1, keepdims=True)
    scaled = lax.rsqrt(jnp.mean(centre * centre, axis=-1, keepdims=True) + NORM_EPS)
    normal = centre * scaled
    return normal * gain + shift, normal, scaled


def fwd_kernel(
    layers, segs,
    tok, ids, pair, b_query, b_value, b_out, gain_one, shift_one, b_up, b_down, gain_two, shift_two,
    w_qkv, w_out, w_up, w_down,
    grad_out, loss_out, o_qkv, o_p, o_rl, o_pv, o_hidT, o_mixT, o_nrmT, o_actT, o_gp, o_n1, o_r1, o_n2, o_r2,
    wq, wo, wu, wd, bias, hid, low, idbuf, qkv, pb, rl, pv, mix, nrm, gp, n1, r1, n2, r2,
    hidT, mixT, nrmT, actT, acc, ubuf, gbuf, prow,
    wsem, osem, tsem, usem,
):
    T, D = hid.shape
    FF = w_up.shape[2]
    piece = tok.shape[1]
    parts = T // piece
    me = lax.axis_index("dp")
    zi = lax.axis_index("seq")
    pairs = ((w_qkv, wq), (w_out, wo), (w_up, wu), (w_down, wd))

    def wcopy(l, i):
        return pltpu.make_async_copy(pairs[i][0].at[l], pairs[i][1], wsem.at[i])

    def peer(k):
        return lax.rem(zi + k, parts)

    mine = pl.ds(pl.multiple_of(zi * piece, piece), piece)

    def tcopy(k, n):
        src, dst = ((tok, low.at[mine]), (ids, idbuf.at[zi]))[n]
        if k == 0:
            return pltpu.make_async_copy(src.at[zi], dst, tsem.at[n, 0, 0])
        return remote(src.at[peer(k)], dst, tsem.at[n, 0, k], tsem.at[n, 1, k], (me, peer(k)))

    peers = [(me, peer(k)) for k in range(1, parts)]
    greet(peers)
    await_greetings(peers)
    for k in (2, 1, 3, 0):
        for n in (1, 0):
            tcopy(k, n).start()
    for i in range(4):
        wcopy(0, i).start()

    def refill(l, *which):
        @pl.when(l + 1 < layers)
        def _():
            for i in which:
                wcopy(l + 1, i).start()

    lane = lax.broadcasted_iota(jnp.int32, (T, 128), 1)
    first = lane < HD

    homes = (
        (qkv, o_qkv), (hidT, o_hidT), (rl, o_rl), (pv, o_pv), (mixT, o_mixT), (n1, o_n1), (r1, o_r1),
        (nrmT, o_nrmT), (gp, o_gp), (actT, o_actT), (n2, o_n2), (r2, o_r2), (pb, o_p),
    )

    def home(l, k):
        return pltpu.make_async_copy(homes[k][0], homes[k][1].at[l], osem.at[k])

    def ship(l, *keys):
        for k in keys:
            home(l, k).start()

    def claim(l, *keys):
        @pl.when(l > 0)
        def _():
            for k in keys:
                home(l - 1, k).wait()

    for k in range(parts):
        tcopy(k, 1).wait()
    id_rows = [idbuf[k] for k in range(parts)]
    id_cols = jnp.concatenate(
        id_rows + [jnp.zeros((8 - parts, piece), jnp.int32)], axis=0
    ).astype(jnp.float32).T
    for i in range(parts):
        for j in range(parts):
            same = id_cols[:, i : i + 1] == id_rows[j].astype(jnp.float32)
            bias[i * piece : (i + 1) * piece, j * piece : (j + 1) * piece] = jnp.where(same, 0.0, -1e30)
    for k in (0, 1, 3, 2):
        tcopy(k, 0).wait()
        source = pl.ds(pl.multiple_of(lax.rem(zi + parts - k, parts) * piece, piece), piece)
        arrived = low[source, :]
        hid[source, :] = arrived.astype(jnp.float32)
        hidT[:, source] = arrived.T

    def layer(l, carry):
        row = pl.ds(l, 1)
        wcopy(l, 0).wait()
        y = dot(low[...], wq[...])
        refill(l, 0)
        claim(l, 0)
        qkv[:, :D] = ((y[:, :D] + b_query[row, :]) * 0.125).astype(jnp.bfloat16)
        qkv[:, D : 2 * D] = y[:, D : 2 * D].astype(jnp.bfloat16)
        qkv[:, 2 * D :] = (y[:, 2 * D :] + b_value[row, :]).astype(jnp.bfloat16)
        ship(l, 0)
        ship(l, 1)

        def scores(n):
            o = n // 2 * 128
            q2 = qkv[:, o : o + 128]
            sel = first if n % 2 == 0 else ~first
            return dot_t(jnp.where(sel, q2, jnp.zeros_like(q2)), qkv[:, D + o : D + o + 128]) + bias[...]

        claim(l, 2, 3, 4, 12)
        made = {0: scores(0)}
        for n in range(D // HD):
            if n + 1 < D // HD:
                made[n + 1] = scores(n + 1)
            cols = slice(n // 2 * 128, n // 2 * 128 + 128)
            v2 = qkv[:, 2 * D + cols.start : 2 * D + cols.stop]
            sel = first if n % 2 == 0 else ~first
            sc = made.pop(n)
            e = jnp.exp(sc - jnp.max(sc, axis=-1, keepdims=True))
            recip = 1.0 / jnp.sum(e, axis=-1, keepdims=True)
            p = e.astype(jnp.bfloat16)
            pb[n] = p
            part = dot(p, jnp.where(sel, v2, jnp.zeros_like(v2))) * recip
            if n % 2 == 0:
                total, before = part, recip
                continue
            total = total + part
            rl[:, cols] = jnp.where(first, before, recip)
            pv[:, cols] = total
            low_total = total.astype(jnp.bfloat16)
            mix[:, cols] = low_total
            mixT[cols, :] = low_total.T
        ship(l, 12)
        ship(l, 2)
        ship(l, 3)
        wcopy(l, 1).wait()
        acc[...] = dot(mix[...], wo[...])
        refill(l, 1)
        ship(l, 4)

        claim(l, 5, 6, 7)
        x = hid[...] + acc[...] + b_out[row, :]
        y, n, r = norm(x, gain_one[row, :], shift_one[row, :])
        nrm[...] = y
        rounded = y.astype(jnp.bfloat16)
        low[...] = rounded
        nrmT[...] = rounded.T
        n1[...] = n.astype(jnp.bfloat16)
        r1[...] = jnp.broadcast_to(r, (T, 128))
        ship(l, 5)
        ship(l, 6)
        ship(l, 7)
        wcopy(l, 2).wait()
        wcopy(l, 3).wait()
        acc[...] = nrm[...]
        claim(l, 8, 9)

        def raised(j):
            cols = slice(j * WIDE, (j + 1) * WIDE)
            return dot(low[...], wu[:, cols]) + b_up[row, cols]

        made = {0: raised(0)}
        for j in range(FF // WIDE):
            cols = slice(j * WIDE, (j + 1) * WIDE)
            if j + 1 < FF // WIDE:
                made[j + 1] = raised(j + 1)
            a, g = gelu_pair(made.pop(j))
            al = a.astype(jnp.bfloat16)
            gp[:, cols] = g.astype(jnp.bfloat16)
            actT[cols, :] = al.T
            acc[...] += dot(al, wd[cols, :])
        refill(l, 2, 3)
        ship(l, 8)
        ship(l, 9)

        claim(l, 10, 11)
        home(l, 1).wait()
        x = acc[...] + b_down[row, :]
        y, n, r = norm(x, gain_two[row, :], shift_two[row, :])
        hid[...] = y

        @pl.when(l + 1 < layers)
        def _():
            rounded = hid[...].astype(jnp.bfloat16)
            low[...] = rounded
            hidT[...] = rounded.T

        n2[...] = n.astype(jnp.bfloat16)
        r2[...] = jnp.broadcast_to(r, (T, 128))
        ship(l, 10)
        ship(l, 11)
        return carry

    lax.fori_loop(0, layers, layer, 0)

    count = parts * segs
    member_t = jnp.concatenate(
        [
            (lax.broadcasted_iota(jnp.int32, (segs, piece), 0) == row).astype(jnp.float32)
            for row in id_rows
        ],
        axis=1,
    )
    sizes = jnp.sum(member_t, axis=-1, keepdims=True)
    member_t = member_t.astype(jnp.bfloat16)
    high, rest = split(hid[...])
    embed = (dot(member_t, high) + dot(member_t, rest)) / sizes
    scale = lax.rsqrt(jnp.sum(embed * embed, axis=-1, keepdims=True) + NORM_EPS)
    unit = embed * scale
    ubuf[...] = jnp.zeros_like(ubuf)
    gbuf[zi] = unit

    def ucopy(k):
        return remote(gbuf.at[zi], gbuf.at[zi], usem.at[0, k], usem.at[1, k], (me, peer(k)))

    for k in range(1, parts):
        ucopy(k).start()
    prow[...] = jnp.zeros_like(prow)
    prow[:1, :count] = pair[...].astype(jnp.float32)
    partner = prow[...].T[:, :1]
    side = ubuf.shape[0]
    row_no = lax.broadcasted_iota(jnp.int32, (side, side), 0)
    col_no = lax.broadcasted_iota(jnp.int32, (side, side), 1)
    live = (row_no < count) & (col_no < count)
    chosen = jnp.where(live & (partner == col_no.astype(jnp.float32)), 1.0, 0.0)
    for k in range(1, parts):
        ucopy(k).wait()
    for k in range(parts):
        ubuf[k * segs : (k + 1) * segs, :] = gbuf[k]
    high, rest = split(ubuf[...])
    logits = 20.0 * (dot_t(high, high) + dot_t(high, rest) + dot_t(rest, high))
    logits = jnp.where(live, logits, -1e30)
    top = jnp.max(logits, axis=-1, keepdims=True)
    grown = jnp.exp(logits - top)
    total = jnp.sum(grown, axis=-1, keepdims=True)
    pull = jnp.where(live, (grown / total - chosen) * (20.0 * LOSS_SCALE / count), 0.0)
    acc[:side, :side] = pull + pull.T
    own = pl.ds(pl.multiple_of(zi * segs, segs), segs)
    ours, ours_rest = split(acc[own, :side])
    grad_unit = dot(ours, high) + dot(ours, rest) + dot(ours_rest, high)
    inner = jnp.sum(grad_unit * unit, axis=-1, keepdims=True)
    grad_sums = scale * (grad_unit - unit * inner) / sizes
    high, rest = split(grad_sums)
    both = jnp.concatenate([grad_sums, grad_sums - high.astype(jnp.float32)], axis=0).astype(jnp.bfloat16)
    lanes = lax.broadcasted_iota(jnp.int32, (piece, 2 * segs), 1)
    lanes = jnp.where(lanes < segs, lanes, lanes - segs).astype(jnp.float32)
    for i in range(parts):
        member = (lanes == id_cols[:, i : i + 1]).astype(jnp.bfloat16)
        grad_out[i * piece : (i + 1) * piece, :] = dot(member, both)
    picked = jnp.sum(chosen * logits, axis=-1, keepdims=True)
    losses = jnp.where(row_no[:, :1] < count, top + jnp.log(total) - picked, 0.0)
    loss_out[...] = jnp.sum(losses, axis=0, keepdims=True) / count
    for k in range(len(homes)):
        if k != 1:
            home(layers - 1, k).wait()


def forward(tokens, segment_ids, pair_ids, w):
    parts, piece, D = tokens.shape
    T = parts * piece
    L = w["w_qkv"].shape[0]
    FF = w["w_up"].shape[2]
    segs = pair_ids.shape[0] // parts
    side = 128
    bf, f32 = jnp.bfloat16, jnp.float32
    S = jax.ShapeDtypeStruct
    V = pltpu.VMEM
    vm = pl.BlockSpec(memory_space=V)
    anyspec = pl.BlockSpec(memory_space=pl.ANY)
    H = D // HD
    dma = pltpu.SemaphoreType.DMA
    out_shape = (
        S((T, D), f32), S((1, 1), f32), S((L, T, 3 * D), bf), S((L, H, T, T), bf), S((L, T, D), f32), S((L, T, D), f32),
        S((L, D, T), bf), S((L, D, T), bf), S((L, D, T), bf), S((L, FF, T), bf), S((L, T, FF), bf),
        S((L, T, D), bf), S((L, T, 128), f32), S((L, T, D), bf), S((L, T, 128), f32),
    )
    scratch = [
        V((D, 3 * D), bf), V((D, D), bf), V((D, FF), bf), V((FF, D), bf),
        V((T, T), f32), V((T, D), f32), V((T, D), bf), V((parts, 1, piece), jnp.int32),
        V((T, 3 * D), bf), V((H, T, T), bf), V((T, D), f32), V((T, D), f32), V((T, D), bf), V((T, D), f32), V((T, FF), bf),
        V((T, D), bf), V((T, 128), f32), V((T, D), bf), V((T, 128), f32),
        V((D, T), bf), V((D, T), bf), V((D, T), bf), V((FF, T), bf), V((T, D), f32),
        V((side, D), f32), V((parts, segs, D), f32), V((8, side), f32),
        dma((4,)), dma((13,)), dma((2, 2, parts)), dma((2, parts)),
    ]
    return pl.pallas_call(
        functools.partial(fwd_kernel, L, segs),
        out_shape=out_shape,
        in_specs=[anyspec] * 2 + [vm] * 10 + [anyspec] * 4,
        out_specs=(vm, vm) + (anyspec,) * 13,
        scratch_shapes=scratch,
        compiler_params=pltpu.CompilerParams(
            vmem_limit_bytes=60 * 1024 * 1024, collective_id=1, has_side_effects=True
        ),
        name="forward",
    )(
        tokens, segment_ids.reshape(parts, 1, piece), pair_ids.reshape(1, -1),
        *(w[k] for k in ("b_query", "b_value", "b_out", "gain_one", "shift_one", "b_up", "b_down", "gain_two", "shift_two")),
        *(w[k] for k in ("w_qkv", "w_out", "w_up", "w_down")),
    )


def low_sum(one, other):
    return one + other


def bwd_kernel(
    layers, g_in, gain_one, gain_two,
    w_qkv, w_out, w_up, w_down,
    h_qkv, h_p, h_rl, h_pv, h_hidT, h_mixT, h_nrmT, h_actT, h_gp, h_n1, h_r1, h_n2, h_r2,
    out, gt_out, vec_out,
    wd, wu, gp, actT, wq, qkv, pb, rl, pv, wo, hidT, mixT, nrmT, n1, r1, n2, r2,
    acc, second, gm, rhs, vec, vlow, vrecv,
    sendc, keepq, recvq, s1, k1, t1, s2, k2, t2, za, zr, zb, zt, zf,
    zq, zin, e1, h1, f1, e2, h2, f2, ef, qsem, esem, gather,
    fsem, asem, lsem, csem, dsem, xsem, ysem, zsem, osem, vsem, gsem,
):
    T, D = g_in.shape
    FF = w_up.shape[2]
    R = D // WAYS
    U = 4 * R
    n_ffn = FF // D
    n_att = D // 128
    group = D // C
    macros = n_ffn + n_att
    per = n_ffn * group + n_att
    n_units = layers * per
    n_main = n_units - EARLY
    n_macros = layers * macros

    me = lax.axis_index("dp")
    zi = lax.axis_index("seq")
    oc = lax.rem(me, 2)
    ox = lax.rem(lax.div(me, 2), 2)
    oy = lax.rem(lax.div(me, 4), 2)
    core = (me + 1 - 2 * oc, zi)
    xdev = (me + 2 - 4 * ox, zi)
    ydev = (me + 4 - 8 * oy, zi)
    inner = (zi == 1) | (zi == 2)
    outer = (zi == 0) | (zi == 3)
    to_inner = (me, 1 + lax.div(zi, 2))
    across = (me, 3 - zi)
    to_outer = (me, 3 * lax.div(zi, 2))

    def place(n):
        y = lax.rem(oy + n // 2 % 2, 2)
        x = lax.rem(ox + n % 2, 2)
        return 4 * y + 2 * x + lax.rem(oc + n // 4, 2)

    def turned(src, dst, l):
        return [(src.at[l, place(n)], dst.at[pl.ds(n * R, R)]) for n in range(WAYS)]

    def copies(parts, sem):
        return [pltpu.make_async_copy(a, b, sem.at[k]) for k, (a, b) in enumerate(parts)]

    def ffn_tile(f):
        l = layers - 1 - lax.div(f, n_ffn)
        rb = lax.rem(f, n_ffn)
        s = lax.rem(f, 2)
        span = pl.ds(pl.multiple_of(rb * D, D), D)
        parts = [(w_down.at[l, span], wd.at[s]), (w_up.at[l, :, span], wu.at[s]), (h_gp.at[l, :, span], gp.at[s])]
        parts += [(h_actT.at[l, place(n), rb], actT.at[s, pl.ds(n * R, R)]) for n in range(WAYS)]
        return copies(parts, fsem.at[s])

    def att_tile(a):
        l = layers - 1 - lax.div(a, n_att)
        i = lax.rem(a, n_att)
        s = lax.rem(a, 2)
        parts = [(h_p.at[l, pl.ds(2 * i, 2)], pb.at[s])]
        for k in range(3):
            span = pl.ds(pl.multiple_of(i * 128 + k * D, 128), 128)
            parts.append((w_qkv.at[l, :, span], wq.at[s, :, pl.ds(k * 128, 128)]))
            parts.append((h_qkv.at[l, :, span], qkv.at[s, :, pl.ds(k * 128, 128)]))
        span = pl.ds(pl.multiple_of(i * 128, 128), 128)
        parts += [(h_rl.at[l, :, span], rl.at[s]), (h_pv.at[l, :, span], pv.at[s])]
        return copies(parts, asem.at[s])

    def ffn_layer(l):
        return copies([(h_n2.at[l], n2), (h_r2.at[l], r2)] + turned(h_nrmT, nrmT, l), lsem.at[0])

    def att_layer(l):
        parts = [(h_n1.at[l], n1), (h_r1.at[l], r1), (w_out.at[l], wo)]
        return copies(parts + turned(h_hidT, hidT, l) + turned(h_mixT, mixT, l), lsem.at[1])

    peers = [core, xdev, ydev] + [(me, lax.rem(zi + k, 4)) for k in range(1, 4)]
    greet(peers)

    def start(made):
        for c in made:
            c.start()

    def wait(made):
        for c in made:
            c.wait()

    arriving = pltpu.make_async_copy(g_in, acc, lsem.at[0, 2 + 2 * WAYS])
    arriving.start()
    start(ffn_layer(layers - 1))
    start(ffn_tile(jnp.int32(0)))
    vec[...] = jnp.zeros_like(vec)

    lane = lax.broadcasted_iota(jnp.int32, (T, 128), 1)
    first = lane < HD

    def norm_back(g, n, r, gain):
        e = g * gain
        return r * (e - jnp.mean(e, axis=-1, keepdims=True) - n * jnp.mean(e * n, axis=-1, keepdims=True))

    def col_sum(v):
        return jnp.sum(v.astype(jnp.float32), axis=0, keepdims=True)

    branch, gpre = second, gm

    def through_norm(l, base, normal, root, gain, rounded):
        g = acc[...]
        n = normal[...].astype(jnp.float32)
        d = norm_back(g, n, root[:, :1], gain)
        acc[...] = d
        low = d.astype(jnp.bfloat16)
        rounded[...] = low
        for k, v in enumerate((low, g * n, g)):
            vec[l, base + k : base + k + 1, :] = col_sum(v)

    def prologue(l):
        wait(ffn_layer(l))
        through_norm(l, 5 + n_ffn, n2, r2, gain_two[pl.ds(l, 1), :], second)

    def middle(l):
        wait(att_layer(l))
        through_norm(l, 2, n1, r1, gain_one[pl.ds(l, 1), :], branch)
        gm[...] = dot_t(branch[...], wo[...]).astype(jnp.bfloat16)

    def ffn(l, rb, c, send=None):
        f = (layers - 1 - l) * n_ffn + rb
        s = lax.rem(f, 2)
        q = rb * group
        wait(ffn_tile(f))
        low = (dot_t(second[...], wd[s]) * gp[s].astype(jnp.float32)).astype(jnp.bfloat16)
        gpre[...] = low
        vec[l, pl.ds(5 + rb, 1), :] = col_sum(low)
        for k, (left, right) in enumerate(((nrmT, gpre), (actT.at[s], second))):
            made = dot(left[...], right[...]).astype(jnp.bfloat16)
            for n in range(group):
                keepq[q + n, k] = made[:U, n * C : (n + 1) * C]
                sendc[c, n, k] = made[U:, n * C : (n + 1) * C]
        if send is not None:
            send()
        acc[...] += dot_t(gpre[...], wu[s])

        @pl.when(f + 2 < layers * n_ffn)
        def _():
            start(ffn_tile(f + 2))

    def attend(l, i, c):
        a = (layers - 1 - l) * n_att + i
        o = pl.multiple_of(i * 128, 128)
        s = lax.rem(a, 2)
        q = n_ffn * group + i
        wait(att_tile(a))
        q2, k2, v2 = (qkv[s, :, k * 128 : (k + 1) * 128] for k in range(3))
        g2 = (gm[:, pl.ds(o, 128)].astype(jnp.float32) * rl[s]).astype(jnp.bfloat16)
        weighed = g2.astype(jnp.float32) * pv[s]
        zero = jnp.zeros_like(q2)
        q2t, g2t = q2.T, g2.T
        dq = None
        dkt, dvt = [], []
        for h in range(2):
            sel = first if h == 0 else ~first
            p = pb[s, h]
            gprob = dot_t(jnp.where(sel, g2, zero), v2)
            centre = jnp.sum(jnp.where(sel, weighed, 0.0), axis=-1, keepdims=True)
            ds = (p.astype(jnp.float32) * (gprob - centre)).astype(jnp.bfloat16)
            part = dot(ds, jnp.where(sel, k2, zero))
            dq = part if h == 0 else dq + part
            dkt.append(dot(q2t[h * HD : (h + 1) * HD], ds))
            dvt.append(dot(g2t[h * HD : (h + 1) * HD], p))
        dq = (dq * 0.125).astype(jnp.bfloat16)
        dk = jnp.concatenate(dkt, axis=0).astype(jnp.bfloat16).T
        dv = jnp.concatenate(dvt, axis=0).astype(jnp.bfloat16).T
        vec[l, 0:1, pl.ds(o, 128)] = col_sum(dq)
        vec[l, 1:2, pl.ds(o, 128)] = col_sum(dv)
        rhs[:, :128] = dq
        rhs[:, 128:256] = dk
        rhs[:, 256:] = dv
        made = dot(hidT[...], rhs[...]).astype(jnp.bfloat16)
        keepq[q, 0] = made[:U, :C]
        sendc[c, 0, 0] = made[U:, :C]
        keepq[q, 1, :, :128] = made[:U, C:]
        sendc[c, 0, 1, :, :128] = made[U:, C:]
        made = dot(mixT[...], branch[:, pl.ds(o, 128)]).astype(jnp.bfloat16)
        keepq[q, 1, :, 128:] = made[:U]
        sendc[c, 0, 1, :, 128:] = made[U:]
        acc[...] += dot_t(rhs[...], wq[s])

        @pl.when(a + 2 < layers * n_att)
        def _():
            start(att_tile(a + 2))

    def core_copy(m, wide):
        c = lax.rem(m, 2)
        k = lax.rem(m, macros)
        q = k * group if wide else n_ffn * group + k - n_ffn
        size = group if wide else 1
        return remote(
            sendc.at[c, pl.ds(0, size)], recvq.at[pl.ds(q, size)], csem.at[0, m], csem.at[1, m], core
        )

    def first_copy(n):
        return remote(sendc.at[0, n], recvq.at[n], dsem.at[0, n], dsem.at[1, n], core)

    def is_wide(m):
        return lax.rem(m, macros) < n_ffn

    def unit_of(v):
        return v + jnp.minimum(lax.div(v, 2), EARLY)

    def copies_one(u):
        s = lax.rem(u, SLOTS_ONE)
        return [
            remote(s1.at[s, k], t1.at[s, k], xsem.at[0, k, s], xsem.at[1, k, s], (xdev, ydev)[k]) for k in range(2)
        ]

    def copy_two(u, k):
        s = lax.rem(u, SLOTS)
        return remote(s2.at[s, k], t2.at[s, k], ysem.at[0, k, s], ysem.at[1, k, s], (ydev, xdev)[k])

    def copy_in(u, k):
        s = lax.rem(u, SLOTS)
        return remote(za.at[s, k], zr.at[s, k], zsem.at[0, k, s], zsem.at[1, k, s], to_inner)

    def copy_across(u, k):
        s = lax.rem(u, SLOTS)
        return remote(zb.at[s, k], zt.at[s, k], zsem.at[2, k, s], zsem.at[3, k, s], across)

    def copy_out(u, k):
        s = lax.rem(u, SLOTS)
        return remote(zf.at[s, k], out.at[unit_of(u), k], zsem.at[4, k, s], zsem.at[5, k, s], to_outer)

    def copy_home(u):
        s = lax.rem(u, SLOTS)
        return pltpu.make_async_copy(zf.at[s], out.at[unit_of(u)], osem.at[s])

    def stage_one(v):
        u = unit_of(v)
        s = lax.rem(u, QUEUE)
        d = lax.rem(v, SLOTS_ONE)

        @pl.when(u < group)
        def _():
            first_copy(u).wait_recv()

        @pl.when(u == n_units - 1)
        def _():
            core_copy(jnp.int32(n_macros - 1), False).wait_recv()

        for k in range(2):
            sent, kept = ((1, 3), (0, 2)) if k == 0 else ((2, 3), (0, 1))
            for n, (a, b) in enumerate(zip(sent, kept)):
                to = pl.ds(n * R, R)
                s1[d, k, to] = low_sum(keepq[s, k, pl.ds(a * R, R)], recvq[s, k, pl.ds(a * R, R)])
                k1[d, k, to] = low_sum(keepq[s, k, pl.ds(b * R, R)], recvq[s, k, pl.ds(b * R, R)])
        start(copies_one(v))

    def stage_two(u):
        d = lax.rem(u, SLOTS_ONE)
        e = lax.rem(u, SLOTS)
        wait(copies_one(u))
        for k in range(2):
            s2[e, k] = low_sum(k1[d, k, pl.ds(R, R)], t1[d, k, pl.ds(R, R)])
            k2[e, k] = low_sum(k1[d, k, pl.ds(0, R)], t1[d, k, pl.ds(0, R)])
        start([copy_two(u, k) for k in range(2)])

    def stage_three(u):
        d = lax.rem(u, SLOTS)
        for k in range(2):
            copy_two(u, k).wait()
            za[d, k] = low_sum(k2[d, k], t2[d, k])

            @pl.when(outer)
            def _(k=k):
                copy_in(u, k).start()

    def stage_four(u):
        d = lax.rem(u, SLOTS)

        @pl.when(outer)
        def _():
            for k in range(2):
                copy_in(u, k).wait_send()

        @pl.when(inner)
        def _():
            for k in range(2):
                copy_in(u, k).wait_recv()
                zb[d, k] = low_sum(za[d, k], zr[d, k])
                copy_across(u, k).start()

    def stage_five(u):
        d = lax.rem(u, SLOTS)

        @pl.when(inner)
        def _():
            for k in range(2):
                copy_across(u, k).wait()
                zf[d, k] = low_sum(zb[d, k], zt[d, k])
                copy_out(u, k).start()
            copy_home(u).start()

    def stage_six(u):
        @pl.when(inner)
        def _():
            for k in range(2):
                copy_out(u, k).wait_send()
            copy_home(u).wait()

        @pl.when(outer)
        def _():
            for k in range(2):
                copy_out(u, k).wait_recv()

    stages = (None, stage_one, stage_two, stage_three, stage_four, stage_five, stage_six)

    def run_stage(i, k):
        u = i - LAGS[k]

        @pl.when((u >= 0) & (u < n_main))
        def _():
            stages[k](u)

    def quarter_copy(n, d):
        peer = lax.rem(zi + d, 4)
        return remote(
            zq.at[n, peer], zin.at[n, d - 1], qsem.at[0, n, d - 1], qsem.at[1, n, d - 1], (me, peer)
        )

    def early_one(n):
        return remote(e1.at[n], f1.at[n], esem.at[0, n], esem.at[1, n], (xdev, ydev)[n % 2])

    def early_two(n):
        return remote(e2.at[n], f2.at[n], esem.at[2, n], esem.at[3, n], (ydev, xdev)[n % 2])

    def early_place(n):
        half = pl.ds(pl.multiple_of(lax.rem(zi, 2) * 128, 128), 128)
        return out.at[group * n + group - 1, lax.div(zi, 2), :, half]

    def early_out(n, d):
        peer = lax.rem(zi + d, 4)
        return remote(ef.at[n], early_place(n), gather.at[0, n, d], gather.at[1, n, d], (me, peer))

    def early_home(n):
        return pltpu.make_async_copy(ef.at[n], early_place(n), gather.at[0, n, 0])

    def early_steps(i, n):
        u = group * n + group - 1

        @pl.when(i == 1 + 2 * n)
        def _():
            if n == 0:
                first_copy(u).wait_recv()
            for k in range(2):
                made = low_sum(keepq[u, k], recvq[u, k])
                for h in range(2):
                    zq[n, 2 * k + h] = made[:, h * 128 : (h + 1) * 128]
            for d in (2, 1, 3):
                quarter_copy(n, d).start()

        @pl.when(i == 10 + 2 * n)
        def _():
            for d in range(1, 4):
                quarter_copy(n, d).wait()
            made = zq[n, zi].astype(jnp.float32)
            for d in range(3):
                made = made + zin[n, d].astype(jnp.float32)
            made = made.astype(jnp.bfloat16)
            sent, kept = ((1, 3), (0, 2)) if n % 2 == 0 else ((2, 3), (0, 1))
            for j in range(2):
                e1[n, j * R : (j + 1) * R] = made[sent[j] * R : (sent[j] + 1) * R]
                h1[n, j * R : (j + 1) * R] = made[kept[j] * R : (kept[j] + 1) * R]

        @pl.when(i == n_main + 1)
        def _():
            early_one(n).start()

        @pl.when(i == n_main + 5)
        def _():
            early_one(n).wait()
            e2[n] = low_sum(h1[n, R:], f1[n, R:])
            h2[n] = low_sum(h1[n, :R], f1[n, :R])
            early_two(n).start()

        @pl.when(i == n_main + 9)
        def _():
            early_two(n).wait()
            ef[n] = low_sum(h2[n], f2[n])
            for d in range(1, 4):
                early_out(n, d).start()
            early_home(n).start()

    def vec_copy(k):
        where = (core, xdev, ydev, to_inner, across, to_outer)[k]
        return remote(vlow, vrecv.at[k], vsem.at[0, k], vsem.at[1, k], where)

    def vec_step(k):
        if 1 <= k <= 3:
            vec_copy(k - 1).wait()
            vlow[...] += vrecv[k - 1]
        if k == 0:
            vlow[...] = vec[...].astype(jnp.bfloat16)
        if k < 3:
            vec_copy(k).start()
        if k == 3:

            @pl.when(outer)
            def _():
                vec_copy(3).start()

        if k == 4:

            @pl.when(outer)
            def _():
                vec_copy(3).wait_send()

            @pl.when(inner)
            def _():
                vec_copy(3).wait_recv()
                vlow[...] += vrecv[3]
                vec_copy(4).start()

        if k == 5:

            @pl.when(inner)
            def _():
                vec_copy(4).wait()
                vlow[...] += vrecv[4]
                vec_copy(5).start()

        if k == 6:

            @pl.when(inner)
            def _():
                vec_copy(5).wait_send()
                vec_out[...] = vlow[...].astype(jnp.float32)

            @pl.when(outer)
            def _():
                vec_copy(5).wait_recv()
                vec_out[...] = vrecv[5].astype(jnp.float32)

    part = T // 4
    slab = part // GT_PARTS

    def gt_own():
        own = pl.ds(pl.multiple_of(zi * part, part), part)
        return pltpu.make_async_copy(gm.at[own], gt_out.at[zi], gsem.at[0, 3 * GT_PARTS])

    def gt_copy(n):
        peer = lax.rem(zi + 1 + lax.rem(n, 3), 4)
        o = lax.div(n, 3) * slab
        src = gm.at[pl.ds(pl.multiple_of(peer * part + o, slab), slab)]
        dst = gt_out.at[zi, pl.ds(pl.multiple_of(o, slab), slab)]
        return remote(src, dst, gsem.at[0, n], gsem.at[1, n], (me, peer))

    def done_by(i):
        num, den = PACE
        return jnp.minimum(lax.div(num * (i + 1) + den - 1, den), n_macros)

    last = 0
    while -(-PACE[0] * (last + 1) // PACE[1]) < n_macros:
        last += 1

    def step(i, carry):
        for k in range(6, 1, -1):
            run_stage(i, k)
        run_stage(i, 1)
        m = done_by(i - 1)
        l = layers - 1 - lax.div(m, macros)
        k = lax.rem(m, macros)
        c = lax.rem(m, 2)
        busy = (done_by(i) > m) & (m > 0)

        @pl.when(busy & (m == 2))
        def _():
            for n in range(group):
                first_copy(n).wait_send()

        @pl.when(busy & (m >= 3) & is_wide(m - 2))
        def _():
            core_copy(m - 2, True).wait_send()

        @pl.when(busy & (m >= 2) & ~is_wide(m - 2))
        def _():
            core_copy(m - 2, False).wait_send()

        @pl.when(busy & (k == 0))
        def _():
            prologue(l)

        @pl.when(busy & (k == 0) & (l < layers - 1))
        def _():
            start(att_layer(l))

        @pl.when(busy & (k < n_ffn))
        def _():
            ffn(l, k, c)

        @pl.when(busy & (k == n_ffn) & (l > 0))
        def _():
            start(ffn_layer(l - 1))

        @pl.when(busy & (k == n_ffn))
        def _():
            middle(l)

        @pl.when(busy & (k >= n_ffn))
        def _():
            attend(l, k - n_ffn, c)

        @pl.when(busy & (m >= 2) & is_wide(m - 1))
        def _():
            core_copy(m - 1, True).wait_recv()

        @pl.when(busy & (m >= 2) & ~is_wide(m - 1))
        def _():
            core_copy(m - 1, False).wait_recv()

        @pl.when(busy & (k < n_ffn))
        def _():
            core_copy(m, True).start()

        @pl.when(busy & (k >= n_ffn))
        def _():
            core_copy(m, False).start()

        for n in range(EARLY):
            early_steps(i, n)

        @pl.when(i == last + 1)
        def _():
            gm[...] = acc[...].astype(jnp.bfloat16)
            gt_own().start()

        @pl.when((i > last) & (i <= last + 3 * GT_PARTS))
        def _():
            gt_copy(i - last - 1).start()

        for n in range(7):

            @pl.when(i == last + 1 + 2 * n)
            def _(n=n):
                vec_step(n)

        return carry

    def first_sends():
        await_greetings(peers)
        for n in range(group):
            first_copy(n).start()

    arriving.wait()
    prologue(layers - 1)
    start(ffn_tile(jnp.int32(1)))
    start(att_layer(layers - 1))
    for n in range(2):
        start(att_tile(jnp.int32(n)))
    ffn(layers - 1, jnp.int32(0), 0, first_sends)
    lax.fori_loop(1, n_main + LAGS[6], step, 0)
    for n in range(EARLY):
        early_home(n).wait()
        for d in range(1, 4):
            early_out(n, d).wait()
    for m in (n_macros - 2, n_macros - 1):
        core_copy(jnp.int32(m), False).wait_send()
    gt_own().wait()

    def gt_wait(n, c):
        gt_copy(n).wait()
        return c

    lax.fori_loop(0, 3 * GT_PARTS, gt_wait, 0)


def backward(grad_hidden, res, w):
    T, D = grad_hidden.shape
    L = w["w_qkv"].shape[0]
    FF = w["w_up"].shape[2]
    bf, f32 = jnp.bfloat16, jnp.float32
    S = jax.ShapeDtypeStruct
    V = pltpu.VMEM
    vm = pl.BlockSpec(memory_space=V)
    anyspec = pl.BlockSpec(memory_space=pl.ANY)
    R = D // WAYS
    U = 4 * R
    group = D // C
    n_units = L * (FF // C + D // 128)
    n_macros = L * (FF // D + D // 128)
    dma = pltpu.SemaphoreType.DMA
    scratch = [
        V((2, D, D), bf), V((2, D, D), bf), V((2, T, D), bf), V((2, D, T), bf),
        V((2, D, 384), bf), V((2, T, 384), bf), V((2, 2, T, T), bf), V((2, T, 128), f32), V((2, T, 128), f32),
        V((D, D), bf), V((D, T), bf), V((D, T), bf), V((D, T), bf),
        V((T, D), bf), V((T, 128), f32), V((T, D), bf), V((T, 128), f32),
        V((T, D), f32), V((T, D), bf), V((T, D), bf), V((T, 384), bf),
        V((L, VEC_ROWS, D), f32), V((L, VEC_ROWS, D), bf), V((6, L, VEC_ROWS, D), bf),
        V((2, group, 2, U, C), bf), V((QUEUE, 2, U, C), bf), V((QUEUE, 2, U, C), bf),
        V((SLOTS_ONE, 2, 2 * R, C), bf), V((SLOTS_ONE, 2, 2 * R, C), bf), V((SLOTS_ONE, 2, 2 * R, C), bf),
        V((SLOTS, 2, R, C), bf), V((SLOTS, 2, R, C), bf), V((SLOTS, 2, R, C), bf),
        V((SLOTS, 2, R, C), bf), V((SLOTS, 2, R, C), bf), V((SLOTS, 2, R, C), bf),
        V((SLOTS, 2, R, C), bf), V((SLOTS, 2, R, C), bf),
        V((EARLY, 4, U, 128), bf), V((EARLY, 3, U, 128), bf),
        V((EARLY, 2 * R, 128), bf), V((EARLY, 2 * R, 128), bf), V((EARLY, 2 * R, 128), bf),
        V((EARLY, R, 128), bf), V((EARLY, R, 128), bf), V((EARLY, R, 128), bf), V((EARLY, R, 128), bf),
        dma((2, EARLY, 3)), dma((4, EARLY)), dma((2, EARLY, 4)),
        dma((2, 3 + WAYS)), dma((2, 9)), dma((2, 3 + 2 * WAYS)), dma((2, n_macros)), dma((2, group)), dma((2, 2, SLOTS_ONE)), dma((2, 2, SLOTS)),
        dma((6, 2, SLOTS)), dma((SLOTS,)), dma((2, 6)), dma((2, 3 * GT_PARTS + 1)),
    ]
    return pl.pallas_call(
        functools.partial(bwd_kernel, L),
        out_shape=(
            S((n_units, 2, R, C), bf), S((4, T // 4, D), bf), S((L, VEC_ROWS, D), f32),
        ),
        in_specs=[anyspec] + [vm] * 2 + [anyspec] * 17,
        out_specs=(anyspec, anyspec, vm),
        scratch_shapes=scratch,
        compiler_params=pltpu.CompilerParams(
            vmem_limit_bytes=60 * 1024 * 1024, collective_id=0, has_side_effects=True
        ),
        name="backward",
    )(
        grad_hidden, w["gain_one"], w["gain_two"],
        *(w[k] for k in ("w_qkv", "w_out", "w_up", "w_down")),
        *res,
    )


def finish_kernel(units, gt, vec, g_tok, g_qkv, g_out, g_up, g_down, *vectors):
    l = pl.program_id(0)
    R, D = g_out.shape[1:]
    n_ffn = g_up.shape[2] // D
    group = D // C
    g_tok[...] = gt[...].astype(jnp.float32)

    def read(n, k, cols=slice(None)):
        return units[0, n, k, :, cols].astype(jnp.float32)

    for rb in range(n_ffn):
        for n in range(group):
            u = rb * group + n
            g_up[0, :, u * C : (u + 1) * C] = read(u, 0)
            g_down[0, rb * R : (rb + 1) * R, n * C : (n + 1) * C] = read(u, 1)
    for i in range(D // 128):
        u = n_ffn * group + i
        for k in range(3):
            half = slice(k % 2 * 128, k % 2 * 128 + 128)
            g_qkv[0, :, k * D + i * 128 : k * D + (i + 1) * 128] = read(u, k // 2, half)
        g_out[0, :, i * 128 : (i + 1) * 128] = read(u, 1, slice(128, 256))
    row = 0
    for ref in vectors:
        for k in range(ref.shape[1] // D):
            ref[pl.ds(l, 1), k * D : (k + 1) * D] = vec[0, row : row + 1, :]
            row += 1


def finish(units, grad_tokens, vec, layers, hidden_units):
    n_units, _, R, _ = units.shape
    parts, piece, D = grad_tokens.shape
    L, FF = layers, hidden_units
    f32 = jnp.float32
    S = jax.ShapeDtypeStruct
    per = n_units // L
    widths = (D, D, D, D, D, FF, D, D, D)
    return pl.pallas_call(
        finish_kernel,
        grid=(L,),
        out_shape=(
            S((parts, piece, D), f32), S((L, R, 3 * D), f32), S((L, R, D), f32), S((L, R, FF), f32),
            S((L, FF // WAYS, D), f32),
        ) + tuple(S((L, width), f32) for width in widths),
        in_specs=[
            pl.BlockSpec((1, per, 2, R, C), lambda l: (L - 1 - l, 0, 0, 0, 0)),
            pl.BlockSpec((parts // L, piece, D), lambda l: (l, 0, 0)),
            pl.BlockSpec((1, VEC_ROWS, D), lambda l: (l, 0, 0)),
        ],
        out_specs=(
            pl.BlockSpec((parts // L, piece, D), lambda l: (l, 0, 0)),
            pl.BlockSpec((1, R, 3 * D), lambda l: (l, 0, 0)),
            pl.BlockSpec((1, R, D), lambda l: (l, 0, 0)),
            pl.BlockSpec((1, R, FF), lambda l: (l, 0, 0)),
            pl.BlockSpec((1, FF // WAYS, D), lambda l: (l, 0, 0)),
        ) + tuple(pl.BlockSpec((L, width), lambda l: (0, 0)) for width in widths),
        compiler_params=pltpu.CompilerParams(vmem_limit_bytes=60 * 1024 * 1024),
        name="finish",
    )(units.reshape(L, per, 2, R, C), grad_tokens, vec)


NAMES = (
    "w_qkv",
    "b_query",
    "b_value",
    "w_out",
    "b_out",
    "gain_one",
    "shift_one",
    "w_up",
    "b_up",
    "w_down",
    "b_down",
    "gain_two",
    "shift_two",
)


def by_class(array, block, ways):
    layers, rows, tokens_here = array.shape
    if ways == 1:
        return array.reshape(layers, WAYS, -1, tokens_here)
    array = array.reshape(layers, ways, WAYS, block, tokens_here)
    return jnp.swapaxes(array, 1, 2).reshape(layers, WAYS, -1, tokens_here)


def on_device(dp_count, tokens, segment_ids, pair_ids, *weights):
    w = dict(zip(NAMES, weights))
    layer_count, model_width, _ = w["w_qkv"].shape
    hidden_units = w["w_up"].shape[2]
    ways = dp_count // WAYS
    grad_hidden, loss_value, *res = forward(tokens, segment_ids, pair_ids, w)
    for place in (4, 5, 6):
        res[place] = by_class(res[place], model_width // dp_count, ways)
    block = model_width // WAYS
    acts = by_class(res[7], hidden_units // dp_count, ways)
    res[7] = acts.reshape(layer_count, WAYS, -1, block, acts.shape[-1])
    units, grad_tokens, vec = backward(grad_hidden, res, w)
    if ways > 1:
        groups = [[low + WAYS * high for high in range(ways)] for low in range(WAYS)]
        vec = lax.psum(vec, "dp", axis_index_groups=groups)
    grad_tokens, *rest = finish(units, grad_tokens, vec, layer_count, hidden_units)
    matrices, vectors = rest[:4], rest[4:]
    if ways > 1:
        matrices = [
            lax.psum_scatter(
                matrix, "dp", scatter_dimension=1, axis_index_groups=groups, tiled=True
            )
            for matrix in matrices
        ]
    g_qkv, g_out, g_up, g_down = matrices
    return (
        loss_value.reshape(1),
        grad_tokens,
        g_qkv,
        vectors[0],
        vectors[1],
        g_out,
        vectors[2],
        vectors[3],
        vectors[4],
        g_up,
        vectors[5],
        g_down,
        vectors[6],
        vectors[7],
        vectors[8],
    )


def solution(mesh):
    return jax.shard_map(
        functools.partial(on_device, mesh.shape["dp"]),
        mesh=mesh,
        in_specs=(P("dp", "seq", None), P("dp", "seq"), P("dp")) + (P(),) * 13,
        out_specs=(
            P("dp"),
            P("dp", "seq", None),
            P(None, "dp", None),
            P(),
            P(),
            P(None, "dp", None),
            P(),
            P(),
            P(),
            P(None, "dp", None),
            P(),
            P(None, "dp", None),
            P(),
            P(),
            P(),
        ),
        check_vma=False,
    )
```
